32 devices in a mesh: dp: 8 (over z, core), shard: 4 (over y, x).
Axes of the slice: x: 2, y: 2, z: 4, core: 2. Of those that a mesh axis runs over, the one named last changes fastest.
Arguments:
- tokens: bfloat16 [8192, 1024], P(('dp', 'shard')), may hold values from -6 to 6
- cotangent: bfloat16 [8192, 1024], P(('dp', 'shard')), may hold values from -6 to 6
- segments: int32 [8192], P(('dp', 'shard')), may hold values from 0 to 3, as said below
- master_query: float32 [1024, 2048], P('shard'), may hold values from -0.1875 to 0.1875
- master_key: float32 [1024, 1024], P('shard'), may hold values from -0.1875 to 0.1875
- master_value: float32 [1024, 1024], P('shard'), may hold values from -0.1875 to 0.1875
- master_out: float32 [2048, 1024], P('shard'), may hold values from -0.125 to 0.125
- master_gate: float32 [1024, 3072], P('shard'), may hold values from -0.1875 to 0.1875
- master_up: float32 [1024, 3072], P('shard'), may hold values from -0.1875 to 0.1875
- master_down: float32 [3072, 1024], P('shard'), may hold values from -0.109375 to 0.109375
- moment_query: float32 [1024, 2048], P('shard'), may hold values from -512 to 512
- moment_key: float32 [1024, 1024], P('shard'), may hold values from -512 to 512
- moment_value: float32 [1024, 1024], P('shard'), may hold values from -512 to 512
- moment_out: float32 [2048, 1024], P('shard'), may hold values from -512 to 512
- moment_gate: float32 [1024, 3072], P('shard'), may hold values from -512 to 512
- moment_up: float32 [1024, 3072], P('shard'), may hold values from -512 to 512
- moment_down: float32 [3072, 1024], P('shard'), may hold values from -512 to 512
- gains: float32 [2304], replicated, may hold values from 0.5 to 1.5
- gain_first: float32 [2304], P('shard'), may hold values from -128 to 128
- gain_second: float32 [2304], P('shard'), may hold values from 409.6 to 10240
Outputs:
- out_tokens: bfloat16 [8192, 1024], P(('dp', 'shard'))
- grad_tokens: float32 [8192, 1024], P(('dp', 'shard'))
- grad_query: float32 [1024, 2048], P('shard')
- grad_key: float32 [1024, 1024], P('shard')
- grad_value: float32 [1024, 1024], P('shard')
- grad_out: float32 [2048, 1024], P('shard')
- grad_gate: float32 [1024, 3072], P('shard')
- grad_up: float32 [1024, 3072], P('shard')
- grad_down: float32 [3072, 1024], P('shard')
- new_moment_query: float32 [1024, 2048], P('shard')
- new_moment_key: float32 [1024, 1024], P('shard')
- new_moment_value: float32 [1024, 1024], P('shard')
- new_moment_out: float32 [2048, 1024], P('shard')
- new_moment_gate: float32 [1024, 3072], P('shard')
- new_moment_up: float32 [1024, 3072], P('shard')
- new_moment_down: float32 [3072, 1024], P('shard')
- new_master_query: float32 [1024, 2048], P('shard')
- new_master_key: float32 [1024, 1024], P('shard')
- new_master_value: float32 [1024, 1024], P('shard')
- new_master_out: float32 [2048, 1024], P('shard')
- new_master_gate: float32 [1024, 3072], P('shard')
- new_master_up: float32 [1024, 3072], P('shard')
- new_master_down: float32 [3072, 1024], P('shard')
- gain_grads: float32 [2304], P('shard')
- gain_second_new: float32 [2304], P('shard')
- gains_new: float32 [2304], P('shard')
The draws below stay inside these ranges and needn't reach their ends.
Inputs may be any that keep to these rules, and one draw needn't show every extreme that they name: `segments`: each sequence of 1024 tokens holds four documents with ids 0, 1, 2, 3 in order; each document has at least 102 tokens.
All inputs are finite; a program needn't handle non-finite values.
Results may differ from the reference program's by a relative error of at most 0.033.
Values may be sent and summed in bfloat16 or wider, within the bound.
No kernel may reach another device: no remote copies, remote signals or barrier semaphores. Data moves between devices by JAX's collectives and lax.ppermute only.
A program may use at most 320 MiB of HBM per device.

```python
import math
import jax
import jax.numpy as jnp
from jax import lax

D = 1024
HEADS = 16
KV_HEADS = 8
HEAD_DIM = 128
FF = 3072
NS_TURNS = 5
STEP = 10
GROUP = 2
SEQ = 1024
NSEQ = 8
TOKENS = 8192
GAINS = 2304


def draw_segments(key, part):
    key = jax.random.fold_in(key, 11)
    shortest = SEQ // 10
    lengths = jax.random.randint(key, (NSEQ, 3), shortest, 3 * SEQ // 10)
    boundaries = jnp.cumsum(lengths, axis=1).astype(jnp.int32)
    positions = jnp.arange(SEQ, dtype=jnp.int32)
    counted = jnp.sum((positions[None, :, None] >= boundaries[:, None, :]).astype(jnp.int32), axis=-1)
    return counted.reshape(TOKENS).astype(jnp.int32)


def shard_levels(rng, dims, pieces, low, largest):
    def one(axis_at, parts):
        steps = jax.random.uniform(jax.random.fold_in(jax.random.fold_in(rng, 6), axis_at), (parts,), jnp.float32, low / len(pieces), largest / len(pieces))
        return jnp.repeat(jnp.exp(steps), dims[axis_at] // parts).reshape((-1,) + (1,) * (len(dims) - axis_at - 1))

    level = one(*pieces[0])
    for cut in pieces[1:]:
        level = level * one(*cut)
    return level


def scatter_about(stream_key, extent, scale, bound, shards=(), held_as=jnp.bfloat16):
    level = shard_levels(stream_key, extent, shards, -0.22, 0.18) if shards else 1.0
    values = jax.random.normal(stream_key, extent, jnp.float32) * scale * level
    return jnp.minimum(jnp.maximum(values, -bound), bound).astype(held_as)


def setup_inputs(seed: int = 0) -> dict:
    seeds = jax.random.split(jax.random.key(seed), 21)
    return {
        "tokens": scatter_about(seeds[0], (TOKENS, D), 1.0, 6.0, ((0, 32),)),
        "cotangent": scatter_about(seeds[1], (TOKENS, D), 1.0, 6.0, ((0, 32),)),
        "segments": draw_segments(jax.random.fold_in(seeds[20], 71), 0),
        "master_query": scatter_about(seeds[3], (D, HEADS * HEAD_DIM), D ** -0.5, 0.1875, ((0, 4),), jnp.float32),
        "master_key": scatter_about(seeds[4], (D, KV_HEADS * HEAD_DIM), D ** -0.5, 0.1875, ((0, 4),), jnp.float32),
        "master_value": scatter_about(seeds[5], (D, KV_HEADS * HEAD_DIM), D ** -0.5, 0.1875, ((0, 4),), jnp.float32),
        "master_out": scatter_about(seeds[6], (HEADS * HEAD_DIM, D), (HEADS * HEAD_DIM) ** -0.5, 0.125, ((0, 4),), jnp.float32),
        "master_gate": scatter_about(seeds[7], (D, FF), D ** -0.5, 0.1875, ((0, 4),), jnp.float32),
        "master_up": scatter_about(seeds[8], (D, FF), D ** -0.5, 0.1875, ((0, 4),), jnp.float32),
        "master_down": scatter_about(seeds[9], (FF, D), FF ** -0.5, 0.109375, ((0, 4),), jnp.float32),
        "moment_query": scatter_about(seeds[10], (D, HEADS * HEAD_DIM), (TOKENS ** 0.5), 512.0, ((0, 4),), jnp.float32),
        "moment_key": scatter_about(seeds[11], (D, KV_HEADS * HEAD_DIM), (TOKENS ** 0.5), 512.0, ((0, 4),), jnp.float32),
        "moment_value": scatter_about(seeds[12], (D, KV_HEADS * HEAD_DIM), (TOKENS ** 0.5), 512.0, ((0, 4),), jnp.float32),
        "moment_out": scatter_about(seeds[13], (HEADS * HEAD_DIM, D), (TOKENS ** 0.5), 512.0, ((0, 4),), jnp.float32),
        "moment_gate": scatter_about(seeds[14], (D, FF), (TOKENS ** 0.5), 512.0, ((0, 4),), jnp.float32),
        "moment_up": scatter_about(seeds[15], (D, FF), (TOKENS ** 0.5), 512.0, ((0, 4),), jnp.float32),
        "moment_down": scatter_about(seeds[16], (FF, D), (TOKENS ** 0.5), 512.0, ((0, 4),), jnp.float32),
        "gains": jnp.clip(1.0 + 0.1 * jax.random.normal(seeds[17], (GAINS,), jnp.float32), 0.5, 1.5),
        "gain_first": scatter_about(seeds[18], (GAINS,), (0.25 * TOKENS ** 0.5), 128.0, ((0, 4),), jnp.float32),
        "gain_second": jnp.clip(jnp.exp(math.log(10240.0) - 3.218876 * jax.random.uniform(seeds[19], (GAINS,), jnp.float32) ** shard_levels(seeds[19], (GAINS,), ((0, 4),), -0.2, 0.2)), 409.6, 10240.0),
    }


HIGH = lax.Precision.HIGHEST
EPS_NORM = 1e-06
ROPE_BASE = 1000000.0
MOMENTUM = 0.95
MUON_RATE = 0.5
MUON_DECAY = 0.1
BETA_FIRST = 0.9
BETA_SECOND = 0.95
GAIN_RATE = 0.6
ADAM_EPS = 1e-08
COEF_LINEAR = 3.4445
COEF_SQUARE = -4.775
COEF_CUBE = 2.0315
MASKED = -1e+30

@jax.custom_vjp
def low(v):
    return lax.optimization_barrier(v.astype(jnp.bfloat16)).astype(jnp.float32)

@jax.custom_vjp
def low_back(v):
    return v

def low_keep(v):
    return (low(v), None)

def low_pass(kept, grad):
    return (grad,)

def back_keep(v):
    return (v, None)

def back_low(kept, grad):
    return (low(grad),)
low.defvjp(low_keep, low_pass)
low_back.defvjp(back_keep, back_low)

def rms_norm(values, gain):
    return values * lax.rsqrt(lax.optimization_barrier(jnp.mean(values * values, axis=-1, keepdims=True)) + EPS_NORM) * gain

def rope_tables(positions):
    half_dim = HEAD_DIM // 2
    inverse = ROPE_BASE ** (-(jnp.arange(half_dim, dtype=jnp.float32) * 2.0 / HEAD_DIM))
    angles = positions.astype(jnp.float32)[:, None] * inverse[None, :]
    cos_table = jnp.cos(angles)
    sin_table = jnp.sin(angles)
    return (jnp.concatenate([cos_table, cos_table], axis=-1), jnp.concatenate([sin_table, sin_table], axis=-1))

def rotate(values, cos_table, sin_table):
    half_dim = values.shape[-1] // 2
    turned = jnp.concatenate([-values[..., half_dim:], values[..., :half_dim]], axis=-1)
    return values * cos_table[:, None, :] + turned * sin_table[:, None, :]

def prepare_heads(query_pre, key_pre, query_gain, key_gain, cos_table, sin_table):
    token_count = query_pre.shape[0]
    query_heads = rms_norm(query_pre.reshape(token_count, -1, HEAD_DIM), query_gain)
    key_heads = rms_norm(key_pre.reshape(token_count, -1, HEAD_DIM), key_gain)
    return (rotate(query_heads, cos_table, sin_table) * HEAD_DIM ** (-0.5), rotate(key_heads, cos_table, sin_table))

def attend_block(query_block, key_part, value_part, seg_query, seg_keys, pos_query):
    block_len = query_block.shape[0]
    grouped = query_block.reshape(block_len, KV_HEADS, GROUP, HEAD_DIM)
    scores = low_back(jnp.einsum('bkgd,skd->kgbs', grouped, key_part, precision=HIGH))
    key_pos = jnp.arange(key_part.shape[0], dtype=jnp.int32)
    allowed = (seg_query[:, None] == seg_keys[None, :]) & (key_pos[None, :] <= pos_query[:, None])
    masked = jnp.where(allowed, scores, MASKED)
    row_max = lax.optimization_barrier(jnp.max(masked, axis=-1, keepdims=True))
    exp_scores = jnp.exp(masked - row_max)
    attn_weights = low(exp_scores / lax.optimization_barrier(jnp.sum(exp_scores, axis=-1, keepdims=True)))
    mixed_values = jnp.einsum('kgbs,skd->bkgd', attn_weights, value_part, precision=HIGH)
    return mixed_values.reshape(block_len, KV_HEADS * GROUP * HEAD_DIM)

def attention(query_low, key_low, value_low, segments):
    block_len = min(512, SEQ)
    blocks = SEQ // block_len
    query_seq = query_low.reshape(NSEQ, blocks, block_len, HEADS, HEAD_DIM)
    key_seq = key_low.reshape(NSEQ, SEQ, KV_HEADS, HEAD_DIM)
    value_seq = value_low.reshape(NSEQ, SEQ, KV_HEADS, HEAD_DIM)
    seg_seq = segments.reshape(NSEQ, SEQ)
    checked = jax.checkpoint(attend_block)

    def one_sequence(operands):
        query_part, key_part, value_part, seg_part = operands
        starts = jnp.arange(blocks, dtype=jnp.int32) * block_len

        def one_block(block_operands):
            query_block, block_start = block_operands
            pos_query = block_start + jnp.arange(block_len, dtype=jnp.int32)
            seg_query = lax.dynamic_slice_in_dim(seg_part, block_start, block_len)
            return checked(query_block, key_part, value_part, seg_query, seg_part, pos_query)
        return lax.map(one_block, (query_part, starts))
    result = lax.map(one_sequence, (query_seq, key_seq, value_seq, seg_seq))
    return result.reshape(TOKENS, HEADS * HEAD_DIM)

def block_forward(inputs, masters, gains, segments):
    w_query, w_key, w_value, w_out, w_gate, w_up, w_down = [low(weight) for weight in masters]
    query_gain = gains[:HEAD_DIM]
    key_gain = gains[HEAD_DIM:2 * HEAD_DIM]
    attn_gain = gains[2 * HEAD_DIM:2 * HEAD_DIM + D]
    ffn_gain = gains[2 * HEAD_DIM + D:]
    inputs_low = low(inputs)
    query_pre = low_back(jnp.dot(inputs_low, w_query, precision=HIGH))
    key_pre = low_back(jnp.dot(inputs_low, w_key, precision=HIGH))
    value_low = low(low_back(jnp.dot(inputs_low, w_value, precision=HIGH)))
    positions = jnp.arange(TOKENS, dtype=jnp.int32) % SEQ
    cos_table, sin_table = rope_tables(positions)
    query_hat, key_hat = prepare_heads(query_pre, key_pre, query_gain, key_gain, cos_table, sin_table)
    attended = attention(low(query_hat), low(key_hat), value_low.reshape(TOKENS, KV_HEADS, HEAD_DIM), segments)
    mixed_low = low(low_back(attended))
    branch = low_back(jnp.dot(mixed_low, w_out, precision=HIGH))
    hidden_in = inputs + rms_norm(branch, attn_gain)
    hidden_low = low(hidden_in)
    gate_values = low_back(jnp.dot(hidden_low, w_gate, precision=HIGH))
    up_values = low_back(jnp.dot(hidden_low, w_up, precision=HIGH))
    inner_low = low(low_back(jax.nn.silu(gate_values) * up_values))
    ffn_out = low_back(jnp.dot(inner_low, w_down, precision=HIGH))
    return hidden_in + rms_norm(ffn_out, ffn_gain)

def newton_schulz(matrix):
    is_tall = matrix.shape[0] > matrix.shape[1]
    current = matrix.T if is_tall else matrix
    as_float = current.astype(jnp.float32)
    scale_norm = jnp.sqrt(jnp.sum(as_float * as_float))
    current = (as_float / (scale_norm + 1e-07)).astype(jnp.bfloat16)
    for iteration in range(NS_TURNS):
        gram_matrix = jnp.dot(current, current.T, preferred_element_type=jnp.float32).astype(jnp.bfloat16)
        square = jnp.dot(gram_matrix, gram_matrix, preferred_element_type=jnp.float32)
        polynomial = (COEF_SQUARE * gram_matrix.astype(jnp.float32) + COEF_CUBE * square).astype(jnp.bfloat16)
        current = (COEF_LINEAR * current.astype(jnp.float32) + jnp.dot(polynomial, current, preferred_element_type=jnp.float32)).astype(jnp.bfloat16)
    return current.T if is_tall else current

def reference(tokens, cotangent, segments, master_query, master_key, master_value, master_out, master_gate, master_up, master_down, moment_query, moment_key, moment_value, moment_out, moment_gate, moment_up, moment_down, gains, gain_first, gain_second):
    masters = (master_query, master_key, master_value, master_out, master_gate, master_up, master_down)
    moments = (moment_query, moment_key, moment_value, moment_out, moment_gate, moment_up, moment_down)

    def forward(inputs, weights, gain_vec):
        return block_forward(inputs, weights, gain_vec, segments)
    outputs, pullback = jax.vjp(forward, tokens.astype(jnp.float32), masters, gains)
    grad_tokens, grads, gain_grads = pullback(cotangent.astype(jnp.float32))
    new_moments = []
    new_masters = []
    for master, grad_part, moment in zip(masters, grads, moments):
        moment_new = MOMENTUM * moment + grad_part
        orthogonal = newton_schulz((grad_part + MOMENTUM * moment_new).astype(jnp.bfloat16))
        step_scale = max(1.0, master.shape[1] / master.shape[0]) ** 0.5
        new_moments.append(moment_new)
        new_masters.append(master * (1.0 - MUON_RATE * MUON_DECAY) - MUON_RATE * step_scale * orthogonal.astype(jnp.float32))
    first_new = BETA_FIRST * gain_first + (1.0 - BETA_FIRST) * gain_grads
    second_new = BETA_SECOND * gain_second + (1.0 - BETA_SECOND) * gain_grads * gain_grads
    gains_new = gains - GAIN_RATE * (first_new / (1.0 - BETA_FIRST ** STEP)) / (jnp.sqrt(second_new / (1.0 - BETA_SECOND ** STEP)) + ADAM_EPS)
    return (outputs.astype(jnp.bfloat16), grad_tokens, grads[0], grads[1], grads[2], grads[3], grads[4], grads[5], grads[6], new_moments[0], new_moments[1], new_moments[2], new_moments[3], new_moments[4], new_moments[5], new_moments[6], new_masters[0], new_masters[1], new_masters[2], new_masters[3], new_masters[4], new_masters[5], new_masters[6], gain_grads, second_new, gains_new)
```

```python
import functools

import jax
import jax.numpy as jnp
from jax import lax
from jax.experimental import pallas as pl
from jax.experimental.pallas import tpu as pltpu
from jax.sharding import PartitionSpec as P

D = 1024
HEADS = 16
KV_HEADS = 8
HEAD_DIM = 128
FF = 3072
NS_TURNS = 5
STEP = 10
GROUP = 2

EPS_NORM = 1e-06
ROPE_BASE = 1000000.0
MOMENTUM = 0.95
MUON_RATE = 0.5
MUON_DECAY = 0.1
BETA_FIRST = 0.9
BETA_SECOND = 0.95
GAIN_RATE = 0.6
ADAM_EPS = 1e-08
COEF_LINEAR = 3.4445
COEF_SQUARE = -4.775
COEF_CUBE = 2.0315
MASKED = -1e30

BF = jnp.bfloat16
F32 = jnp.float32
NT = (((1,), (1,)), ((), ()))
TN = (((0,), (0,)), ((), ()))


def dot(a, b):
    return jnp.dot(a, b, preferred_element_type=F32)


def dot_nt(a, b):
    return lax.dot_general(a, b, NT, preferred_element_type=F32)


def dot_tn(a, b):
    return lax.dot_general(a, b, TN, preferred_element_type=F32)


def params(*semantics, limit=32):
    return pltpu.CompilerParams(
        dimension_semantics=semantics or None, vmem_limit_bytes=limit * 1024 * 1024
    )


def cost(flops, moved, exps=0):
    return pl.CostEstimate(flops=int(flops), bytes_accessed=int(moved), transcendentals=int(exps))


def xor_permute(value, axis, size, mask):
    return lax.ppermute(value, axis, [(i, i ^ mask) for i in range(size)])


def exchange(blocks, size):
    return [blocks[0]] + [xor_permute(blocks[r], "shard", size, r) for r in range(1, size)]


def gather_blocks(value, size):
    if size != 4:
        return exchange([value] * size, size)
    half = value.shape[0] // 2
    low, high = value[:half], value[half:]
    low_two = xor_permute(low, "shard", size, 2)
    high_one = xor_permute(high, "shard", size, 1)
    high_two = xor_permute(high, "shard", size, 2)
    low_one = xor_permute(low, "shard", size, 1)
    low_three = xor_permute(low_two, "shard", size, 1)
    high_three = xor_permute(high_one, "shard", size, 2)
    return [
        value,
        jnp.concatenate([low_one, high_one], axis=0),
        jnp.concatenate([low_two, high_two], axis=0),
        jnp.concatenate([low_three, high_three], axis=0),
    ]


def pick(stacked, place):
    return lax.dynamic_index_in_dim(stacked, place, 0, keepdims=False)


def in_order(blocks, place):
    stacked = jnp.stack(blocks)
    return [pick(stacked, place ^ r) for r in range(len(blocks))]


def to_other_core(value, copies, from_core):
    return lax.ppermute(value, "dp", [(i + from_core, i + 1 - from_core) for i in range(0, copies, 2)])


def send_one_core(value, copies, size, mask, core, sources=None, targets=None):
    pairs = []
    for copy in range(core, copies, 2):
        for i in range(size):
            if sources is not None and i not in sources:
                continue
            if targets is not None and i ^ mask not in targets:
                continue
            pairs.append((copy * size + i, copy * size + (i ^ mask)))
    return lax.ppermute(value, ("dp", "shard"), pairs)


def pack_kernel(spots, *refs):
    *weights, packed = refs
    start = 0
    for weight in weights:
        width = weight.shape[1]
        packed[:, start : start + width] = weight[...].astype(BF)
        start += width


def pack(weights, spots, size):
    edge = weights[0].shape[0]
    widths = [w.shape[1] // size for w in weights]
    return pl.pallas_call(
        pack_kernel,
        grid_spec=pltpu.PrefetchScalarGridSpec(
            num_scalar_prefetch=1,
            grid=(size,),
            in_specs=[
                pl.BlockSpec((edge // 2, n), lambda r, spots: (spots[size], spots[r])) for n in widths
            ],
            out_specs=pl.BlockSpec((edge // 2, sum(widths)), lambda r, spots: (r, 0)),
        ),
        out_shape=jax.ShapeDtypeStruct((size * edge // 2, sum(widths)), BF),
        compiler_params=params("arbitrary", limit=16),
        cost_estimate=cost(0, 3 * size * edge * sum(widths)),
        name="pack",
    )(spots, *weights)


def pack_first_kernel(spots, tokens, extra, *refs):
    *weights, packed = refs
    rows, half = tokens.shape[0], weights[0].shape[0]
    packed[:rows, :] = tokens[...]
    start = 0
    for weight in weights:
        width = weight.shape[1]
        packed[rows : rows + half, start : start + width] = weight[...].astype(BF)
        start += width
    if start < packed.shape[1]:
        packed[rows : rows + half, start:] = jnp.zeros((half, packed.shape[1] - start), BF)
    packed[rows + half :, :] = extra[...]


def pack_first(tokens, extra, weights, spots, size):
    edge = weights[0].shape[0]
    widths = [w.shape[1] // size for w in weights]
    packed_rows = tokens.shape[0] + edge // 2 + extra.shape[0]
    return pl.pallas_call(
        pack_first_kernel,
        grid_spec=pltpu.PrefetchScalarGridSpec(
            num_scalar_prefetch=1,
            grid=(size,),
            in_specs=[
                pl.BlockSpec(tokens.shape, lambda r, spots: (0, 0)),
                pl.BlockSpec(extra.shape, lambda r, spots: (0, 0)),
            ]
            + [
                pl.BlockSpec((edge // 2, n), lambda r, spots: (spots[size], spots[r])) for n in widths
            ],
            out_specs=pl.BlockSpec((packed_rows, D), lambda r, spots: (r, 0)),
        ),
        out_shape=jax.ShapeDtypeStruct((size * packed_rows, D), BF),
        compiler_params=params("arbitrary", limit=16),
        cost_estimate=cost(0, 3 * size * edge * sum(widths)),
        name="pack_first",
    )(spots, tokens, extra, *weights)


def assemble_into(out, spots, mine, other):
    size = len(mine)
    half = out.shape[0] // (2 * size)
    core = spots[size]
    for r in range(size):
        for pieces, at in ((mine, core), (other, 1 - core)):
            rows = pl.ds(pl.multiple_of((2 * spots[r] + at) * half, half), half)
            out[rows, :] = pieces[r][...]


def assemble_kernel(spots, *refs):
    *pieces, out = refs
    size = len(pieces) // 2
    assemble_into(out, spots, pieces[:size], pieces[size:])


def assemble(pieces, spots):
    size = len(pieces) // 2
    half, cols = pieces[1].shape
    spec = pl.BlockSpec((half, cols), lambda i, spots: (0, 0))
    return pl.pallas_call(
        assemble_kernel,
        grid_spec=pltpu.PrefetchScalarGridSpec(
            num_scalar_prefetch=1,
            grid=(1,),
            in_specs=[spec] * (2 * size),
            out_specs=pl.BlockSpec((2 * size * half, cols), lambda i, spots: (0, 0)),
        ),
        out_shape=jax.ShapeDtypeStruct((2 * size * half, cols), BF),
        compiler_params=params("arbitrary", limit=24),
        cost_estimate=cost(0, 8 * size * half * cols),
        name="assemble",
    )(spots, *pieces)


def project_kernel(spots, gain_q, gain_k, cos, sin, *refs):
    *inputs, q_out, k_out, v_out, pre_out, w = refs
    size = len(inputs) // 3
    x_refs, pieces = inputs[:size], inputs[size:]

    @pl.when(pl.program_id(0) == 0)
    def _():
        assemble_into(w, spots, pieces[:size], pieces[size:])

    for r in range(size):
        pl.when(pl.program_id(0) == r)(
            functools.partial(
                project_block, x_refs[r], gain_q, gain_k, cos, sin, q_out, k_out, v_out, pre_out, w
            )
        )


def project_block(x, gain_q, gain_k, cos, sin, q_out, k_out, v_out, pre_out, w):
    heads_q = q_out.shape[1] // HEAD_DIM
    heads_k = k_out.shape[1] // HEAD_DIM
    cos_now, sin_now = cos[...], sin[...]
    for head in range(heads_q + 2 * heads_k):
        cols = slice(head * HEAD_DIM, (head + 1) * HEAD_DIM)
        if head % 2 == 0:
            wide = slice(head * HEAD_DIM, min(head + 2, heads_q + 2 * heads_k) * HEAD_DIM)
            both = dot(x[...], w[:, wide])
        pre = both[:, (head % 2) * HEAD_DIM : (head % 2 + 1) * HEAD_DIM]
        if head >= heads_q + heads_k:
            at = head - heads_q - heads_k
            v_out[:, at * HEAD_DIM : (at + 1) * HEAD_DIM] = pre.astype(BF)
            continue
        pre_out[:, cols] = pre
        inverse = lax.rsqrt(jnp.mean(pre * pre, axis=-1, keepdims=True) + EPS_NORM)
        normed = pre * inverse * (gain_q[...] if head < heads_q else gain_k[...])
        turned = normed * cos_now + rotate_half(normed) * sin_now
        if head < heads_q:
            q_out[:, cols] = (turned * HEAD_DIM ** (-0.5)).astype(BF)
        else:
            at = head - heads_q
            k_out[:, at * HEAD_DIM : (at + 1) * HEAD_DIM] = turned.astype(BF)


def project(messages, others, part, gain_q, gain_k, cos, sin, spots, heads_q, heads_k):
    size = len(messages)
    rows = part * size
    half, cols = others[0].shape
    width = 2 * size * half
    there = lambda r, spots: (spots[r], 0)
    whole = lambda r, spots: (0, 0)
    near = pl.BlockSpec((half, cols), lambda r, spots: (part // half, 0))
    widths = (heads_q * HEAD_DIM, heads_k * HEAD_DIM, heads_k * HEAD_DIM, (heads_q + heads_k) * HEAD_DIM)
    return pl.pallas_call(
        project_kernel,
        grid_spec=pltpu.PrefetchScalarGridSpec(
            num_scalar_prefetch=1,
            grid=(size,),
            in_specs=[
                pl.BlockSpec((1, HEAD_DIM), whole),
                pl.BlockSpec((1, HEAD_DIM), whole),
                pl.BlockSpec((part, HEAD_DIM), there),
                pl.BlockSpec((part, HEAD_DIM), there),
            ]
            + [pl.BlockSpec((part, width), whole)] * size
            + [near] * size
            + [pl.BlockSpec((half, cols), whole)] * size,
            out_specs=[pl.BlockSpec((part, n), there) for n in widths]
            + [pl.BlockSpec((width, cols), whole)],
        ),
        out_shape=[
            jax.ShapeDtypeStruct((rows, n), F32 if i == 3 else BF) for i, n in enumerate(widths)
        ]
        + [jax.ShapeDtypeStruct((width, cols), BF)],
        compiler_params=params("arbitrary", limit=32),
        cost_estimate=cost(2 * rows * width * cols, 2 * rows * width + 4 * width * cols + 6 * rows * cols),
        name="project",
    )(spots, gain_q, gain_k, cos, sin, *messages, *messages, *others)


def rotate_half(values):
    return pltpu.roll(values, HEAD_DIM // 2, 1)


def attend_kernel(q, k, v, first, o_out):
    rows = q.shape[0]
    part = min(256, rows)
    for i in range(rows // part):
        at = slice(i * part, (i + 1) * part)
        keys = (i + 1) * part
        scores = dot_nt(q[at, :], k[:keys, :])
        key_pos = lax.broadcasted_iota(jnp.int32, (part, keys), 1)
        row_pos = i * part + lax.broadcasted_iota(jnp.int32, (part, keys), 0)
        allowed = (key_pos >= first[at, :]) & (key_pos <= row_pos)
        masked = jnp.where(allowed, scores, MASKED)
        powers = jnp.exp(masked - jnp.max(masked, axis=-1, keepdims=True))
        weights = powers * (1.0 / jnp.sum(powers, axis=-1, keepdims=True))
        o_out[at, :] = dot(weights.astype(BF), v[:keys, :]).astype(BF)


def attend(q, k, v, first):
    rows, cols = q.shape
    heads = cols // HEAD_DIM
    return pl.pallas_call(
        attend_kernel,
        grid=(heads,),
        in_specs=[
            pl.BlockSpec((rows, HEAD_DIM), lambda h: (0, h)),
            pl.BlockSpec((rows, HEAD_DIM), lambda h: (0, h // GROUP)),
            pl.BlockSpec((rows, HEAD_DIM), lambda h: (0, h // GROUP)),
            pl.BlockSpec((rows, 1), lambda h: (0, 0)),
        ],
        out_specs=pl.BlockSpec((rows, HEAD_DIM), lambda h: (0, h)),
        out_shape=jax.ShapeDtypeStruct((rows, cols), BF),
        compiler_params=params("arbitrary"),
        cost_estimate=cost(3 * rows * rows * cols, 6 * rows * cols, heads * rows * rows),
        name="attend",
    )(q, k, v, first)


def attend_back_kernel(q, k, v, do, first, dq_out, dk_out, dv_out):
    rows = q.shape[0]
    part = min(256, rows)
    k_turned = k[...].T
    dk_out[...] = jnp.zeros_like(dk_out)
    dv_out[...] = jnp.zeros_like(dv_out)
    for head in range(GROUP):
        cols = slice(head * HEAD_DIM, (head + 1) * HEAD_DIM)
        for i in range(rows // part):
            at = slice(i * part, (i + 1) * part)
            keys = (i + 1) * part
            q_now, do_now = q[at, cols], do[at, cols]
            scores = dot_nt(k[:keys, :], q_now)
            key_pos = lax.broadcasted_iota(jnp.int32, (keys, part), 0)
            row_pos = i * part + lax.broadcasted_iota(jnp.int32, (keys, part), 1)
            allowed = (key_pos >= first[:, at]) & (key_pos <= row_pos)
            masked = jnp.where(allowed, scores, MASKED)
            powers = jnp.exp(masked - jnp.max(masked, axis=0, keepdims=True))
            weights = powers * (1.0 / jnp.sum(powers, axis=0, keepdims=True))
            dv_out[:keys, :] += dot(weights.astype(BF), do_now)
            dweights = dot_nt(v[:keys, :], do_now)
            delta = jnp.sum(weights * dweights, axis=0, keepdims=True)
            dscores = (weights * (dweights - delta)).astype(BF)
            dk_out[:keys, :] += dot(dscores, q_now)
            dq_out[at, cols] = dot(k_turned[:, :keys], dscores).T


def attend_back(q, k, v, do, first):
    rows, cols = q.shape
    groups = k.shape[1] // HEAD_DIM
    wide = pl.BlockSpec((rows, GROUP * HEAD_DIM), lambda g: (0, g))
    thin = pl.BlockSpec((rows, HEAD_DIM), lambda g: (0, g))
    return pl.pallas_call(
        attend_back_kernel,
        grid=(groups,),
        in_specs=[wide, thin, thin, wide, pl.BlockSpec((1, rows), lambda g: (0, 0))],
        out_specs=[wide, thin, thin],
        out_shape=[
            jax.ShapeDtypeStruct((rows, cols), F32),
            jax.ShapeDtypeStruct(k.shape, F32),
            jax.ShapeDtypeStruct(k.shape, F32),
        ],
        compiler_params=params("arbitrary"),
        cost_estimate=cost(7 * rows * rows * cols, 16 * rows * cols, rows * rows * cols // HEAD_DIM),
        name="attend_back",
    )(q, k, v, do, first)


def out_kernel(perm, o, w, a_out):
    a_out[...] = dot(o[...], w[...]).astype(BF)


def project_out(o, w, perm):
    rows, width = o.shape
    blocks = perm.shape[0]
    part = rows // blocks
    return pl.pallas_call(
        out_kernel,
        grid_spec=pltpu.PrefetchScalarGridSpec(
            num_scalar_prefetch=1,
            grid=(blocks,),
            in_specs=[
                pl.BlockSpec((part, width), lambda r, perm: (perm[r], 0)),
                pl.BlockSpec(w.shape, lambda r, perm: (0, 0)),
            ],
            out_specs=pl.BlockSpec((part, w.shape[1]), lambda r, perm: (r, 0)),
        ),
        out_shape=jax.ShapeDtypeStruct((rows, w.shape[1]), BF),
        compiler_params=params("arbitrary"),
        cost_estimate=cost(2 * rows * width * w.shape[1], 2 * rows * (width + D) + 2 * w.size),
        name="project_out",
    )(perm, o, w)


def out_back_kernel(perm, da, w, do_out, da_out):
    da_out[...] = da[...]
    do_out[...] = dot_nt(da[...], w[...]).astype(BF)


def project_out_back(da_rel, w, perm):
    rows, width = da_rel.shape
    blocks = perm.shape[0]
    part = rows // blocks
    return pl.pallas_call(
        out_back_kernel,
        grid_spec=pltpu.PrefetchScalarGridSpec(
            num_scalar_prefetch=1,
            grid=(blocks,),
            in_specs=[
                pl.BlockSpec((part, width), lambda r, perm: (r, 0)),
                pl.BlockSpec(w.shape, lambda r, perm: (0, 0)),
            ],
            out_specs=[
                pl.BlockSpec((part, w.shape[0]), lambda r, perm: (perm[r], 0)),
                pl.BlockSpec((part, width), lambda r, perm: (perm[r], 0)),
            ],
        ),
        out_shape=[
            jax.ShapeDtypeStruct((rows, w.shape[0]), BF),
            jax.ShapeDtypeStruct((rows, width), BF),
        ],
        compiler_params=params("arbitrary"),
        cost_estimate=cost(2 * rows * width * w.shape[0], 4 * rows * width + 2 * w.size),
        name="project_out_back",
    )(perm, da_rel, w)


def feed_kernel(h, w_gate, w_up, w_down, gate_out, up_out, hid_out, f_out, total):
    step = pl.program_id(0)
    gate = dot(h[...], w_gate[...])
    up = dot(h[...], w_up[...])
    gate_out[...] = gate
    up_out[...] = up
    hid = (gate * (1.0 / (1.0 + jnp.exp(-gate))) * up).astype(BF)
    hid_out[...] = hid
    part = dot(hid, w_down[...])

    @pl.when(step == 0)
    def _():
        total[...] = part

    @pl.when(step > 0)
    def _():
        total[...] += part

    @pl.when(step == pl.num_programs(0) - 1)
    def _():
        f_out[...] = total[...].astype(BF)


def feed(h, w_in, w_down):
    rows = h.shape[0]
    width = w_down.shape[0]
    tile = width // 3
    cols = lambda i: (0, i)
    return pl.pallas_call(
        feed_kernel,
        grid=(3,),
        in_specs=[
            pl.BlockSpec((rows, D), lambda i: (0, 0)),
            pl.BlockSpec((D, tile), cols),
            pl.BlockSpec((D, tile), lambda i: (0, i + 3)),
            pl.BlockSpec((tile, D), lambda i: (i, 0)),
        ],
        out_specs=[pl.BlockSpec((rows, tile), cols)] * 3
        + [pl.BlockSpec((rows, D), lambda i: (0, 0))],
        out_shape=[
            jax.ShapeDtypeStruct((rows, width), F32),
            jax.ShapeDtypeStruct((rows, width), F32),
            jax.ShapeDtypeStruct((rows, width), BF),
            jax.ShapeDtypeStruct((rows, D), BF),
        ],
        scratch_shapes=[pltpu.VMEM((rows, D), F32)],
        compiler_params=params("arbitrary", limit=24),
        cost_estimate=cost(6 * rows * width * D, 6 * width * D + 10 * rows * width + 4 * rows * D, rows * width),
        name="feed",
    )(h, w_in, w_in, w_down)


def feed_back_kernel(df, gate_in, up_in, w_gate, w_up, w_down, dgate_out, dup_out, dh_out, total):
    step = pl.program_id(0)
    dhid = dot_nt(df[...], w_down[...]).astype(BF).astype(F32)
    gate, up = gate_in[...], up_in[...]
    sigma = 1.0 / (1.0 + jnp.exp(-gate))
    dgate = (dhid * up * sigma * (1.0 + gate * (1.0 - sigma))).astype(BF)
    dup = (dhid * (gate * sigma)).astype(BF)
    dgate_out[...] = dgate
    dup_out[...] = dup
    part = dot_nt(dgate, w_gate[...]) + dot_nt(dup, w_up[...])

    @pl.when(step == 0)
    def _():
        total[...] = part

    @pl.when(step > 0)
    def _():
        total[...] += part

    @pl.when(step == pl.num_programs(0) - 1)
    def _():
        dh_out[...] = total[...].astype(BF)


def feed_back(df, gate, up, w_in, w_down):
    rows = df.shape[0]
    width = w_down.shape[0]
    tile = width // 3
    cols = lambda i: (0, i)
    return pl.pallas_call(
        feed_back_kernel,
        grid=(3,),
        in_specs=[
            pl.BlockSpec((rows, D), lambda i: (0, 0)),
            pl.BlockSpec((rows, tile), cols),
            pl.BlockSpec((rows, tile), cols),
            pl.BlockSpec((D, tile), cols),
            pl.BlockSpec((D, tile), lambda i: (0, i + 3)),
            pl.BlockSpec((tile, D), lambda i: (i, 0)),
        ],
        out_specs=[pl.BlockSpec((rows, tile), cols)] * 2
        + [pl.BlockSpec((rows, D), lambda i: (0, 0))],
        out_shape=[
            jax.ShapeDtypeStruct((rows, width), BF),
            jax.ShapeDtypeStruct((rows, width), BF),
            jax.ShapeDtypeStruct((rows, D), BF),
        ],
        scratch_shapes=[pltpu.VMEM((rows, D), F32)],
        compiler_params=params("arbitrary", limit=24),
        cost_estimate=cost(6 * rows * width * D, 6 * width * D + 12 * rows * width + 4 * rows * D, rows * width),
        name="feed_back",
    )(df, gate, up, w_in, w_in, w_down)


def project_back_kernel(
    perm, dq, dk, dv, pre_in, w, gain_q, gain_k, cos, sin, dqkv_out, dx_out, dgain_out
):
    heads_q = dq.shape[1] // HEAD_DIM
    heads_k = dk.shape[1] // HEAD_DIM

    @pl.when(pl.program_id(0) == 0)
    def _():
        dgain_out[...] = jnp.zeros_like(dgain_out)

    cos_now, sin_now = cos[...], sin[...]
    for head in range(heads_q + heads_k):
        cols = slice(head * HEAD_DIM, (head + 1) * HEAD_DIM)
        if head < heads_q:
            grad = dq[:, cols] * HEAD_DIM ** (-0.5)
            gain = gain_q[...]
        else:
            grad = dk[:, (head - heads_q) * HEAD_DIM : (head - heads_q + 1) * HEAD_DIM]
            gain = gain_k[...]
        turned = grad * cos_now - rotate_half(grad) * sin_now
        pre = pre_in[:, cols]
        inverse = lax.rsqrt(jnp.mean(pre * pre, axis=-1, keepdims=True) + EPS_NORM)
        scaled = gain * turned
        inner = jnp.mean(pre * scaled, axis=-1, keepdims=True)
        dqkv_out[:, cols] = (inverse * scaled - pre * (inverse * inverse * inverse * inner)).astype(BF)
        row = 0 if head < heads_q else 1
        dgain_out[row : row + 1, :] += jnp.sum(turned * pre * inverse, axis=0, keepdims=True)
    dqkv_out[:, (heads_q + heads_k) * HEAD_DIM :] = dv[...].astype(BF)
    dx_out[...] = dot_nt(dqkv_out[...], w[...]).astype(BF)


def project_back(dq, dk, dv, pre, w, gain_q, gain_k, cos, sin, perm):
    rows = dq.shape[0]
    blocks = perm.shape[0]
    part = rows // blocks
    width, cols = w.shape
    there = lambda r, perm: (perm[r], 0)
    here = lambda r, perm: (r, 0)
    whole = lambda r, perm: (0, 0)
    return pl.pallas_call(
        project_back_kernel,
        grid_spec=pltpu.PrefetchScalarGridSpec(
            num_scalar_prefetch=1,
            grid=(blocks,),
            in_specs=[
                pl.BlockSpec((part, dq.shape[1]), there),
                pl.BlockSpec((part, dk.shape[1]), there),
                pl.BlockSpec((part, dv.shape[1]), there),
                pl.BlockSpec((part, pre.shape[1]), there),
                pl.BlockSpec((width, cols), whole),
                pl.BlockSpec((1, HEAD_DIM), whole),
                pl.BlockSpec((1, HEAD_DIM), whole),
                pl.BlockSpec((part, HEAD_DIM), there),
                pl.BlockSpec((part, HEAD_DIM), there),
            ],
            out_specs=[
                pl.BlockSpec((part, cols), here),
                pl.BlockSpec((part, width), here),
                pl.BlockSpec((8, HEAD_DIM), whole),
            ],
        ),
        out_shape=[
            jax.ShapeDtypeStruct((rows, cols), BF),
            jax.ShapeDtypeStruct((rows, width), BF),
            jax.ShapeDtypeStruct((8, HEAD_DIM), F32),
        ],
        compiler_params=params("arbitrary"),
        cost_estimate=cost(2 * rows * width * cols, 10 * rows * cols + 2 * rows * width + 2 * w.size),
        name="project_back",
    )(perm, dq, dk, dv, pre, w, gain_q, gain_k, cos, sin)


def grad_first_kernel(size, *refs):
    lefts, rights, out = refs[:size], refs[size : 2 * size], refs[-1]
    value = dot_tn(lefts[0][...], rights[0][...])
    for r in range(1, size):
        value += dot_tn(lefts[r][...], rights[r][...])
    out[...] = value.astype(BF).reshape(out.shape)


def grad_down_bucket(hids, dfs, copies, units, size=None):
    count = len(hids)
    size = size or count
    rows, width = hids[0].shape
    edge = D // size
    strip = edge // copies
    return pl.pallas_call(
        functools.partial(grad_first_kernel, count),
        grid=(size,),
        in_specs=[pl.BlockSpec((rows, width), lambda i: (0, 0))] * count
        + [pl.BlockSpec((rows, edge), lambda i: (0, i))] * count,
        out_specs=pl.BlockSpec((copies, width // copies // strip, strip, edge), lambda i: (0, i, 0, 0)),
        out_shape=jax.ShapeDtypeStruct((copies, units, strip, edge), BF),
        compiler_params=params("arbitrary", limit=32),
        cost_estimate=cost(2 * size * rows * width * D, 2 * size * rows * (width + D) + 2 * width * D),
        name="grad_down",
    )(*hids, *dfs)


def grad_in_kernel(size, *refs):
    lefts, rights, out = refs[:size], refs[size : 2 * size], refs[-1]
    value = dot_tn(lefts[0][...], rights[0][...])
    for r in range(1, size):
        value += dot_tn(lefts[r][...], rights[r][...])
    copies, units, strip, edge = out.shape
    for unit in range(units):
        cols = slice(unit * edge, (unit + 1) * edge)
        out[:, unit] = value[:, cols].astype(BF).reshape(copies, strip, edge)


def grad_columns(lefts, rights, bucket, start, stride, size=None):
    count = len(lefts)
    size = size or count
    copies, _, strip, edge = bucket.shape
    width = rights[0].shape[1]
    rows = rights[0].shape[0]
    if all(right is rights[0] for right in rights):
        rows = rows // count
    units = width // edge
    row_blocks = range(count) if rights[0].shape[0] == count * rows else [0] * count
    return pl.pallas_call(
        functools.partial(grad_in_kernel, count),
        grid=(size,),
        in_specs=[pl.BlockSpec((rows, edge), lambda s: (0, s))] * count
        + [pl.BlockSpec((rows, width), lambda s, b=b: (b, 0)) for b in row_blocks]
        + [pl.BlockSpec(memory_space=pl.ANY)],
        out_specs=pl.BlockSpec(
            (copies, units, strip, edge), lambda s: (0, start // units + stride // units * s, 0, 0)
        ),
        out_shape=jax.ShapeDtypeStruct(bucket.shape, BF),
        input_output_aliases={2 * count: 0},
        compiler_params=params("arbitrary", limit=32),
        cost_estimate=cost(
            2 * size * rows * width * D, 2 * size * rows * (width + D) + 2 * width * D
        ),
        name="grad_columns",
    )(*lefts, *rights, bucket)


def wide_look(piece, moment_in, slots, slot):
    copies, units, strip, edge = piece.shape
    for unit in range(units):
        cols = slice(unit * edge, (unit + 1) * edge)
        grad = piece[:, unit].reshape(copies * strip, edge).astype(F32)
        moment = MOMENTUM * moment_in[:, cols] + grad
        slots[slot, 0, unit] = (grad + MOMENTUM * moment).astype(BF)


def tall_look(piece, moment_in, slots, slot):
    copies, strips, strip, edge = piece.shape
    grad = piece[...].astype(F32).reshape(copies * strips * strip, edge)
    moment = MOMENTUM * moment_in[...] + grad
    look = (grad + MOMENTUM * moment).astype(BF)
    for unit in range(look.shape[0] // edge):
        slots[slot, 0, unit] = look[unit * edge : (unit + 1) * edge, :].T


def look_kernel(talls, order, spots, *refs):
    count = len(talls)
    pieces, moments, slots = refs[:count], refs[count : 2 * count], refs[-1]
    for at in range(count):
        (tall_look if talls[at] else wide_look)(pieces[at], moments[at], slots, order[at])


def state_kernel(talls, spots, *refs):
    count = len(talls)
    pieces, moments = refs[:count], refs[count : 2 * count]
    grads, news = refs[2 * count : 3 * count], refs[3 * count : 4 * count]
    for at in range(count):
        copies, units, strip, edge = pieces[at].shape
        for unit in range(1 if talls[at] else units):
            if talls[at]:
                cols = slice(0, edge)
                grad = pieces[at][...].astype(F32).reshape(copies * units * strip, edge)
            else:
                cols = slice(unit * edge, (unit + 1) * edge)
                grad = pieces[at][:, unit].reshape(copies * strip, edge).astype(F32)
            grads[at][:, cols] = grad
            news[at][:, cols] = MOMENTUM * moments[at][:, cols] + grad


def state_spec(state, tall, size):
    rows, cols = state.shape
    if tall:
        return pl.BlockSpec((rows, D // size), lambda j, spots: (0, j))
    return pl.BlockSpec((rows, cols // size), lambda j, spots: (0, j))


def look_specs(whole, pieces, moments, talls, size):
    copies, _, strip, edge = whole.shape
    return [
        pl.BlockSpec((copies, units, strip, edge), functools.partial(where, size))
        for units, where in pieces
    ], [state_spec(m, tall, size) for m, tall in zip(moments, talls)]


def look(whole, pieces, moments, talls, order, slot_shape, spots, name):
    size = slot_shape[1]
    piece_specs, specs = look_specs(whole, pieces, moments, talls, size)
    return pl.pallas_call(
        functools.partial(look_kernel, talls, order),
        grid_spec=pltpu.PrefetchScalarGridSpec(
            num_scalar_prefetch=1,
            grid=(size,),
            in_specs=piece_specs + specs,
            out_specs=pl.BlockSpec(
                (slot_shape[0], 1) + slot_shape[2:], lambda j, spots: (0, j, 0, 0, 0)
            ),
        ),
        out_shape=jax.ShapeDtypeStruct(slot_shape, BF),
        compiler_params=params("arbitrary", limit=60),
        cost_estimate=cost(0, whole.size * 2 + 6 * sum(m.size for m in moments)),
        name=name,
    )(spots, *[whole] * len(pieces), *moments)


def state(whole, pieces, moments, talls, spots, size, name):
    piece_specs, specs = look_specs(whole, pieces, moments, talls, size)
    return pl.pallas_call(
        functools.partial(state_kernel, talls),
        grid_spec=pltpu.PrefetchScalarGridSpec(
            num_scalar_prefetch=1,
            grid=(size,),
            in_specs=piece_specs + specs,
            out_specs=specs + specs,
        ),
        out_shape=[jax.ShapeDtypeStruct(m.shape, F32) for m in moments] * 2,
        compiler_params=params("arbitrary", limit=60),
        cost_estimate=cost(0, whole.size * 2 + 12 * sum(m.size for m in moments)),
        name=name,
    )(spots, *[whole] * len(pieces), *moments)


def ortho_kernel(sizes, groups, info, *refs):
    inputs, outputs = refs[: len(groups)], refs[len(groups) : 2 * len(groups)]
    z, gram, poly = refs[2 * len(groups) :]
    subs, _, edge, _ = inputs[0].shape
    place, tall, units = info[0], info[1], info[2]

    def each_block(action):
        for index, (source, first) in enumerate(groups):
            for inner in range(inputs[index].shape[1]):
                unit = first + inner

                @pl.when(unit < units)
                def _():
                    def body(sub, carry):
                        action(index, source, inner, unit, sub)
                        return carry

                    lax.fori_loop(0, subs, body, 0)

    def target(source, unit, sub):
        at = source ^ place
        row = jnp.where(tall == 1, sub, at)
        col = unit * subs + jnp.where(tall == 1, at, sub)
        return (
            pl.ds(pl.multiple_of(row * edge, edge), edge),
            pl.ds(pl.multiple_of(col * edge, edge), edge),
        )

    def run(total_ref):
        total_ref[...] = jnp.zeros_like(total_ref)

        def add_square(index, source, inner, unit, sub):
            block = inputs[index][sub, inner].astype(F32)
            total_ref[...] += jnp.sum((block * block).reshape(edge // 8, 8, edge), axis=0)

        each_block(add_square)
        total = jnp.sum(total_ref[...], keepdims=True)
        total_ref[...] = jnp.broadcast_to(1.0 / (jnp.sqrt(total) + 1e-07), total_ref.shape)

        def put(index, source, inner, unit, sub):
            block = inputs[index][sub, inner].astype(F32) * total_ref[0:1, :]
            rows, cols = target(source, unit, sub)
            z[rows, cols] = block.astype(BF)

        each_block(put)

    tile = 256

    def turns(count):
        width = count * D

        def turn(step, carry):
            for j in range(D // tile):
                at, below = slice(j * tile, (j + 1) * tile), slice((j + 1) * tile, D)
                block = dot_nt(z[j * tile :, :width], z[at, :width]).astype(BF)
                gram[j * tile :, at] = block
                if j < D // tile - 1:
                    gram[at, below] = block[tile:].T
            for j in range(D // tile):
                at, below = slice(j * tile, (j + 1) * tile), slice((j + 1) * tile, D)
                square = dot(gram[j * tile :, :], gram[:, at])
                block = COEF_SQUARE * gram[j * tile :, at].astype(F32) + COEF_CUBE * square
                block = block.astype(BF)
                poly[j * tile :, at] = block
                if j < D // tile - 1:
                    poly[at, below] = block[tile:].T
            wide = min(width, 1024)

            def update(p, c):
                cols = pl.ds(pl.multiple_of(p * wide, wide), wide)
                now = z[:, cols]
                z[:, cols] = (COEF_LINEAR * now.astype(F32) + dot(poly[...], now)).astype(BF)
                return c

            lax.fori_loop(0, width // wide, update, 0)
            return carry

        lax.fori_loop(0, NS_TURNS, turn, 0)

    @pl.when(units > 0)
    def _():
        pl.run_scoped(run, pltpu.VMEM((8, edge), F32))

    for count in sizes:
        pl.when(units == count)(functools.partial(turns, count))

    def take(index, source, inner, unit, sub):
        rows, cols = target(source, unit, sub)
        outputs[index][sub, inner] = z[rows, cols]

    each_block(take)


def ortho(info, blocks, groups, sizes):
    spec = pl.BlockSpec(memory_space=pltpu.VMEM)
    return pl.pallas_call(
        functools.partial(ortho_kernel, sizes, groups),
        in_specs=[pl.BlockSpec(memory_space=pltpu.SMEM)] + [spec] * len(blocks),
        out_specs=[spec] * len(blocks),
        out_shape=[jax.ShapeDtypeStruct(b.shape, BF) for b in blocks],
        scratch_shapes=[
            pltpu.VMEM((D, max(sizes) * D), BF),
            pltpu.VMEM((D, D), BF),
            pltpu.VMEM((D, D), BF),
        ],
        compiler_params=params(limit=56),
        cost_estimate=cost(25e9 * max(sizes), 8e6 * max(sizes)),
        name="ortho",
    )(info, *blocks)


def master_step(out, master, columns, block, scale):
    out[:, columns] = master[:, columns] * (1.0 - MUON_RATE * MUON_DECAY) - scale * block.astype(F32)


def update_kernel(table, groups, spots, *refs):
    count = len(table)
    near, far = refs[: len(groups)], refs[len(groups) : 2 * len(groups)]
    masters = refs[2 * len(groups) : 2 * len(groups) + count]
    outs = refs[2 * len(groups) + count :]
    size = len(groups)
    for index, (source, first) in enumerate(groups):
        for chip, (at, tall, units) in enumerate(table):
            for piece, used in ((near, 1), (far, 0)):
                inner_units = [u for u in range(piece[index].shape[1]) if first + u < units]
                if not inner_units:
                    continue

                @pl.when((spots[source] == chip) & (spots[size + 1] == used))
                def _():
                    edge = piece[index].shape[2]
                    scale = MUON_RATE * (1.0 if tall else float(units) ** 0.5)
                    for inner in inner_units:
                        unit = first + inner
                        block = piece[index][0, inner]
                        span = slice(unit * edge, (unit + 1) * edge)
                        if tall:
                            outs[at][span, :] = masters[at][span, :] * (
                                1.0 - MUON_RATE * MUON_DECAY
                            ) - scale * block.T.astype(F32)
                        else:
                            master_step(outs[at], masters[at], span, block, scale)


def update(near, far, groups, table, masters, talls, spots, name):
    size = near[0].shape[0]
    specs = [state_spec(m, tall, size) for m, tall in zip(masters, talls)]

    def block_spec(value, used):
        shape = (1,) + value.shape[1:]
        return pl.BlockSpec(shape, lambda j, spots: (j * (spots[size + 1] == used), 0, 0, 0))

    return pl.pallas_call(
        functools.partial(update_kernel, table, groups),
        grid_spec=pltpu.PrefetchScalarGridSpec(
            num_scalar_prefetch=1,
            grid=(size,),
            in_specs=[block_spec(v, 1) for v in near] + [block_spec(v, 0) for v in far] + specs,
            out_specs=specs,
        ),
        out_shape=[jax.ShapeDtypeStruct(m.shape, F32) for m in masters],
        compiler_params=params("arbitrary", limit=60),
        cost_estimate=cost(0, 10 * sum(m.size for m in masters)),
        name=name,
    )(spots, *near, *far, *masters)


def norm_parts(values):
    return lax.rsqrt(jnp.mean(values * values, axis=-1, keepdims=True) + EPS_NORM)


def norm_back(values, gain, inverse, grad):
    scaled = gain * grad
    inner = jnp.mean(values * scaled, axis=-1, keepdims=True)
    return (
        inverse * scaled - values * (inverse * inverse * inverse * inner),
        jnp.sum(grad * values * inverse, axis=0),
    )


def on_device(
    tokens,
    cotangent,
    segments,
    master_query,
    master_key,
    master_value,
    master_out,
    master_gate,
    master_up,
    master_down,
    moment_query,
    moment_key,
    moment_value,
    moment_out,
    moment_gate,
    moment_up,
    moment_down,
    gains,
    gain_first,
    gain_second,
):
    size = lax.axis_size("shard")
    copies = lax.axis_size("dp")
    place = lax.axis_index("shard")
    core = lax.axis_index("dp") % 2
    part = tokens.shape[0]
    seq_len = part * size
    edge = D // size
    heads_q = HEADS // size
    heads_k = KV_HEADS // size
    perm = place ^ jnp.arange(size, dtype=jnp.int32)
    spots = jnp.concatenate([perm, jnp.stack([core, core, lax.axis_index("dp")]).astype(jnp.int32)])

    half = edge // 2
    qkv_cols = (heads_q + 2 * heads_k) * HEAD_DIM
    extra = jnp.pad(segments.astype(BF).reshape(1, part), ((0, 15), (0, D - part)))
    packed = pack_first(tokens, extra, [master_query, master_key, master_value], spots, size)
    packed = packed.reshape(size, -1, D)
    messages = exchange([packed[r] for r in range(size)], size)
    qkv_others = [xor_permute(m[part : part + half, :qkv_cols], "dp", copies, 1) for m in messages]
    later_spots, messages = lax.optimization_barrier((spots, messages))
    packed = pack([master_gate, master_up], later_spots, size).reshape(size, half, -1)
    in_pieces = exchange([packed[r] for r in range(size)], size)
    w_out, w_down = master_out.astype(BF), master_down.astype(BF)

    gain_q = gains[:HEAD_DIM].reshape(1, HEAD_DIM)
    gain_k = gains[HEAD_DIM : 2 * HEAD_DIM].reshape(1, HEAD_DIM)
    gain_a = gains[2 * HEAD_DIM : 2 * HEAD_DIM + D]
    gain_f = gains[2 * HEAD_DIM + D :]

    positions = jnp.arange(seq_len, dtype=jnp.int32)
    inverse_freq = ROPE_BASE ** (-(jnp.arange(HEAD_DIM // 2, dtype=F32) * 2.0 / HEAD_DIM))
    angles = positions.astype(F32)[:, None] * inverse_freq[None, :]
    cos_half, sin_half = jnp.cos(angles), jnp.sin(angles)
    cos = jnp.concatenate([cos_half, cos_half], axis=-1)
    sin = jnp.concatenate([-sin_half, sin_half], axis=-1)

    segment_blocks = [m[part + half, :part] for m in messages]
    seq_segments = jnp.concatenate(in_order(segment_blocks, place))
    first = jnp.sum(
        (seq_segments[None, :] < seq_segments[:, None]).astype(jnp.int32), axis=1, dtype=jnp.int32
    )

    def scatter(bucket):
        units = bucket.shape[1]
        flat = bucket.reshape(copies * units, *bucket.shape[2:])
        return lax.psum_scatter(flat, "dp", scatter_dimension=0, tiled=True)

    def to_rows(summed, start, units):
        shared = summed[start + size * units :]
        received = exchange(
            [
                jnp.concatenate(
                    [lax.dynamic_slice_in_dim(summed, start + (place ^ r) * units, units, 0), shared]
                )
                for r in range(size)
            ],
            size,
        )
        shared = sum(block[units:].astype(F32) for block in received).astype(BF)
        return jnp.concatenate([summed[:start], *[b[:units] for b in received], shared], axis=0)

    q_low, k_low, v_low, pre, w_qkv = project(
        messages, qkv_others, part, gain_q, gain_k, cos, sin, spots, heads_q, heads_k
    )
    q_low, in_pieces = lax.optimization_barrier((q_low, in_pieces))
    in_pieces = in_pieces + [xor_permute(piece, "dp", copies, 1) for piece in in_pieces]
    w_in = assemble(in_pieces, spots)
    o_low = attend(q_low, k_low, v_low, first.reshape(seq_len, 1))
    a_part = project_out(o_low, w_out, perm)

    def own_sum(partial):
        pieces = exchange([partial[r * part : (r + 1) * part] for r in range(size)], size)
        return sum(piece.astype(F32) for piece in pieces)

    a = own_sum(a_part)
    a_inverse = norm_parts(a)
    h = tokens.astype(F32) + a * a_inverse * gain_a
    h_blocks = gather_blocks(h.astype(BF), size)
    gates, ups, hids, f_parts = zip(*[feed(block, w_in, w_down) for block in h_blocks])
    f = sum(piece.astype(F32) for piece in exchange(list(f_parts), size))
    f_inverse = norm_parts(f)
    out_tokens = (h + f * f_inverse * gain_f).astype(BF)

    dy = cotangent.astype(F32)
    df, dgain_f = norm_back(f, gain_f, f_inverse, dy)
    df_blocks = gather_blocks(df.astype(BF), size)
    strip = edge // copies
    first_bucket = grad_down_bucket(hids, df_blocks, copies, 9 * size)
    dgates, dups, dh_parts = zip(
        *[
            feed_back(df_blocks[r], gates[r], ups[r], w_in, w_down)
            for r in range(size)
        ]
    )
    first_bucket = grad_columns(h_blocks, dgates, first_bucket, 3 * size, 6)
    first_bucket = grad_columns(h_blocks, dups, first_bucket, 3 * size + 3, 6)
    dh_pieces = exchange(list(dh_parts), size)
    dh_pieces, first_bucket = lax.optimization_barrier((dh_pieces, first_bucket))
    dh = dy + sum(piece.astype(F32) for piece in dh_pieces)
    first_sum = scatter(first_bucket)
    da, dgain_a = norm_back(a, gain_a, a_inverse, dh)
    da_blocks = gather_blocks(da.astype(BF), size)
    do_low, da_abs = project_out_back(jnp.concatenate(da_blocks, axis=0), w_out, perm)
    dq, dk, dv = attend_back(q_low, k_low, v_low, do_low, first.reshape(1, seq_len))
    dqkv, dx_part, dgain_qk = project_back(
        dq, dk, dv, pre, w_qkv, gain_q, gain_k, cos, sin, perm
    )
    first_sum, dqkv = lax.optimization_barrier((first_sum, dqkv))
    gain_terms = jnp.concatenate([dgain_qk[0], dgain_qk[1], dgain_a, dgain_f])
    gain_count = gain_terms.shape[0] // copies
    gain_unit = jnp.pad(
        gain_terms.astype(BF).reshape(copies, gain_count), ((0, 0), (0, strip * edge - gain_count))
    ).reshape(copies, 1, strip, edge)
    second_bucket = grad_down_bucket([o_low], [da_abs], copies, 6 * size + 1, size)
    second_bucket = lax.dynamic_update_slice(second_bucket, gain_unit, (0, 6 * size, 0, 0))
    second_bucket = grad_columns(messages, [dqkv] * size, second_bucket, 2 * size, 4)
    second_sum = scatter(second_bucket)
    dx = own_sum(dx_part)
    dx, second_sum = lax.optimization_barrier((dx, second_sum))
    grad_tokens = dh + dx

    first_whole = lax.all_gather(to_rows(first_sum, 3 * size, 6), "dp", axis=0)
    first_pieces = [
        (3, lambda size, j, spots: (0, size + 2 * spots[j], 0, 0)),
        (3, lambda size, j, spots: (0, size + 2 * spots[j] + 1, 0, 0)),
        (3, lambda size, j, spots: (0, j, 0, 0)),
    ]
    first_moments, first_talls = [moment_gate, moment_up, moment_down], (False, False, True)
    first_slots = look(
        first_whole,
        first_pieces,
        first_moments,
        first_talls,
        (0, 1, 2),
        (3, size, 3, edge, edge),
        spots,
        "look_first",
    )
    second_whole = lax.all_gather(to_rows(second_sum, 2 * size, 4), "dp", axis=0)
    def first_sent(r):
        return lax.dynamic_index_in_dim(first_slots, jnp.minimum(place ^ r, 2), 0, keepdims=False)

    three, four = (0, 1, 2), (0, 1, 2, 3)
    groups = tuple((r, 0) for r in range(size))
    first_in = [first_sent(0)] + [
        send_one_core(first_sent(r), copies, size, r, 0, targets=three) for r in range(1, size)
    ]
    is_two = (place == 2).astype(jnp.int32)
    first_units = jnp.where((core == 0) & (place < 3), 3, 0)
    second_units = jnp.where((core == 1) & (place < 4), jnp.where(place < 2, 1, 2), 0)
    first_info = jnp.stack([place, is_two, first_units]).astype(jnp.int32)
    second_info = jnp.stack([place, is_two, second_units]).astype(jnp.int32)
    first_made = ortho(first_info, first_in, groups, (3,))
    first_near = [first_made[0]] + [
        send_one_core(first_made[r], copies, size, r, 0, sources=three) for r in range(1, size)
    ]
    state_spots, first_made = lax.optimization_barrier((spots, first_made))
    first_state = state(
        first_whole, first_pieces, first_moments, first_talls, state_spots, size, "state_first"
    )
    second_whole, first_state = lax.optimization_barrier((second_whole, first_state))
    g_gate, g_up, g_down, n_gate, n_up, n_down = first_state
    second_pieces = [
        (2, lambda size, j, spots: (0, size + 2 * spots[j], 0, 0)),
        (1, lambda size, j, spots: (0, 2 * size + 4 * spots[j] + 2, 0, 0)),
        (1, lambda size, j, spots: (0, 2 * size + 4 * spots[j] + 3, 0, 0)),
        (2, lambda size, j, spots: (0, j, 0, 0)),
    ]
    second_moments = [moment_query, moment_key, moment_value, moment_out]
    second_talls = (False, False, False, True)
    second_slots = look(
        second_whole,
        second_pieces,
        second_moments,
        second_talls,
        (3, 0, 1, 2),
        (4, size, 2, edge, edge),
        spots,
        "look_second",
    )

    def second_sent(r):
        return lax.dynamic_index_in_dim(second_slots, jnp.minimum(place ^ r, 3), 0, keepdims=False)

    second_slots, first_near = lax.optimization_barrier((second_slots, first_near))
    second_in = [second_sent(0)] + [
        send_one_core(second_sent(r), copies, size, r, 1, targets=four) for r in range(1, size)
    ]
    second_made = ortho(second_info, second_in, groups, (1, 2))

    second_made, first_near = lax.optimization_barrier((second_made, first_near))
    first_far = [to_other_core(value, copies, 0) for value in first_near]
    second_near = [second_made[0]] + [
        send_one_core(second_made[r], copies, size, r, 1, sources=four) for r in range(1, size)
    ]
    g_query, g_key, g_value, g_out, n_query, n_key, n_value, n_out = state(
        second_whole, second_pieces, second_moments, second_talls, spots, size, "state_second"
    )
    first_spots = spots.at[size + 1].set((1 - core).astype(jnp.int32))
    u_gate, u_up, u_down = update(
        first_near,
        first_far,
        groups,
        ((0, False, 3), (1, False, 3), (2, True, 3)),
        [master_gate, master_up, master_down],
        (False, False, True),
        first_spots,
        "update_first",
    )
    second_near, first_done = lax.optimization_barrier(
        (second_near, ((u_gate, u_up, u_down), (g_query, g_key, g_value, g_out)))
    )
    (u_gate, u_up, u_down), (g_query, g_key, g_value, g_out) = first_done
    second_far = [to_other_core(value, copies, 1) for value in second_near]

    second_spots = spots.at[size + 1].set(core.astype(jnp.int32))
    u_key, u_value, u_out, u_query = update(
        second_near,
        second_far,
        groups,
        ((0, False, 1), (1, False, 1), (2, True, 2), (3, False, 2)),
        [master_key, master_value, master_out, master_query],
        (False, False, True, False),
        second_spots,
        "update_second",
    )
    grads = (g_query, g_key, g_value, g_out, g_gate, g_up, g_down)
    new_moments = (n_query, n_key, n_value, n_out, n_gate, n_up, n_down)
    new_masters = (u_query, u_key, u_value, u_out, u_gate, u_up, u_down)

    gain_part = gain_first.shape[0]
    gain_sums = second_whole[:, 6 * size].reshape(copies, strip * edge)[:, :gain_count]
    gain_grad = lax.dynamic_slice_in_dim(gain_sums.reshape(-1), place * gain_part, gain_part)
    gain_grad = gain_grad.astype(F32)
    own_gains = lax.dynamic_slice_in_dim(gains, place * gain_part, gain_part)
    first_new = BETA_FIRST * gain_first + (1.0 - BETA_FIRST) * gain_grad
    second_new = BETA_SECOND * gain_second + (1.0 - BETA_SECOND) * gain_grad * gain_grad
    gains_new = own_gains - GAIN_RATE * (first_new / (1.0 - BETA_FIRST**STEP)) / (
        jnp.sqrt(second_new / (1.0 - BETA_SECOND**STEP)) + ADAM_EPS
    )
    return (out_tokens, grad_tokens, *grads, *new_moments, *new_masters, gain_grad, second_new, gains_new)


def solution(mesh):
    rows = P(("dp", "shard"), None)
    state = P("shard", None)
    return jax.shard_map(
        on_device,
        mesh=mesh,
        in_specs=(rows, rows, P(("dp", "shard")), *[state] * 14, P(), P("shard"), P("shard")),
        out_specs=(rows, rows, *[state] * 21, P("shard"), P("shard"), P("shard")),
        check_vma=False,
    )
```

```python
import functools

import jax
import jax.numpy as jnp
from jax import lax
from jax.experimental import pallas as pl
from jax.experimental.pallas import tpu as pltpu
from jax.sharding import PartitionSpec as P

D = 1024
HEADS = 16
KV_HEADS = 8
HEAD_DIM = 128
FF = 3072
NS_TURNS = 5
STEP = 10
DOCUMENTS = 4
GROUP = 2

EPS_NORM = 1e-06
ROPE_BASE = 1000000.0
MOMENTUM = 0.95
MUON_RATE = 0.5
MUON_DECAY = 0.1
BETA_FIRST = 0.9
BETA_SECOND = 0.95
GAIN_RATE = 0.6
ADAM_EPS = 1e-08
COEF_LINEAR = 3.4445
COEF_SQUARE = -4.775
COEF_CUBE = 2.0315
MASKED = -1e30

BF = jnp.bfloat16
F32 = jnp.float32
NT = (((1,), (1,)), ((), ()))
TN = (((0,), (0,)), ((), ()))


def dot(a, b):
    return jnp.dot(a, b, preferred_element_type=F32)


def dot_nt(a, b):
    return lax.dot_general(a, b, NT, preferred_element_type=F32)


def dot_tn(a, b):
    return lax.dot_general(a, b, TN, preferred_element_type=F32)


def params(*semantics, limit=32):
    return pltpu.CompilerParams(
        dimension_semantics=semantics or None, vmem_limit_bytes=limit * 1024 * 1024
    )


def cost(flops, moved, exps=0):
    return pl.CostEstimate(flops=int(flops), bytes_accessed=int(moved), transcendentals=int(exps))


def xor_permute(value, axis, size, mask):
    return lax.ppermute(value, axis, [(i, i ^ mask) for i in range(size)])


def exchange(blocks, size):
    return [blocks[0]] + [xor_permute(blocks[r], "shard", size, r) for r in range(1, size)]


def gather_blocks(value, size):
    if size != 4:
        return [[block] for block in exchange([value] * size, size)]
    half = value.shape[0] // 2
    low, high = value[:half], value[half:]
    low_two = xor_permute(low, "shard", size, 2)
    high_one = xor_permute(high, "shard", size, 1)
    high_two = xor_permute(high, "shard", size, 2)
    low_one = xor_permute(low, "shard", size, 1)
    low_three = xor_permute(low_two, "shard", size, 1)
    high_three = xor_permute(high_one, "shard", size, 2)
    return [[value], [low_one, high_one], [low_two, high_two], [low_three, high_three]]


def joined(blocks):
    return [jnp.concatenate(block, axis=0) if len(block) > 1 else block[0] for block in blocks]


def lay(parts, out):
    start = 0
    for part in parts:
        out[start : start + part.shape[0], :] = part[...]
        start += part.shape[0]


def pick(stacked, place):
    return lax.dynamic_index_in_dim(stacked, place, 0, keepdims=False)


def in_order(blocks, place):
    stacked = jnp.stack(blocks)
    return [pick(stacked, place ^ r) for r in range(len(blocks))]


def to_other_core(value, copies, from_core):
    return lax.ppermute(value, "dp", [(i + from_core, i + 1 - from_core) for i in range(0, copies, 2)])


def send_one_core(value, copies, size, mask, core, sources=None, targets=None):
    pairs = []
    for copy in range(core, copies, 2):
        for i in range(size):
            if sources is not None and i not in sources:
                continue
            if targets is not None and i ^ mask not in targets:
                continue
            pairs.append((copy * size + i, copy * size + (i ^ mask)))
    return lax.ppermute(value, ("dp", "shard"), pairs)


def pack_kernel(counts, spots, tail, *refs):
    weights, outs = refs[: sum(counts)], refs[sum(counts) :]
    size = len(outs) // len(counts)
    half = weights[0].shape[0]
    for group, count in enumerate(counts):
        for r in range(size):
            out = outs[group * size + r]
            start = 0
            for weight in weights[sum(counts[:group]) :][:count]:
                width = weight.shape[1] // size
                cols = pl.ds(pl.multiple_of(spots[r] * width, width), width)
                out[:half, start : start + width] = weight[:, cols].astype(BF)
                start += width
            if group == 0:
                out[half:, :] = tail[...]


def pack(groups, tail, spots, size):
    half = groups[0][0].shape[0] // 2
    whole = lambda i, spots: (0, 0)
    cols = [sum(w.shape[1] // size for w in group) for group in groups]
    weights = [w for group in groups for w in group]
    shapes = [
        (half + tail.shape[0] * (at == 0), n) for at, n in enumerate(cols) for _ in range(size)
    ]
    return pl.pallas_call(
        functools.partial(pack_kernel, [len(group) for group in groups]),
        grid_spec=pltpu.PrefetchScalarGridSpec(
            num_scalar_prefetch=1,
            grid=(1,),
            in_specs=[pl.BlockSpec(tail.shape, whole)]
            + [pl.BlockSpec((half, w.shape[1]), lambda i, spots: (spots[size], 0)) for w in weights],
            out_specs=[pl.BlockSpec(shape, whole) for shape in shapes],
        ),
        out_shape=[jax.ShapeDtypeStruct(shape, BF) for shape in shapes],
        compiler_params=params("arbitrary", limit=60),
        cost_estimate=cost(0, 1),
        name="pack",
    )(spots, tail, *weights)


def assemble_into(out, spots, mine, other):
    size = len(mine)
    half = out.shape[0] // (2 * size)
    core = spots[size]
    for r in range(size):
        for pieces, at in ((mine, core), (other, 1 - core)):
            rows = pl.ds(pl.multiple_of((2 * spots[r] + at) * half, half), half)
            out[rows, :] = pieces[r][...]


def assemble_kernel(spots, *refs):
    *pieces, out = refs
    size = len(pieces) // 2
    assemble_into(out, spots, pieces[:size], pieces[size:])


def assemble(pieces, spots):
    size = len(pieces) // 2
    half, cols = pieces[1].shape
    spec = pl.BlockSpec((half, cols), lambda i, spots: (0, 0))
    return pl.pallas_call(
        assemble_kernel,
        grid_spec=pltpu.PrefetchScalarGridSpec(
            num_scalar_prefetch=1,
            grid=(1,),
            in_specs=[spec] * (2 * size),
            out_specs=pl.BlockSpec((2 * size * half, cols), lambda i, spots: (0, 0)),
        ),
        out_shape=jax.ShapeDtypeStruct((2 * size * half, cols), BF),
        compiler_params=params("arbitrary", limit=24),
        cost_estimate=cost(0, 8 * size * half * cols),
        name="assemble",
    )(spots, *pieces)


def project_kernel(spots, gain_q, gain_k, cos, sin, *refs):
    *inputs, q_out, k_out, v_out, pre_out, w = refs
    size = len(inputs) // 3
    x_refs, pieces = inputs[:size], inputs[size:]

    @pl.when(pl.program_id(0) == 0)
    def _():
        assemble_into(w, spots, pieces[:size], pieces[size:])

    for r in range(size):
        pl.when(pl.program_id(0) == r)(
            functools.partial(
                project_block, x_refs[r], gain_q, gain_k, cos, sin, q_out, k_out, v_out, pre_out, w
            )
        )


def project_block(x, gain_q, gain_k, cos, sin, q_out, k_out, v_out, pre_out, w):
    heads_q = q_out.shape[1] // HEAD_DIM
    heads_k = k_out.shape[1] // HEAD_DIM
    cos_now, sin_now = cos[...], sin[...]
    for head in range(heads_q + 2 * heads_k):
        cols = slice(head * HEAD_DIM, (head + 1) * HEAD_DIM)
        if head % 2 == 0:
            wide = slice(head * HEAD_DIM, min(head + 2, heads_q + 2 * heads_k) * HEAD_DIM)
            both = dot(x[...], w[:, wide])
        pre = both[:, (head % 2) * HEAD_DIM : (head % 2 + 1) * HEAD_DIM]
        if head >= heads_q + heads_k:
            at = head - heads_q - heads_k
            v_out[:, at * HEAD_DIM : (at + 1) * HEAD_DIM] = pre.astype(BF)
            continue
        pre_out[:, cols] = pre
        inverse = lax.rsqrt(jnp.mean(pre * pre, axis=-1, keepdims=True) + EPS_NORM)
        normed = pre * inverse * (gain_q[...] if head < heads_q else gain_k[...])
        turned = normed * cos_now + rotate_half(normed) * sin_now
        if head < heads_q:
            q_out[:, cols] = (turned * HEAD_DIM ** (-0.5)).astype(BF)
        else:
            at = head - heads_q
            k_out[:, at * HEAD_DIM : (at + 1) * HEAD_DIM] = turned.astype(BF)


def project(x_blocks, mine, others, part, gain_q, gain_k, cos, sin, spots, heads_q, heads_k):
    size = len(x_blocks)
    rows = part * size
    cols = (heads_q + 2 * heads_k) * HEAD_DIM
    width = x_blocks[0].shape[1]
    half = width // size // 2
    there = lambda r, spots: (spots[r], 0)
    whole = lambda r, spots: (0, 0)
    piece_specs = [pl.BlockSpec((half, cols), whole)] * (2 * size)
    widths = (heads_q * HEAD_DIM, heads_k * HEAD_DIM, heads_k * HEAD_DIM, (heads_q + heads_k) * HEAD_DIM)
    return pl.pallas_call(
        project_kernel,
        grid_spec=pltpu.PrefetchScalarGridSpec(
            num_scalar_prefetch=1,
            grid=(size,),
            in_specs=[
                pl.BlockSpec((1, HEAD_DIM), whole),
                pl.BlockSpec((1, HEAD_DIM), whole),
                pl.BlockSpec((part, HEAD_DIM), there),
                pl.BlockSpec((part, HEAD_DIM), there),
            ]
            + [pl.BlockSpec((part, width), whole)] * size
            + piece_specs,
            out_specs=[pl.BlockSpec((part, n), there) for n in widths]
            + [pl.BlockSpec((width, cols), whole)],
        ),
        out_shape=[
            jax.ShapeDtypeStruct((rows, n), F32 if i == 3 else BF) for i, n in enumerate(widths)
        ]
        + [jax.ShapeDtypeStruct((width, cols), BF)],
        compiler_params=params("arbitrary", limit=32),
        cost_estimate=cost(2 * rows * width * cols, 2 * rows * width + 4 * width * cols + 6 * rows * cols),
        name="project",
    )(spots, gain_q, gain_k, cos, sin, *x_blocks, *mine, *others)


def rotate_half(values):
    return pltpu.roll(values, HEAD_DIM // 2, 1)


def attend_kernel(spots, q, k, v, *refs):
    *tails, o_out, first_out, first_col = refs
    rows = q.shape[0]
    part = min(256, rows)
    size = len(tails)
    block = rows // size

    @pl.when(pl.program_id(0) == 0)
    def _():
        for r in range(size):
            cols = pl.ds(pl.multiple_of(spots[r] * block, block), block)
            first_out[:, cols] = jnp.broadcast_to(tails[r][0:1, :block].astype(F32), (8, block))
        ids = first_out[...]
        found = jnp.zeros_like(ids)
        for document in range(1, DOCUMENTS):
            count = jnp.sum((ids == document - 1).astype(F32), axis=1, keepdims=True)
            found += jnp.where(ids >= document, count, 0.0)
        first_out[...] = found
        first_col[...] = jnp.broadcast_to(found[0:1, :], (128, rows)).T

    for i in range(rows // part):
        at = slice(i * part, (i + 1) * part)
        keys = (i + 1) * part
        scores = dot_nt(q[at, :], k[:keys, :])
        key_pos = lax.broadcasted_iota(jnp.int32, (part, keys), 1)
        row_pos = i * part + lax.broadcasted_iota(jnp.int32, (part, keys), 0)
        first = first_col[at, 0:1].astype(jnp.int32)
        allowed = (key_pos >= first) & (key_pos <= row_pos)
        masked = jnp.where(allowed, scores, MASKED)
        powers = jnp.exp(masked - jnp.max(masked, axis=-1, keepdims=True))
        weights = powers * (1.0 / jnp.sum(powers, axis=-1, keepdims=True))
        o_out[at, :] = dot(weights.astype(BF), v[:keys, :]).astype(BF)


def attend(q, k, v, messages, spots):
    rows, cols = q.shape
    heads = cols // HEAD_DIM
    tail = messages[0].shape[0] // 16 - 1
    return pl.pallas_call(
        attend_kernel,
        grid_spec=pltpu.PrefetchScalarGridSpec(
            num_scalar_prefetch=1,
            grid=(heads,),
            in_specs=[
                pl.BlockSpec((rows, HEAD_DIM), lambda h, spots: (0, h)),
                pl.BlockSpec((rows, HEAD_DIM), lambda h, spots: (0, h // GROUP)),
                pl.BlockSpec((rows, HEAD_DIM), lambda h, spots: (0, h // GROUP)),
            ]
            + [
                pl.BlockSpec((16, m.shape[1]), lambda h, spots: (tail, 0)) for m in messages
            ],
            out_specs=[
                pl.BlockSpec((rows, HEAD_DIM), lambda h, spots: (0, h)),
                pl.BlockSpec((8, rows), lambda h, spots: (0, 0)),
            ],
            scratch_shapes=[pltpu.VMEM((rows, 128), F32)],
        ),
        out_shape=[
            jax.ShapeDtypeStruct((rows, cols), BF),
            jax.ShapeDtypeStruct((8, rows), F32),
        ],
        compiler_params=params("arbitrary"),
        cost_estimate=cost(3 * rows * rows * cols, 6 * rows * cols, heads * rows * rows),
        name="attend",
    )(spots, q, k, v, *messages)


def attend_back_kernel(q, k, v, do, first, dq_out, dk_out, dv_out):
    rows = q.shape[0]
    part = min(256, rows)
    k_turned = k[...].T
    dk_out[...] = jnp.zeros_like(dk_out)
    dv_out[...] = jnp.zeros_like(dv_out)
    for head in range(GROUP):
        cols = slice(head * HEAD_DIM, (head + 1) * HEAD_DIM)
        for i in range(rows // part):
            at = slice(i * part, (i + 1) * part)
            keys = (i + 1) * part
            q_now, do_now = q[at, cols], do[at, cols]
            scores = dot_nt(k[:keys, :], q_now)
            key_pos = lax.broadcasted_iota(jnp.int32, (keys, part), 0)
            row_pos = i * part + lax.broadcasted_iota(jnp.int32, (keys, part), 1)
            allowed = (key_pos >= first[0:1, at].astype(jnp.int32)) & (key_pos <= row_pos)
            masked = jnp.where(allowed, scores, MASKED)
            powers = jnp.exp(masked - jnp.max(masked, axis=0, keepdims=True))
            weights = powers * (1.0 / jnp.sum(powers, axis=0, keepdims=True))
            dv_out[:keys, :] += dot(weights.astype(BF), do_now)
            dweights = dot_nt(v[:keys, :], do_now)
            delta = jnp.sum(weights * dweights, axis=0, keepdims=True)
            dscores = (weights * (dweights - delta)).astype(BF)
            dk_out[:keys, :] += dot(dscores, q_now)
            dq_out[at, cols] = dot(k_turned[:, :keys], dscores).T


def attend_back(q, k, v, do, first):
    rows, cols = q.shape
    groups = k.shape[1] // HEAD_DIM
    wide = pl.BlockSpec((rows, GROUP * HEAD_DIM), lambda g: (0, g))
    thin = pl.BlockSpec((rows, HEAD_DIM), lambda g: (0, g))
    return pl.pallas_call(
        attend_back_kernel,
        grid=(groups,),
        in_specs=[wide, thin, thin, wide, pl.BlockSpec((8, rows), lambda g: (0, 0))],
        out_specs=[wide, thin, thin],
        out_shape=[
            jax.ShapeDtypeStruct((rows, cols), F32),
            jax.ShapeDtypeStruct(k.shape, F32),
            jax.ShapeDtypeStruct(k.shape, F32),
        ],
        compiler_params=params("arbitrary"),
        cost_estimate=cost(7 * rows * rows * cols, 16 * rows * cols, rows * rows * cols // HEAD_DIM),
        name="attend_back",
    )(q, k, v, do, first)


def out_kernel(perm, o, w, a_out):
    a_out[...] = dot(o[...], w[...].astype(BF)).astype(BF)


def project_out(o, w, perm):
    rows, width = o.shape
    blocks = perm.shape[0]
    part = rows // blocks
    return pl.pallas_call(
        out_kernel,
        grid_spec=pltpu.PrefetchScalarGridSpec(
            num_scalar_prefetch=1,
            grid=(blocks,),
            in_specs=[
                pl.BlockSpec((part, width), lambda r, perm: (perm[r], 0)),
                pl.BlockSpec(w.shape, lambda r, perm: (0, 0)),
            ],
            out_specs=pl.BlockSpec((part, w.shape[1]), lambda r, perm: (r, 0)),
        ),
        out_shape=jax.ShapeDtypeStruct((rows, w.shape[1]), BF),
        compiler_params=params("arbitrary"),
        cost_estimate=cost(2 * rows * width * w.shape[1], 2 * rows * (width + D) + 2 * w.size),
        name="project_out",
    )(perm, o, w)


def out_back_kernel(counts, perm, *refs):
    *parts, w, do_out, da_out = refs
    for r in range(len(counts)):

        @pl.when(pl.program_id(0) == r)
        def _():
            start = sum(counts[:r])
            lay(parts[start : start + counts[r]], da_out)

    do_out[...] = dot_nt(da_out[...], w[...].astype(BF)).astype(BF)


def project_out_back(da_blocks, w, perm):
    blocks = perm.shape[0]
    parts = [part for block in da_blocks for part in block]
    width = parts[0].shape[1]
    rows = sum(part.shape[0] for part in parts)
    part = rows // blocks
    return pl.pallas_call(
        functools.partial(out_back_kernel, [len(block) for block in da_blocks]),
        grid_spec=pltpu.PrefetchScalarGridSpec(
            num_scalar_prefetch=1,
            grid=(blocks,),
            in_specs=[pl.BlockSpec(p.shape, lambda r, perm: (0, 0)) for p in parts]
            + [pl.BlockSpec(w.shape, lambda r, perm: (0, 0))],
            out_specs=[
                pl.BlockSpec((part, w.shape[0]), lambda r, perm: (perm[r], 0)),
                pl.BlockSpec((part, width), lambda r, perm: (perm[r], 0)),
            ],
        ),
        out_shape=[
            jax.ShapeDtypeStruct((rows, w.shape[0]), BF),
            jax.ShapeDtypeStruct((rows, width), BF),
        ],
        compiler_params=params("arbitrary"),
        cost_estimate=cost(2 * rows * width * w.shape[0], 4 * rows * width + 2 * w.size),
        name="project_out_back",
    )(perm, *parts, w)


def feed_kernel(*refs):
    *parts, w_gate, w_up, w_down, gate_out, up_out, hid_out, f_out, total, h = refs
    step = pl.program_id(0)

    @pl.when(step == 0)
    def _():
        lay(parts, h)

    gate = dot(h[...], w_gate[...])
    up = dot(h[...], w_up[...])
    gate_out[...] = gate
    up_out[...] = up
    hid = (gate * (1.0 / (1.0 + jnp.exp(-gate))) * up).astype(BF)
    hid_out[...] = hid
    part = dot(hid, w_down[...])

    @pl.when(step == 0)
    def _():
        total[...] = part

    @pl.when(step > 0)
    def _():
        total[...] += part

    @pl.when(step == pl.num_programs(0) - 1)
    def _():
        f_out[...] = total[...].astype(BF)


def feed(parts, w_in, w_down):
    rows = sum(part.shape[0] for part in parts)
    width = w_down.shape[0]
    tile = width // 3
    cols = lambda i: (0, i)
    return pl.pallas_call(
        feed_kernel,
        grid=(3,),
        in_specs=[
            *[pl.BlockSpec(part.shape, lambda i: (0, 0)) for part in parts],
            pl.BlockSpec((D, tile), cols),
            pl.BlockSpec((D, tile), lambda i: (0, i + 3)),
            pl.BlockSpec((tile, D), lambda i: (i, 0)),
        ],
        out_specs=[pl.BlockSpec((rows, tile), cols)] * 3
        + [pl.BlockSpec((rows, D), lambda i: (0, 0))],
        out_shape=[
            jax.ShapeDtypeStruct((rows, width), F32),
            jax.ShapeDtypeStruct((rows, width), F32),
            jax.ShapeDtypeStruct((rows, width), BF),
            jax.ShapeDtypeStruct((rows, D), BF),
        ],
        scratch_shapes=[pltpu.VMEM((rows, D), F32), pltpu.VMEM((rows, D), BF)],
        compiler_params=params("arbitrary", limit=24),
        cost_estimate=cost(1, 1),
        name="feed",
    )(*parts, w_in, w_in, w_down)


def feed_back_kernel(*refs):
    *parts, gate_in, up_in, w_gate, w_up, w_down, dgate_out, dup_out, dh_out, total, df = refs
    step = pl.program_id(0)

    @pl.when(step == 0)
    def _():
        lay(parts, df)

    dhid = dot_nt(df[...], w_down[...]).astype(BF).astype(F32)
    gate, up = gate_in[...], up_in[...]
    sigma = 1.0 / (1.0 + jnp.exp(-gate))
    dgate = (dhid * up * sigma * (1.0 + gate * (1.0 - sigma))).astype(BF)
    dup = (dhid * (gate * sigma)).astype(BF)
    dgate_out[...] = dgate
    dup_out[...] = dup
    part = dot_nt(dgate, w_gate[...]) + dot_nt(dup, w_up[...])

    @pl.when(step == 0)
    def _():
        total[...] = part

    @pl.when(step > 0)
    def _():
        total[...] += part

    @pl.when(step == pl.num_programs(0) - 1)
    def _():
        dh_out[...] = total[...].astype(BF)


def feed_back(parts, gate, up, w_in, w_down):
    rows = sum(part.shape[0] for part in parts)
    width = w_down.shape[0]
    tile = width // 3
    cols = lambda i: (0, i)
    return pl.pallas_call(
        feed_back_kernel,
        grid=(3,),
        in_specs=[
            *[pl.BlockSpec(part.shape, lambda i: (0, 0)) for part in parts],
            pl.BlockSpec((rows, tile), cols),
            pl.BlockSpec((rows, tile), cols),
            pl.BlockSpec((D, tile), cols),
            pl.BlockSpec((D, tile), lambda i: (0, i + 3)),
            pl.BlockSpec((tile, D), lambda i: (i, 0)),
        ],
        out_specs=[pl.BlockSpec((rows, tile), cols)] * 2
        + [pl.BlockSpec((rows, D), lambda i: (0, 0))],
        out_shape=[
            jax.ShapeDtypeStruct((rows, width), BF),
            jax.ShapeDtypeStruct((rows, width), BF),
            jax.ShapeDtypeStruct((rows, D), BF),
        ],
        scratch_shapes=[pltpu.VMEM((rows, D), F32), pltpu.VMEM((rows, D), BF)],
        compiler_params=params("arbitrary", limit=24),
        cost_estimate=cost(1, 1),
        name="feed_back",
    )(*parts, gate, up, w_in, w_in, w_down)


def project_back_kernel(
    perm, dq, dk, dv, pre_in, w, gain_q, gain_k, cos, sin, dqkv_out, dx_out, dgain_out
):
    heads_q = dq.shape[1] // HEAD_DIM
    heads_k = dk.shape[1] // HEAD_DIM

    @pl.when(pl.program_id(0) == 0)
    def _():
        dgain_out[...] = jnp.zeros_like(dgain_out)

    cos_now, sin_now = cos[...], sin[...]
    for head in range(heads_q + heads_k):
        cols = slice(head * HEAD_DIM, (head + 1) * HEAD_DIM)
        if head < heads_q:
            grad = dq[:, cols] * HEAD_DIM ** (-0.5)
            gain = gain_q[...]
        else:
            grad = dk[:, (head - heads_q) * HEAD_DIM : (head - heads_q + 1) * HEAD_DIM]
            gain = gain_k[...]
        turned = grad * cos_now - rotate_half(grad) * sin_now
        pre = pre_in[:, cols]
        inverse = lax.rsqrt(jnp.mean(pre * pre, axis=-1, keepdims=True) + EPS_NORM)
        scaled = gain * turned
        inner = jnp.mean(pre * scaled, axis=-1, keepdims=True)
        dqkv_out[:, cols] = (inverse * scaled - pre * (inverse * inverse * inverse * inner)).astype(BF)
        row = 0 if head < heads_q else 1
        dgain_out[row : row + 1, :] += jnp.sum(turned * pre * inverse, axis=0, keepdims=True)
    dqkv_out[:, (heads_q + heads_k) * HEAD_DIM :] = dv[...].astype(BF)
    dx_out[...] = dot_nt(dqkv_out[...], w[...]).astype(BF)


def project_back(dq, dk, dv, pre, w, gain_q, gain_k, cos, sin, perm):
    rows = dq.shape[0]
    blocks = perm.shape[0]
    part = rows // blocks
    width, cols = w.shape
    there = lambda r, perm: (perm[r], 0)
    here = lambda r, perm: (r, 0)
    whole = lambda r, perm: (0, 0)
    return pl.pallas_call(
        project_back_kernel,
        grid_spec=pltpu.PrefetchScalarGridSpec(
            num_scalar_prefetch=1,
            grid=(blocks,),
            in_specs=[
                pl.BlockSpec((part, dq.shape[1]), there),
                pl.BlockSpec((part, dk.shape[1]), there),
                pl.BlockSpec((part, dv.shape[1]), there),
                pl.BlockSpec((part, pre.shape[1]), there),
                pl.BlockSpec((width, cols), whole),
                pl.BlockSpec((1, HEAD_DIM), whole),
                pl.BlockSpec((1, HEAD_DIM), whole),
                pl.BlockSpec((part, HEAD_DIM), there),
                pl.BlockSpec((part, HEAD_DIM), there),
            ],
            out_specs=[
                pl.BlockSpec((part, cols), here),
                pl.BlockSpec((part, width), here),
                pl.BlockSpec((8, HEAD_DIM), whole),
            ],
        ),
        out_shape=[
            jax.ShapeDtypeStruct((rows, cols), BF),
            jax.ShapeDtypeStruct((rows, width), BF),
            jax.ShapeDtypeStruct((8, HEAD_DIM), F32),
        ],
        compiler_params=params("arbitrary"),
        cost_estimate=cost(2 * rows * width * cols, 10 * rows * cols + 2 * rows * width + 2 * w.size),
        name="project_back",
    )(perm, dq, dk, dv, pre, w, gain_q, gain_k, cos, sin)


def grad_first_kernel(size, *refs):
    lefts, rights, out = refs[:size], refs[size : 2 * size], refs[-1]
    value = dot_tn(lefts[0][...], rights[0][...])
    for r in range(1, size):
        value += dot_tn(lefts[r][...], rights[r][...])
    copies, units, strip, edge = out.shape
    for unit in range(units):
        rows = slice(unit * copies * strip, (unit + 1) * copies * strip)
        out[:, unit] = value[rows, :].astype(BF).reshape(copies, strip, edge)


def grad_down_bucket(hids, dfs, copies, units, size=None):
    count = len(hids)
    size = size or count
    rows, width = hids[0].shape
    edge = D // size
    strip = edge // copies
    return pl.pallas_call(
        functools.partial(grad_first_kernel, count),
        grid=(size,),
        in_specs=[pl.BlockSpec((rows, width), lambda i: (0, 0))] * count
        + [pl.BlockSpec((rows, edge), lambda i: (0, i))] * count,
        out_specs=pl.BlockSpec((copies, width // copies // strip, strip, edge), lambda i: (0, i, 0, 0)),
        out_shape=jax.ShapeDtypeStruct((copies, units, strip, edge), BF),
        compiler_params=params("arbitrary", limit=32),
        cost_estimate=cost(2 * size * rows * width * D, 2 * size * rows * (width + D) + 2 * width * D),
        name="grad_down",
    )(*hids, *dfs)


def grad_in_kernel(size, *refs):
    lefts, rights, out = refs[:size], refs[size : 2 * size], refs[-1]
    value = dot_tn(lefts[0][...], rights[0][...])
    for r in range(1, size):
        value += dot_tn(lefts[r][...], rights[r][...])
    copies, units, strip, edge = out.shape
    for unit in range(units):
        cols = slice(unit * edge, (unit + 1) * edge)
        out[:, unit] = value[:, cols].astype(BF).reshape(copies, strip, edge)


def grad_columns(lefts, rights, bucket, start, stride, size=None):
    count = len(lefts)
    size = size or count
    copies, _, strip, edge = bucket.shape
    width = rights[0].shape[1]
    rows = rights[0].shape[0]
    if all(right is rights[0] for right in rights):
        rows = rows // count
    units = width // edge
    row_blocks = range(count) if rights[0].shape[0] == count * rows else [0] * count
    return pl.pallas_call(
        functools.partial(grad_in_kernel, count),
        grid=(size,),
        in_specs=[pl.BlockSpec((rows, edge), lambda s: (0, s))] * count
        + [pl.BlockSpec((rows, width), lambda s, b=b: (b, 0)) for b in row_blocks]
        + [pl.BlockSpec(memory_space=pl.ANY)],
        out_specs=pl.BlockSpec(
            (copies, units, strip, edge), lambda s: (0, start // units + stride // units * s, 0, 0)
        ),
        out_shape=jax.ShapeDtypeStruct(bucket.shape, BF),
        input_output_aliases={2 * count: 0},
        compiler_params=params("arbitrary", limit=32),
        cost_estimate=cost(
            2 * size * rows * width * D, 2 * size * rows * (width + D) + 2 * width * D
        ),
        name="grad_columns",
    )(*lefts, *rights, bucket)


def state_kernel(talls, spots, *refs):
    count = len(talls)
    pieces, moments = refs[:count], refs[count : 2 * count]
    grads, news = refs[2 * count : 3 * count], refs[3 * count : 4 * count]
    for at in range(count):
        copies, units, strip, edge = pieces[at].shape
        for unit in range(units):
            span = slice(unit * edge, (unit + 1) * edge)
            span = (span, slice(None)) if talls[at] else (slice(None), span)
            grad = pieces[at][:, unit].reshape(copies * strip, edge).astype(F32)
            grads[at][span] = grad
            news[at][span] = MOMENTUM * moments[at][span] + grad


def state_spec(state, tall, size):
    rows, cols = state.shape
    if tall:
        return pl.BlockSpec((rows, D // size), lambda j, spots: (0, j))
    return pl.BlockSpec((rows, cols // size), lambda j, spots: (0, j))


def look_specs(whole, pieces, moments, talls, size):
    copies, _, strip, edge = whole.shape
    return [
        pl.BlockSpec((copies, units, strip, edge), functools.partial(where, size))
        for units, where in pieces
    ], [state_spec(m, tall, size) for m, tall in zip(moments, talls)]


FIRST = (3, 3, 6, {0: 0, 1: 1, 2: 2}, {0: 3, 1: 3, 2: 3})
SECOND = (2, 2, 4, {0: 1, 1: 2, 2: 3, 3: 0}, {0: 1, 1: 1, 2: 2, 3: 2})


def bucket_unit(plan, chip, size, y, unit):
    units, tall_units, row_units, _, counts = plan
    if chip == 2:
        return units * y + unit
    first = {(3, 0): 0, (3, 1): 3, (2, 0): 2, (2, 1): 3, (2, 3): 0}[(units, chip)]
    return tall_units * size + row_units * y + first + min(unit, counts[chip] - 1)


def deal_moments_kernel(plan, spots, *refs):
    units, _, _, places, counts = plan
    size = spots.shape[0] - 3
    refs, outs = refs[:-size], refs[-size:]
    edge = outs[0].shape[3]
    for r in range(size):
        for chip, place in places.items():

            @pl.when(spots[r] == chip)
            def _():
                for y in range(size):
                    for unit in range(units):
                        if chip == 2:
                            ref, at = refs[len(refs) - units + unit], y
                        else:
                            ref, at = refs[place], counts[chip] * y + min(unit, counts[chip] - 1)
                        outs[r][y, unit] = ref[:, at * edge : (at + 1) * edge]


def deal_moments(plan, wides, tall, spots, size, copies):
    units = plan[0]
    edge = D // size
    strip = edge // copies
    return pl.pallas_call(
        functools.partial(deal_moments_kernel, plan),
        grid_spec=pltpu.PrefetchScalarGridSpec(
            num_scalar_prefetch=1,
            grid=(1,),
            in_specs=[
                pl.BlockSpec((strip, m.shape[1]), lambda i, spots: (spots[size + 2], 0)) for m in wides
            ]
            + [
                pl.BlockSpec((strip, D), lambda i, spots, k=k: (k * copies + spots[size + 2], 0))
                for k in range(units)
            ],
            out_specs=[pl.BlockSpec((size, units, strip, edge), lambda i, spots: (0, 0, 0, 0))] * size,
        ),
        out_shape=[jax.ShapeDtypeStruct((size, units, strip, edge), F32)] * size,
        compiler_params=params("arbitrary", limit=16),
        cost_estimate=cost(0, 1),
        name="deal_moments",
    )(spots, *wides, *[tall] * units)


def deal_grads_kernel(plan, spots, summed, *outs):
    units, tall_units, row_units, places, _ = plan
    size = len(outs)
    start = tall_units * size
    for r in range(size):
        for chip in places:

            @pl.when(spots[r] == chip)
            def _():
                for y in range(size):
                    for unit in range(units):
                        outs[r][units * y + unit] = summed[bucket_unit(plan, chip, size, y, unit)]

        for unit in range(row_units):
            outs[r][units * size + unit] = summed[start + row_units * spots[r] + unit]
        for unit in range(summed.shape[0] - start - row_units * size):
            outs[r][units * size + row_units + unit] = summed[start + row_units * size + unit]


def deal_grads(plan, summed, spots, size):
    count, strip, edge = summed.shape
    units, tall_units, row_units = plan[:3]
    shape = (units * size + row_units + count - (tall_units + row_units) * size, strip, edge)
    return pl.pallas_call(
        functools.partial(deal_grads_kernel, plan),
        grid_spec=pltpu.PrefetchScalarGridSpec(
            num_scalar_prefetch=1,
            grid=(1,),
            in_specs=[pl.BlockSpec(summed.shape, lambda i, spots: (0, 0, 0))],
            out_specs=[pl.BlockSpec(shape, lambda i, spots: (0, 0, 0))] * size,
        ),
        out_shape=[jax.ShapeDtypeStruct(shape, BF)] * size,
        compiler_params=params("arbitrary", limit=16),
        cost_estimate=cost(0, 1),
        name="deal_grads",
    )(spots, summed)


def look_piece_kernel(plan, spots, *refs):
    units, tall_units, row_units = plan[:3]
    size = (len(refs) - 3) // 2
    grads, moments, (summed, out, rows_out) = refs[:size], refs[size:-3], refs[-3:]
    begin, end = tall_units * size, (tall_units + row_units) * size
    rows_out[:begin] = summed[:begin]
    for r in range(size):
        start = begin + row_units * r
        rows_out[start : start + row_units] = grads[r][units * size : units * size + row_units]
    if summed.shape[0] > end:
        rows_out[end:] = sum(g[units * size + row_units :].astype(F32) for g in grads).astype(BF)

    def put(row, sub, unit, grad, old):
        grad = grad.astype(F32)
        value = grad + MOMENTUM * (MOMENTUM * old + grad)
        out[(row * size + sub) * units + unit] = value.astype(BF)

    for r in range(size):
        for other in range(size):
            for unit in range(units):

                @pl.when(spots[0] == 2)
                def _():
                    put(spots[r], other, unit, grads[r][units * other + unit], moments[r][other, unit])

                @pl.when(spots[0] != 2)
                def _():
                    row, sub = spots[other], spots[r]
                    put(row, sub, unit, grads[r][units * row + unit], moments[other][sub, unit])


def look_piece(plan, grads, moments, summed, spots):
    size, units, strip, edge = moments[0].shape
    whole = lambda i, spots: (0, 0, 0)
    return pl.pallas_call(
        functools.partial(look_piece_kernel, plan),
        grid_spec=pltpu.PrefetchScalarGridSpec(
            num_scalar_prefetch=1,
            grid=(1,),
            in_specs=[pl.BlockSpec(grads[0].shape, whole)] * size
            + [pl.BlockSpec(moments[0].shape, lambda i, spots: (0, 0, 0, 0))] * size
            + [pl.BlockSpec(summed.shape, whole)],
            out_specs=[
                pl.BlockSpec((units * size * size, strip, edge), whole),
                pl.BlockSpec(summed.shape, whole),
            ],
        ),
        out_shape=[
            jax.ShapeDtypeStruct((units * size * size, strip, edge), BF),
            jax.ShapeDtypeStruct(summed.shape, BF),
        ],
        compiler_params=params("arbitrary", limit=24),
        cost_estimate=cost(0, 1),
        name="look_piece",
    )(spots, *grads, *moments, summed)


def state(whole, pieces, moments, talls, spots, size, name):
    piece_specs, specs = look_specs(whole, pieces, moments, talls, size)
    return pl.pallas_call(
        functools.partial(state_kernel, talls),
        grid_spec=pltpu.PrefetchScalarGridSpec(
            num_scalar_prefetch=1,
            grid=(size,),
            in_specs=piece_specs + specs,
            out_specs=specs + specs,
        ),
        out_shape=[jax.ShapeDtypeStruct(m.shape, F32) for m in moments] * 2,
        compiler_params=params("arbitrary", limit=60),
        cost_estimate=cost(0, whole.size * 2 + 12 * sum(m.size for m in moments)),
        name=name,
    )(spots, *[whole] * len(pieces), *moments)


def ortho_kernel(sizes, info, pieces, *refs):
    *outputs, z, gram, poly = refs
    subs, inner_units, edge, _ = outputs[0].shape
    place, tall, units = info[0], info[1], info[2]

    def block_in(r, unit, sub):
        at = (((r ^ place) * subs) + sub) * inner_units + unit
        return pieces[:, at].reshape(edge, edge)

    def each_block(action):
        for r in range(len(outputs)):
            for unit in range(inner_units):

                @pl.when(unit < units)
                def _():
                    def body(sub, carry):
                        action(r, unit, sub)
                        return carry

                    lax.fori_loop(0, subs, body, 0)

    def target(source, unit, sub):
        at = source ^ place
        row = jnp.where(tall == 1, sub, at)
        col = unit * subs + jnp.where(tall == 1, at, sub)
        return (
            pl.ds(pl.multiple_of(row * edge, edge), edge),
            pl.ds(pl.multiple_of(col * edge, edge), edge),
        )

    def run(total_ref):
        total_ref[...] = jnp.zeros_like(total_ref)

        def add_square(r, unit, sub):
            block = block_in(r, unit, sub).astype(F32)
            total_ref[...] += jnp.sum((block * block).reshape(edge // 8, 8, edge), axis=0)

        each_block(add_square)
        total = jnp.sum(total_ref[...], keepdims=True)
        total_ref[...] = jnp.broadcast_to(1.0 / (jnp.sqrt(total) + 1e-07), total_ref.shape)

        def put(r, unit, sub):
            block = block_in(r, unit, sub).astype(F32) * total_ref[0:1, :]
            rows, cols = target(r, unit, sub)

            @pl.when(tall == 1)
            def _():
                z[rows, cols] = block.T.astype(BF)

            @pl.when(tall == 0)
            def _():
                z[rows, cols] = block.astype(BF)

        each_block(put)

    tile = 256

    def turns(count):
        width = count * D

        def turn(step, carry):
            for j in range(D // tile):
                at, below = slice(j * tile, (j + 1) * tile), slice((j + 1) * tile, D)
                block = dot_nt(z[j * tile :, :width], z[at, :width]).astype(BF)
                gram[j * tile :, at] = block
                if j < D // tile - 1:
                    gram[at, below] = block[tile:].T
            for j in range(D // tile):
                at, below = slice(j * tile, (j + 1) * tile), slice((j + 1) * tile, D)
                square = dot(gram[j * tile :, :], gram[:, at])
                block = COEF_SQUARE * gram[j * tile :, at].astype(F32) + COEF_CUBE * square
                block = block.astype(BF)
                poly[j * tile :, at] = block
                if j < D // tile - 1:
                    poly[at, below] = block[tile:].T
            wide = min(width, 1024)

            def update(p, c):
                cols = pl.ds(pl.multiple_of(p * wide, wide), wide)
                now = z[:, cols]
                z[:, cols] = (COEF_LINEAR * now.astype(F32) + dot(poly[...], now)).astype(BF)
                return c

            lax.fori_loop(0, width // wide, update, 0)
            return carry

        lax.fori_loop(0, NS_TURNS, turn, 0)

    @pl.when(units > 0)
    def _():
        pl.run_scoped(run, pltpu.VMEM((8, edge), F32))

    for count in sizes:
        pl.when(units == count)(functools.partial(turns, count))

    def take(r, unit, sub):
        rows, cols = target(r, unit, sub)
        outputs[r][sub, unit] = z[rows, cols]

    each_block(take)


def ortho(info, pieces, sizes):
    spec = pl.BlockSpec(memory_space=pltpu.VMEM)
    copies, count, strip, edge = pieces.shape
    size = D // edge
    outs = [jax.ShapeDtypeStruct((size, count // size // size, edge, edge), BF)] * size
    return pl.pallas_call(
        functools.partial(ortho_kernel, sizes),
        in_specs=[pl.BlockSpec(memory_space=pltpu.SMEM), spec],
        out_specs=[spec] * size,
        out_shape=outs,
        scratch_shapes=[
            pltpu.VMEM((D, max(sizes) * D), BF),
            pltpu.VMEM((D, D), BF),
            pltpu.VMEM((D, D), BF),
        ],
        compiler_params=params(limit=56),
        cost_estimate=cost(1, 1),
        name="ortho",
    )(info, pieces)


def update_kernel(table, spots, *refs):
    count = len(table)
    size = spots.shape[0] - 3
    near, far = refs[:size], refs[size : 2 * size]
    masters, outs = refs[2 * size : 2 * size + count], refs[2 * size + count :]
    for r in range(size):
        for chip, (at, tall, units) in enumerate(table):
            for piece, used in ((near[r], 1), (far[r], 0)):

                @pl.when((spots[r] == chip) & (spots[size + 1] == used))
                def _():
                    edge = piece.shape[2]
                    scale = MUON_RATE * (1.0 if tall else float(units) ** 0.5)
                    for unit in range(units):
                        span = slice(unit * edge, (unit + 1) * edge)
                        span = (span, slice(None)) if tall else (slice(None), span)
                        block = piece[0, unit]
                        block = block.T if tall else block
                        outs[at][span] = masters[at][span] * (
                            1.0 - MUON_RATE * MUON_DECAY
                        ) - scale * block.astype(F32)


def update(near, far, table, masters, talls, spots, name):
    size = near[0].shape[0]
    specs = [state_spec(m, tall, size) for m, tall in zip(masters, talls)]

    def block_spec(value, used):
        shape = (1,) + value.shape[1:]
        return pl.BlockSpec(shape, lambda j, spots: (j * (spots[size + 1] == used), 0, 0, 0))

    return pl.pallas_call(
        functools.partial(update_kernel, table),
        grid_spec=pltpu.PrefetchScalarGridSpec(
            num_scalar_prefetch=1,
            grid=(size,),
            in_specs=[block_spec(v, 1) for v in near] + [block_spec(v, 0) for v in far] + specs,
            out_specs=specs,
        ),
        out_shape=[jax.ShapeDtypeStruct(m.shape, F32) for m in masters],
        compiler_params=params("arbitrary", limit=48),
        cost_estimate=cost(0, 10 * sum(m.size for m in masters)),
        name=name,
    )(spots, *near, *far, *masters)


def norm_parts(values):
    return lax.rsqrt(jnp.mean(values * values, axis=-1, keepdims=True) + EPS_NORM)


def norm_back(values, gain, inverse, grad):
    scaled = gain * grad
    inner = jnp.mean(values * scaled, axis=-1, keepdims=True)
    return (
        inverse * scaled - values * (inverse * inverse * inverse * inner),
        jnp.sum(grad * values * inverse, axis=0),
    )


def on_device(
    tokens,
    cotangent,
    segments,
    master_query,
    master_key,
    master_value,
    master_out,
    master_gate,
    master_up,
    master_down,
    moment_query,
    moment_key,
    moment_value,
    moment_out,
    moment_gate,
    moment_up,
    moment_down,
    gains,
    gain_first,
    gain_second,
):
    size = lax.axis_size("shard")
    copies = lax.axis_size("dp")
    place = lax.axis_index("shard")
    core = lax.axis_index("dp") % 2
    part = tokens.shape[0]
    seq_len = part * size
    edge = D // size
    heads_q = HEADS // size
    heads_k = KV_HEADS // size
    perm = place ^ jnp.arange(size, dtype=jnp.int32)
    spots = jnp.concatenate([perm, jnp.stack([core, core, lax.axis_index("dp")]).astype(jnp.int32)])

    half = edge // 2
    qkv_cols = (heads_q + 2 * heads_k) * HEAD_DIM
    tail = jnp.pad(segments.astype(BF).reshape(1, part), ((0, 15), (0, qkv_cols - part)))
    x_sent, tokens = lax.optimization_barrier((tokens, tokens))
    x_blocks = exchange([x_sent] * size, size)
    packed = pack(
        [[master_query, master_key, master_value], [master_gate, master_up]], tail, spots, size
    )
    positions = jnp.arange(seq_len, dtype=jnp.int32)
    inverse_freq = ROPE_BASE ** (-(jnp.arange(HEAD_DIM // 2, dtype=F32) * 2.0 / HEAD_DIM))
    angles = positions.astype(F32)[:, None] * inverse_freq[None, :]
    cos_half, sin_half = jnp.cos(angles), jnp.sin(angles)
    cos = jnp.concatenate([cos_half, cos_half], axis=-1)
    sin = jnp.concatenate([-sin_half, sin_half], axis=-1)
    packed, cos, sin = lax.optimization_barrier((packed, cos, sin))
    messages = exchange(packed[:size], size)
    qkv_others = [xor_permute(m, "dp", copies, 1) for m in messages]
    x_blocks, messages, in_packed = lax.optimization_barrier((x_blocks, messages, packed[size:]))
    in_pieces = exchange(in_packed, size)
    w_down = master_down.astype(BF)

    gain_q = gains[:HEAD_DIM].reshape(1, HEAD_DIM)
    gain_k = gains[HEAD_DIM : 2 * HEAD_DIM].reshape(1, HEAD_DIM)
    gain_a = gains[2 * HEAD_DIM : 2 * HEAD_DIM + D]
    gain_f = gains[2 * HEAD_DIM + D :]

    x_blocks, messages, in_packed = lax.optimization_barrier((x_blocks, messages, in_packed))
    in_pieces = exchange(in_packed, size)
    def scatter(bucket):
        units = bucket.shape[1]
        flat = bucket.reshape(copies * units, *bucket.shape[2:])
        return lax.psum_scatter(flat, "dp", scatter_dimension=0, tiled=True)

    q_low, k_low, v_low, pre, w_qkv = project(
        x_blocks, messages, qkv_others, part, gain_q, gain_k, cos, sin, spots, heads_q, heads_k
    )
    q_low, in_pieces = lax.optimization_barrier((q_low, in_pieces))
    in_pieces = in_pieces + [xor_permute(piece, "dp", copies, 1) for piece in in_pieces]
    w_in = assemble(in_pieces, spots)
    o_low, first = attend(q_low, k_low, v_low, messages, spots)
    a_part = project_out(o_low, master_out, perm)

    def own_sum(partial):
        pieces = exchange([partial[r * part : (r + 1) * part] for r in range(size)], size)
        return sum(piece.astype(F32) for piece in pieces)

    a = own_sum(a_part)
    a_inverse = norm_parts(a)
    h = tokens.astype(F32) + a * a_inverse * gain_a
    h_blocks = gather_blocks(h.astype(BF), size)
    gates, ups, hids, f_parts = zip(*[feed(block, w_in, w_down) for block in h_blocks])
    f = sum(piece.astype(F32) for piece in exchange(list(f_parts), size))
    f_inverse = norm_parts(f)
    out_tokens = (h + f * f_inverse * gain_f).astype(BF)

    dy = cotangent.astype(F32)
    df, dgain_f = norm_back(f, gain_f, f_inverse, dy)
    df_blocks = gather_blocks(df.astype(BF), size)
    strip = edge // copies
    first_bucket = grad_down_bucket(hids, joined(df_blocks), copies, 9 * size)
    dgates, dups, dh_parts = zip(
        *[
            feed_back(df_blocks[r], gates[r], ups[r], w_in, w_down)
            for r in range(size)
        ]
    )
    h_blocks = joined(h_blocks)
    first_bucket = grad_columns(h_blocks, dgates, first_bucket, 3 * size, 6)
    first_bucket = grad_columns(h_blocks, dups, first_bucket, 3 * size + 3, 6)
    dh_pieces = exchange(list(dh_parts), size)
    dh_pieces, first_bucket = lax.optimization_barrier((dh_pieces, first_bucket))
    dh = dy + sum(piece.astype(F32) for piece in dh_pieces)
    first_sum = scatter(first_bucket)
    da, dgain_a = norm_back(a, gain_a, a_inverse, dh)
    da_blocks = gather_blocks(da.astype(BF), size)
    do_low, da_abs = project_out_back(da_blocks, master_out, perm)
    old_spots, do_low = lax.optimization_barrier((spots, do_low))
    first_old = exchange(
        deal_moments(FIRST, [moment_gate, moment_up], moment_down, old_spots, size, copies), size
    )
    dq, dk, dv = attend_back(q_low, k_low, v_low, do_low, first)
    dqkv, dx_part, dgain_qk = project_back(
        dq, dk, dv, pre, w_qkv, gain_q, gain_k, cos, sin, perm
    )
    first_sum, dqkv = lax.optimization_barrier((first_sum, dqkv))
    first_dealt = exchange(deal_grads(FIRST, first_sum, spots, size), size)
    first_piece, first_rows = look_piece(FIRST, first_dealt, first_old, first_sum, spots)
    first_in = lax.all_gather(first_piece, "dp", axis=0)
    old_spots, first_piece = lax.optimization_barrier((spots, first_piece))
    second_old = exchange(
        deal_moments(
            SECOND,
            [moment_query, moment_key, moment_value],
            moment_out,
            old_spots,
            size,
            copies,
        ),
        size,
    )
    gain_terms = jnp.concatenate([dgain_qk[0], dgain_qk[1], dgain_a, dgain_f])
    gain_count = gain_terms.shape[0] // copies
    gain_unit = jnp.pad(
        gain_terms.astype(BF).reshape(copies, gain_count), ((0, 0), (0, strip * edge - gain_count))
    ).reshape(copies, 1, strip, edge)
    second_bucket = grad_down_bucket([o_low], [da_abs], copies, 6 * size + 1, size)
    second_bucket = lax.dynamic_update_slice(second_bucket, gain_unit, (0, 6 * size, 0, 0))
    dqkv, _ = lax.optimization_barrier((dqkv, first_piece))
    second_bucket = grad_columns(x_blocks, [dqkv] * size, second_bucket, 2 * size, 4)
    second_sum = scatter(second_bucket)
    dx = own_sum(dx_part)

    first_in, dx = lax.optimization_barrier((first_in, dx))
    first_pieces = [
        (3, lambda size, j, spots: (0, size + 2 * spots[j], 0, 0)),
        (3, lambda size, j, spots: (0, size + 2 * spots[j] + 1, 0, 0)),
        (3, lambda size, j, spots: (0, j, 0, 0)),
    ]
    first_moments, first_talls = [moment_gate, moment_up, moment_down], (False, False, True)
    grad_tokens = dh + dx
    three, four = (0, 1, 2), (0, 1, 2, 3)
    second_dealt = exchange(deal_grads(SECOND, second_sum, spots, size), size)
    second_piece, second_rows = look_piece(SECOND, second_dealt, second_old, second_sum, spots)
    second_in = lax.all_gather(second_piece, "dp", axis=0)
    first_rows, second_rows, second_piece = lax.optimization_barrier(
        (first_rows, second_rows, second_piece)
    )
    first_whole = lax.all_gather(first_rows, "dp", axis=0)
    second_whole = lax.all_gather(second_rows, "dp", axis=0)

    groups = tuple((r, 0) for r in range(size))
    is_two = (place == 2).astype(jnp.int32)
    first_units = jnp.where((core == 0) & (place < 3), 3, 0)
    second_units = jnp.where((core == 1) & (place < 4), jnp.where(place < 2, 1, 2), 0)
    first_info = jnp.stack([place, is_two, first_units]).astype(jnp.int32)
    second_info = jnp.stack([place, is_two, second_units]).astype(jnp.int32)
    first_in, _ = lax.optimization_barrier((first_in, second_rows))
    first_made = ortho(first_info, first_in, (3,))
    first_near = [first_made[0]] + [
        send_one_core(first_made[r], copies, size, r, 0, sources=three) for r in range(1, size)
    ]
    second_in, first_near[1] = lax.optimization_barrier((second_in, first_near[1]))
    second_made = ortho(second_info, second_in, (1, 2))
    second_pieces = [
        (2, lambda size, j, spots: (0, size + 2 * spots[j], 0, 0)),
        (1, lambda size, j, spots: (0, 2 * size + 4 * spots[j] + 2, 0, 0)),
        (1, lambda size, j, spots: (0, 2 * size + 4 * spots[j] + 3, 0, 0)),
        (2, lambda size, j, spots: (0, j, 0, 0)),
    ]
    second_moments = [moment_query, moment_key, moment_value, moment_out]
    second_talls = (False, False, False, True)

    second_near = [second_made[0]] + [
        send_one_core(second_made[r], copies, size, r, 1, sources=four) for r in range(1, size)
    ]
    state_spots, _ = lax.optimization_barrier((spots, second_made))
    first_state = state(
        first_whole, first_pieces, first_moments, first_talls, state_spots, size, "state_first"
    )
    g_gate, g_up, g_down, n_gate, n_up, n_down = first_state
    first_near, g_gate, second_near[1], second_near[2] = lax.optimization_barrier(
        (first_near, g_gate, second_near[1], second_near[2])
    )
    first_far = [to_other_core(value, copies, 0) for value in first_near]
    first_spots = spots.at[size + 1].set((1 - core).astype(jnp.int32))
    u_gate, u_up, u_down = update(
        first_near,
        first_far,
        ((0, False, 3), (1, False, 3), (2, True, 3)),
        [master_gate, master_up, master_down],
        (False, False, True),
        first_spots,
        "update_first",
    )
    state_spots, u_gate = lax.optimization_barrier((spots, u_gate))
    g_query, g_key, g_value, g_out, n_query, n_key, n_value, n_out = state(
        second_whole, second_pieces, second_moments, second_talls, state_spots, size, "state_second"
    )
    second_near, g_query = lax.optimization_barrier((second_near, g_query))
    second_far = [to_other_core(value, copies, 1) for value in second_near]
    second_spots = spots.at[size + 1].set(core.astype(jnp.int32))
    u_key, u_value, u_out, u_query = update(
        second_near,
        second_far,
        ((0, False, 1), (1, False, 1), (2, True, 2), (3, False, 2)),
        [master_key, master_value, master_out, master_query],
        (False, False, True, False),
        second_spots,
        "update_second",
    )
    grads = (g_query, g_key, g_value, g_out, g_gate, g_up, g_down)
    new_moments = (n_query, n_key, n_value, n_out, n_gate, n_up, n_down)
    new_masters = (u_query, u_key, u_value, u_out, u_gate, u_up, u_down)

    gain_part = gain_first.shape[0]
    gain_sums = second_whole[:, 6 * size].reshape(copies, strip * edge)[:, :gain_count]
    gain_grad = lax.dynamic_slice_in_dim(gain_sums.reshape(-1), place * gain_part, gain_part)
    gain_grad = gain_grad.astype(F32)
    own_gains = lax.dynamic_slice_in_dim(gains, place * gain_part, gain_part)
    first_new = BETA_FIRST * gain_first + (1.0 - BETA_FIRST) * gain_grad
    second_new = BETA_SECOND * gain_second + (1.0 - BETA_SECOND) * gain_grad * gain_grad
    gains_new = own_gains - GAIN_RATE * (first_new / (1.0 - BETA_FIRST**STEP)) / (
        jnp.sqrt(second_new / (1.0 - BETA_SECOND**STEP)) + ADAM_EPS
    )
    return (out_tokens, grad_tokens, *grads, *new_moments, *new_masters, gain_grad, second_new, gains_new)


def solution(mesh):
    rows = P(("dp", "shard"), None)
    state = P("shard", None)
    return jax.shard_map(
        on_device,
        mesh=mesh,
        in_specs=(rows, rows, P(("dp", "shard")), *[state] * 14, P(), P("shard"), P("shard")),
        out_specs=(rows, rows, *[state] * 21, P("shard"), P("shard"), P("shard")),
        check_vma=False,
    )
```

```python
import functools

import jax
import jax.numpy as jnp
import numpy as np
from jax import lax
from jax.experimental import pallas as pl
from jax.experimental.pallas import tpu as pltpu
from jax.sharding import PartitionSpec as P

D = 1024
HEADS = 16
KV_HEADS = 8
HEAD_DIM = 128
FF = 3072
NS_TURNS = 5
STEP = 10
DOCUMENTS = 4
GROUP = 2

EPS_NORM = 1e-06
ROPE_BASE = 1000000.0
MOMENTUM = 0.95
MUON_RATE = 0.5
MUON_DECAY = 0.1
BETA_FIRST = 0.9
BETA_SECOND = 0.95
GAIN_RATE = 0.6
ADAM_EPS = 1e-08
COEF_LINEAR = 3.4445
COEF_SQUARE = -4.775
COEF_CUBE = 2.0315
MASKED = -1e30

BF = jnp.bfloat16
F32 = jnp.float32
NT = (((1,), (1,)), ((), ()))
TN = (((0,), (0,)), ((), ()))


def dot(a, b):
    return jnp.dot(a, b, preferred_element_type=F32)


def dot_nt(a, b):
    return lax.dot_general(a, b, NT, preferred_element_type=F32)


def dot_tn(a, b):
    return lax.dot_general(a, b, TN, preferred_element_type=F32)


def params(*semantics, limit=32):
    return pltpu.CompilerParams(
        dimension_semantics=semantics or None, vmem_limit_bytes=limit * 1024 * 1024
    )


def cost(flops, moved, exps=0):
    return pl.CostEstimate(flops=int(flops), bytes_accessed=int(moved), transcendentals=int(exps))


def xor_permute(value, axis, size, mask):
    return lax.ppermute(value, axis, [(i, i ^ mask) for i in range(size)])


def exchange(blocks, size):
    return [blocks[0]] + [xor_permute(blocks[r], "shard", size, r) for r in range(1, size)]


def gather_blocks(value, size):
    if size != 4:
        return [[block] for block in exchange([value] * size, size)]
    half = value.shape[0] // 2
    low, high = value[:half], value[half:]
    low_two = xor_permute(low, "shard", size, 2)
    high_one = xor_permute(high, "shard", size, 1)
    high_two = xor_permute(high, "shard", size, 2)
    low_one = xor_permute(low, "shard", size, 1)
    low_three = xor_permute(low_two, "shard", size, 1)
    high_three = xor_permute(high_one, "shard", size, 2)
    return [[value], [low_one, high_one], [low_two, high_two], [low_three, high_three]]


def joined(blocks):
    return [jnp.concatenate(block, axis=0) if len(block) > 1 else block[0] for block in blocks]


def lay(parts, out):
    start = 0
    for part in parts:
        out[start : start + part.shape[0], :] = part[...]
        start += part.shape[0]


def pick(stacked, place):
    return lax.dynamic_index_in_dim(stacked, place, 0, keepdims=False)


def in_order(blocks, place):
    stacked = jnp.stack(blocks)
    return [pick(stacked, place ^ r) for r in range(len(blocks))]


def to_other_core(value, copies, from_core):
    return lax.ppermute(value, "dp", [(i + from_core, i + 1 - from_core) for i in range(0, copies, 2)])


def send_one_core(value, copies, size, mask, core, sources=None, targets=None):
    pairs = []
    for copy in range(core, copies, 2):
        for i in range(size):
            if sources is not None and i not in sources:
                continue
            if targets is not None and i ^ mask not in targets:
                continue
            pairs.append((copy * size + i, copy * size + (i ^ mask)))
    return lax.ppermute(value, ("dp", "shard"), pairs)


def pack_kernel(counts, spots, tail, *refs):
    weights, outs = refs[: sum(counts)], refs[sum(counts) :]
    size = len(outs) // len(counts)
    half = weights[0].shape[0]
    for group, count in enumerate(counts):
        for r in range(size):
            out = outs[group * size + r]
            start = 0
            for weight in weights[sum(counts[:group]) :][:count]:
                width = weight.shape[1] // size
                cols = pl.ds(pl.multiple_of(spots[r] * width, width), width)
                out[:half, start : start + width] = weight[:, cols].astype(BF)
                start += width
            if group == 0:
                out[half:, :] = jnp.zeros((16, out.shape[1]), BF)
                out[half : half + 1, : tail.shape[1]] = tail[...].astype(F32).astype(BF)


def pack(groups, tail, spots, size):
    half = groups[0][0].shape[0] // 2
    whole = lambda i, spots: (0, 0)
    cols = [sum(w.shape[1] // size for w in group) for group in groups]
    weights = [w for group in groups for w in group]
    shapes = [
        (half + 16 * (at == 0), n) for at, n in enumerate(cols) for _ in range(size)
    ]
    return pl.pallas_call(
        functools.partial(pack_kernel, [len(group) for group in groups]),
        grid_spec=pltpu.PrefetchScalarGridSpec(
            num_scalar_prefetch=1,
            grid=(1,),
            in_specs=[pl.BlockSpec(tail.shape, whole)]
            + [pl.BlockSpec((half, w.shape[1]), lambda i, spots: (spots[size], 0)) for w in weights],
            out_specs=[pl.BlockSpec(shape, whole) for shape in shapes],
        ),
        out_shape=[jax.ShapeDtypeStruct(shape, BF) for shape in shapes],
        compiler_params=params("arbitrary", limit=60),
        cost_estimate=cost(0, 1),
        name="pack",
    )(spots, tail, *weights)


def assemble_into(out, spots, mine, other):
    size = len(mine)
    half = out.shape[0] // (2 * size)
    core = spots[size]
    for r in range(size):
        for pieces, at in ((mine, core), (other, 1 - core)):
            rows = pl.ds(pl.multiple_of((2 * spots[r] + at) * half, half), half)
            out[rows, :] = pieces[r][...]


def assemble_kernel(spots, *refs):
    *pieces, out = refs
    size = len(pieces) // 2
    assemble_into(out, spots, pieces[:size], pieces[size:])


def assemble(pieces, spots):
    size = len(pieces) // 2
    half, cols = pieces[1].shape
    spec = pl.BlockSpec((half, cols), lambda i, spots: (0, 0))
    return pl.pallas_call(
        assemble_kernel,
        grid_spec=pltpu.PrefetchScalarGridSpec(
            num_scalar_prefetch=1,
            grid=(1,),
            in_specs=[spec] * (2 * size),
            out_specs=pl.BlockSpec((2 * size * half, cols), lambda i, spots: (0, 0)),
        ),
        out_shape=jax.ShapeDtypeStruct((2 * size * half, cols), BF),
        compiler_params=params("arbitrary", limit=24),
        cost_estimate=cost(0, 8 * size * half * cols),
        name="assemble",
    )(spots, *pieces)


def project_kernel(spots, gain_q, gain_k, cos, sin, *refs):
    *inputs, q_out, k_out, v_out, pre_out, w = refs
    size = len(inputs) // 3
    x_refs, pieces = inputs[:size], inputs[size:]

    @pl.when(pl.program_id(0) == 0)
    def _():
        assemble_into(w, spots, pieces[:size], pieces[size:])

    for r in range(size):
        pl.when(pl.program_id(0) == r)(
            functools.partial(
                project_block, x_refs[r], gain_q, gain_k, cos, sin, q_out, k_out, v_out, pre_out, w
            )
        )


def project_block(x, gain_q, gain_k, cos, sin, q_out, k_out, v_out, pre_out, w):
    heads_q = q_out.shape[1] // HEAD_DIM
    heads_k = k_out.shape[1] // HEAD_DIM
    cos_now, sin_now = cos[...], sin[...]
    for head in range(heads_q + 2 * heads_k):
        cols = slice(head * HEAD_DIM, (head + 1) * HEAD_DIM)
        if head % 2 == 0:
            wide = slice(head * HEAD_DIM, min(head + 2, heads_q + 2 * heads_k) * HEAD_DIM)
            both = dot(x[...], w[:, wide])
        pre = both[:, (head % 2) * HEAD_DIM : (head % 2 + 1) * HEAD_DIM]
        if head >= heads_q + heads_k:
            at = head - heads_q - heads_k
            v_out[:, at * HEAD_DIM : (at + 1) * HEAD_DIM] = pre.astype(BF)
            continue
        pre_out[:, cols] = pre
        inverse = lax.rsqrt(jnp.mean(pre * pre, axis=-1, keepdims=True) + EPS_NORM)
        normed = pre * inverse * (gain_q[...] if head < heads_q else gain_k[...])
        turned = normed * cos_now + rotate_half(normed) * sin_now
        if head < heads_q:
            q_out[:, cols] = (turned * HEAD_DIM ** (-0.5)).astype(BF)
        else:
            at = head - heads_q
            k_out[:, at * HEAD_DIM : (at + 1) * HEAD_DIM] = turned.astype(BF)


def project(x_blocks, mine, others, part, gain_q, gain_k, cos, sin, spots, heads_q, heads_k):
    size = len(x_blocks)
    rows = part * size
    cols = (heads_q + 2 * heads_k) * HEAD_DIM
    width = x_blocks[0].shape[1]
    half = width // size // 2
    there = lambda r, spots: (spots[r], 0)
    whole = lambda r, spots: (0, 0)
    piece_specs = [pl.BlockSpec((half, cols), whole)] * (2 * size)
    widths = (heads_q * HEAD_DIM, heads_k * HEAD_DIM, heads_k * HEAD_DIM, (heads_q + heads_k) * HEAD_DIM)
    return pl.pallas_call(
        project_kernel,
        grid_spec=pltpu.PrefetchScalarGridSpec(
            num_scalar_prefetch=1,
            grid=(size,),
            in_specs=[
                pl.BlockSpec((1, HEAD_DIM), whole),
                pl.BlockSpec((1, HEAD_DIM), whole),
                pl.BlockSpec((part, HEAD_DIM), there),
                pl.BlockSpec((part, HEAD_DIM), there),
            ]
            + [pl.BlockSpec((part, width), whole)] * size
            + piece_specs,
            out_specs=[pl.BlockSpec((part, n), there) for n in widths]
            + [pl.BlockSpec((width, cols), whole)],
        ),
        out_shape=[
            jax.ShapeDtypeStruct((rows, n), F32 if i == 3 else BF) for i, n in enumerate(widths)
        ]
        + [jax.ShapeDtypeStruct((width, cols), BF)],
        compiler_params=params("arbitrary", limit=32),
        cost_estimate=cost(2 * rows * width * cols, 2 * rows * width + 4 * width * cols + 6 * rows * cols),
        name="project",
    )(spots, gain_q, gain_k, cos, sin, *x_blocks, *mine, *others)


def rotate_half(values):
    return pltpu.roll(values, HEAD_DIM // 2, 1)


def attend_kernel(spots, q, k, v, *refs):
    *tails, o_out, first_out, first_col = refs
    rows = q.shape[0]
    part = min(256, rows)
    size = len(tails)
    block = rows // size

    @pl.when(pl.program_id(0) == 0)
    def _():
        for r in range(size):
            cols = pl.ds(pl.multiple_of(spots[r] * block, block), block)
            first_out[:, cols] = jnp.broadcast_to(tails[r][0:1, :block].astype(F32), (8, block))
        ids = first_out[...]
        found = jnp.zeros_like(ids)
        for document in range(1, DOCUMENTS):
            count = jnp.sum((ids == document - 1).astype(F32), axis=1, keepdims=True)
            found += jnp.where(ids >= document, count, 0.0)
        first_out[...] = found
        first_col[...] = jnp.broadcast_to(found[0:1, :], (128, rows)).T

    for i in range(rows // part):
        at = slice(i * part, (i + 1) * part)
        keys = (i + 1) * part
        scores = dot_nt(q[at, :], k[:keys, :])
        key_pos = lax.broadcasted_iota(jnp.int32, (part, keys), 1)
        row_pos = i * part + lax.broadcasted_iota(jnp.int32, (part, keys), 0)
        first = first_col[at, 0:1].astype(jnp.int32)
        allowed = (key_pos >= first) & (key_pos <= row_pos)
        masked = jnp.where(allowed, scores, MASKED)
        powers = jnp.exp(masked - jnp.max(masked, axis=-1, keepdims=True))
        weights = powers * (1.0 / jnp.sum(powers, axis=-1, keepdims=True))
        o_out[at, :] = dot(weights.astype(BF), v[:keys, :]).astype(BF)


def attend(q, k, v, messages, spots):
    rows, cols = q.shape
    heads = cols // HEAD_DIM
    tail = messages[0].shape[0] // 16 - 1
    return pl.pallas_call(
        attend_kernel,
        grid_spec=pltpu.PrefetchScalarGridSpec(
            num_scalar_prefetch=1,
            grid=(heads,),
            in_specs=[
                pl.BlockSpec((rows, HEAD_DIM), lambda h, spots: (0, h)),
                pl.BlockSpec((rows, HEAD_DIM), lambda h, spots: (0, h // GROUP)),
                pl.BlockSpec((rows, HEAD_DIM), lambda h, spots: (0, h // GROUP)),
            ]
            + [
                pl.BlockSpec((16, m.shape[1]), lambda h, spots: (tail, 0)) for m in messages
            ],
            out_specs=[
                pl.BlockSpec((rows, HEAD_DIM), lambda h, spots: (0, h)),
                pl.BlockSpec((8, rows), lambda h, spots: (0, 0)),
            ],
            scratch_shapes=[pltpu.VMEM((rows, 128), F32)],
        ),
        out_shape=[
            jax.ShapeDtypeStruct((rows, cols), BF),
            jax.ShapeDtypeStruct((8, rows), F32),
        ],
        compiler_params=params("arbitrary"),
        cost_estimate=cost(3 * rows * rows * cols, 6 * rows * cols, heads * rows * rows),
        name="attend",
    )(spots, q, k, v, *messages)


def attend_back_kernel(q, k, v, do, first, dq_out, dk_out, dv_out):
    rows = q.shape[0]
    part = min(256, rows)
    k_turned = k[...].T
    dk_out[...] = jnp.zeros_like(dk_out)
    dv_out[...] = jnp.zeros_like(dv_out)
    for head in range(GROUP):
        cols = slice(head * HEAD_DIM, (head + 1) * HEAD_DIM)
        for i in range(rows // part):
            at = slice(i * part, (i + 1) * part)
            keys = (i + 1) * part
            q_now, do_now = q[at, cols], do[at, cols]
            scores = dot_nt(k[:keys, :], q_now)
            key_pos = lax.broadcasted_iota(jnp.int32, (keys, part), 0)
            row_pos = i * part + lax.broadcasted_iota(jnp.int32, (keys, part), 1)
            allowed = (key_pos >= first[0:1, at].astype(jnp.int32)) & (key_pos <= row_pos)
            masked = jnp.where(allowed, scores, MASKED)
            powers = jnp.exp(masked - jnp.max(masked, axis=0, keepdims=True))
            weights = powers * (1.0 / jnp.sum(powers, axis=0, keepdims=True))
            dv_out[:keys, :] += dot(weights.astype(BF), do_now)
            dweights = dot_nt(v[:keys, :], do_now)
            delta = jnp.sum(weights * dweights, axis=0, keepdims=True)
            dscores = (weights * (dweights - delta)).astype(BF)
            dk_out[:keys, :] += dot(dscores, q_now)
            dq_out[at, cols] = dot(k_turned[:, :keys], dscores).T


def attend_back(q, k, v, do, first):
    rows, cols = q.shape
    groups = k.shape[1] // HEAD_DIM
    wide = pl.BlockSpec((rows, GROUP * HEAD_DIM), lambda g: (0, g))
    thin = pl.BlockSpec((rows, HEAD_DIM), lambda g: (0, g))
    return pl.pallas_call(
        attend_back_kernel,
        grid=(groups,),
        in_specs=[wide, thin, thin, wide, pl.BlockSpec((8, rows), lambda g: (0, 0))],
        out_specs=[wide, thin, thin],
        out_shape=[
            jax.ShapeDtypeStruct((rows, cols), F32),
            jax.ShapeDtypeStruct(k.shape, F32),
            jax.ShapeDtypeStruct(k.shape, F32),
        ],
        compiler_params=params("arbitrary"),
        cost_estimate=cost(7 * rows * rows * cols, 16 * rows * cols, rows * rows * cols // HEAD_DIM),
        name="attend_back",
    )(q, k, v, do, first)


def out_kernel(perm, o, w, a_out):
    a_out[...] = dot(o[...], w[...].astype(BF)).astype(BF)


def project_out(o, w, perm):
    rows, width = o.shape
    blocks = perm.shape[0]
    part = rows // blocks
    return pl.pallas_call(
        out_kernel,
        grid_spec=pltpu.PrefetchScalarGridSpec(
            num_scalar_prefetch=1,
            grid=(blocks,),
            in_specs=[
                pl.BlockSpec((part, width), lambda r, perm: (perm[r], 0)),
                pl.BlockSpec(w.shape, lambda r, perm: (0, 0)),
            ],
            out_specs=pl.BlockSpec((part, w.shape[1]), lambda r, perm: (r, 0)),
        ),
        out_shape=jax.ShapeDtypeStruct((rows, w.shape[1]), BF),
        compiler_params=params("arbitrary"),
        cost_estimate=cost(2 * rows * width * w.shape[1], 2 * rows * (width + D) + 2 * w.size),
        name="project_out",
    )(perm, o, w)


def out_back_kernel(counts, perm, *refs):
    *parts, w, do_out, da_out = refs
    for r in range(len(counts)):

        @pl.when(pl.program_id(0) == r)
        def _():
            start = sum(counts[:r])
            lay(parts[start : start + counts[r]], da_out)

    do_out[...] = dot_nt(da_out[...], w[...].astype(BF)).astype(BF)


def project_out_back(da_blocks, w, perm):
    blocks = perm.shape[0]
    parts = [part for block in da_blocks for part in block]
    width = parts[0].shape[1]
    rows = sum(part.shape[0] for part in parts)
    part = rows // blocks
    return pl.pallas_call(
        functools.partial(out_back_kernel, [len(block) for block in da_blocks]),
        grid_spec=pltpu.PrefetchScalarGridSpec(
            num_scalar_prefetch=1,
            grid=(blocks,),
            in_specs=[pl.BlockSpec(p.shape, lambda r, perm: (0, 0)) for p in parts]
            + [pl.BlockSpec(w.shape, lambda r, perm: (0, 0))],
            out_specs=[
                pl.BlockSpec((part, w.shape[0]), lambda r, perm: (perm[r], 0)),
                pl.BlockSpec((part, width), lambda r, perm: (perm[r], 0)),
            ],
        ),
        out_shape=[
            jax.ShapeDtypeStruct((rows, w.shape[0]), BF),
            jax.ShapeDtypeStruct((rows, width), BF),
        ],
        compiler_params=params("arbitrary"),
        cost_estimate=cost(2 * rows * width * w.shape[0], 4 * rows * width + 2 * w.size),
        name="project_out_back",
    )(perm, *parts, w)


def feed_kernel(*refs):
    *parts, w_gate, w_up, w_down, gate_out, up_out, hid_out, f_out, total, h = refs
    step = pl.program_id(0)

    @pl.when(step == 0)
    def _():
        lay(parts, h)

    gate = dot(h[...], w_gate[...])
    up = dot(h[...], w_up[...])
    gate_out[...] = gate
    up_out[...] = up
    hid = (gate * (1.0 / (1.0 + jnp.exp(-gate))) * up).astype(BF)
    hid_out[...] = hid
    part = dot(hid, w_down[...])

    @pl.when(step == 0)
    def _():
        total[...] = part

    @pl.when(step > 0)
    def _():
        total[...] += part

    @pl.when(step == pl.num_programs(0) - 1)
    def _():
        f_out[...] = total[...].astype(BF)


def feed(parts, w_in, w_down):
    rows = sum(part.shape[0] for part in parts)
    width = w_down.shape[0]
    tile = width // 3
    cols = lambda i: (0, i)
    return pl.pallas_call(
        feed_kernel,
        grid=(3,),
        in_specs=[
            *[pl.BlockSpec(part.shape, lambda i: (0, 0)) for part in parts],
            pl.BlockSpec((D, tile), cols),
            pl.BlockSpec((D, tile), lambda i: (0, i + 3)),
            pl.BlockSpec((tile, D), lambda i: (i, 0)),
        ],
        out_specs=[pl.BlockSpec((rows, tile), cols)] * 3
        + [pl.BlockSpec((rows, D), lambda i: (0, 0))],
        out_shape=[
            jax.ShapeDtypeStruct((rows, width), F32),
            jax.ShapeDtypeStruct((rows, width), F32),
            jax.ShapeDtypeStruct((rows, width), BF),
            jax.ShapeDtypeStruct((rows, D), BF),
        ],
        scratch_shapes=[pltpu.VMEM((rows, D), F32), pltpu.VMEM((rows, D), BF)],
        compiler_params=params("arbitrary", limit=24),
        cost_estimate=cost(1, 1),
        name="feed",
    )(*parts, w_in, w_in, w_down)


def feed_back_kernel(*refs):
    *parts, gate_in, up_in, w_gate, w_up, w_down, dgate_out, dup_out, dh_out, total, df = refs
    step = pl.program_id(0)

    @pl.when(step == 0)
    def _():
        lay(parts, df)

    dhid = dot_nt(df[...], w_down[...]).astype(BF).astype(F32)
    gate, up = gate_in[...], up_in[...]
    sigma = 1.0 / (1.0 + jnp.exp(-gate))
    dgate = (dhid * up * sigma * (1.0 + gate * (1.0 - sigma))).astype(BF)
    dup = (dhid * (gate * sigma)).astype(BF)
    dgate_out[...] = dgate
    dup_out[...] = dup
    part = dot_nt(dgate, w_gate[...]) + dot_nt(dup, w_up[...])

    @pl.when(step == 0)
    def _():
        total[...] = part

    @pl.when(step > 0)
    def _():
        total[...] += part

    @pl.when(step == pl.num_programs(0) - 1)
    def _():
        dh_out[...] = total[...].astype(BF)


def feed_back(parts, gate, up, w_in, w_down):
    rows = sum(part.shape[0] for part in parts)
    width = w_down.shape[0]
    tile = width // 3
    cols = lambda i: (0, i)
    return pl.pallas_call(
        feed_back_kernel,
        grid=(3,),
        in_specs=[
            *[pl.BlockSpec(part.shape, lambda i: (0, 0)) for part in parts],
            pl.BlockSpec((rows, tile), cols),
            pl.BlockSpec((rows, tile), cols),
            pl.BlockSpec((D, tile), cols),
            pl.BlockSpec((D, tile), lambda i: (0, i + 3)),
            pl.BlockSpec((tile, D), lambda i: (i, 0)),
        ],
        out_specs=[pl.BlockSpec((rows, tile), cols)] * 2
        + [pl.BlockSpec((rows, D), lambda i: (0, 0))],
        out_shape=[
            jax.ShapeDtypeStruct((rows, width), BF),
            jax.ShapeDtypeStruct((rows, width), BF),
            jax.ShapeDtypeStruct((rows, D), BF),
        ],
        scratch_shapes=[pltpu.VMEM((rows, D), F32), pltpu.VMEM((rows, D), BF)],
        compiler_params=params("arbitrary", limit=24),
        cost_estimate=cost(1, 1),
        name="feed_back",
    )(*parts, gate, up, w_in, w_in, w_down)


def project_back_kernel(
    perm, dq, dk, dv, pre_in, w, gain_q, gain_k, cos, sin, dqkv_out, dx_out, dgain_out
):
    heads_q = dq.shape[1] // HEAD_DIM
    heads_k = dk.shape[1] // HEAD_DIM

    @pl.when(pl.program_id(0) == 0)
    def _():
        dgain_out[...] = jnp.zeros_like(dgain_out)

    cos_now, sin_now = cos[...], sin[...]
    for head in range(heads_q + heads_k):
        cols = slice(head * HEAD_DIM, (head + 1) * HEAD_DIM)
        if head < heads_q:
            grad = dq[:, cols] * HEAD_DIM ** (-0.5)
            gain = gain_q[...]
        else:
            grad = dk[:, (head - heads_q) * HEAD_DIM : (head - heads_q + 1) * HEAD_DIM]
            gain = gain_k[...]
        turned = grad * cos_now - rotate_half(grad) * sin_now
        pre = pre_in[:, cols]
        inverse = lax.rsqrt(jnp.mean(pre * pre, axis=-1, keepdims=True) + EPS_NORM)
        scaled = gain * turned
        inner = jnp.mean(pre * scaled, axis=-1, keepdims=True)
        dqkv_out[:, cols] = (inverse * scaled - pre * (inverse * inverse * inverse * inner)).astype(BF)
        row = 0 if head < heads_q else 1
        dgain_out[row : row + 1, :] += jnp.sum(turned * pre * inverse, axis=0, keepdims=True)
    dqkv_out[:, (heads_q + heads_k) * HEAD_DIM :] = dv[...].astype(BF)
    dx_out[...] = dot_nt(dqkv_out[...], w[...]).astype(BF)


def project_back(dq, dk, dv, pre, w, gain_q, gain_k, cos, sin, perm):
    rows = dq.shape[0]
    blocks = perm.shape[0]
    part = rows // blocks
    width, cols = w.shape
    there = lambda r, perm: (perm[r], 0)
    here = lambda r, perm: (r, 0)
    whole = lambda r, perm: (0, 0)
    return pl.pallas_call(
        project_back_kernel,
        grid_spec=pltpu.PrefetchScalarGridSpec(
            num_scalar_prefetch=1,
            grid=(blocks,),
            in_specs=[
                pl.BlockSpec((part, dq.shape[1]), there),
                pl.BlockSpec((part, dk.shape[1]), there),
                pl.BlockSpec((part, dv.shape[1]), there),
                pl.BlockSpec((part, pre.shape[1]), there),
                pl.BlockSpec((width, cols), whole),
                pl.BlockSpec((1, HEAD_DIM), whole),
                pl.BlockSpec((1, HEAD_DIM), whole),
                pl.BlockSpec((part, HEAD_DIM), there),
                pl.BlockSpec((part, HEAD_DIM), there),
            ],
            out_specs=[
                pl.BlockSpec((part, cols), here),
                pl.BlockSpec((part, width), here),
                pl.BlockSpec((8, HEAD_DIM), whole),
            ],
        ),
        out_shape=[
            jax.ShapeDtypeStruct((rows, cols), BF),
            jax.ShapeDtypeStruct((rows, width), BF),
            jax.ShapeDtypeStruct((8, HEAD_DIM), F32),
        ],
        compiler_params=params("arbitrary"),
        cost_estimate=cost(2 * rows * width * cols, 10 * rows * cols + 2 * rows * width + 2 * w.size),
        name="project_back",
    )(perm, dq, dk, dv, pre, w, gain_q, gain_k, cos, sin)


def grad_first_kernel(size, *refs):
    lefts, rights, out = refs[:size], refs[size : 2 * size], refs[-1]
    value = dot_tn(lefts[0][...], rights[0][...])
    for r in range(1, size):
        value += dot_tn(lefts[r][...], rights[r][...])
    copies, units, strip, edge = out.shape
    for unit in range(units):
        rows = slice(unit * copies * strip, (unit + 1) * copies * strip)
        out[:, unit] = value[rows, :].astype(BF).reshape(copies, strip, edge)


def grad_down_bucket(hids, dfs, copies, units, size=None):
    count = len(hids)
    size = size or count
    rows, width = hids[0].shape
    edge = D // size
    strip = edge // copies
    return pl.pallas_call(
        functools.partial(grad_first_kernel, count),
        grid=(size,),
        in_specs=[pl.BlockSpec((rows, width), lambda i: (0, 0))] * count
        + [pl.BlockSpec((rows, edge), lambda i: (0, i))] * count,
        out_specs=pl.BlockSpec((copies, width // copies // strip, strip, edge), lambda i: (0, i, 0, 0)),
        out_shape=jax.ShapeDtypeStruct((copies, units, strip, edge), BF),
        compiler_params=params("arbitrary", limit=32),
        cost_estimate=cost(2 * size * rows * width * D, 2 * size * rows * (width + D) + 2 * width * D),
        name="grad_down",
    )(*hids, *dfs)


def grad_in_kernel(size, *refs):
    lefts, rights, out = refs[:size], refs[size : 2 * size], refs[-1]
    value = dot_tn(lefts[0][...], rights[0][...])
    for r in range(1, size):
        value += dot_tn(lefts[r][...], rights[r][...])
    copies, units, strip, edge = out.shape
    for unit in range(units):
        cols = slice(unit * edge, (unit + 1) * edge)
        out[:, unit] = value[:, cols].astype(BF).reshape(copies, strip, edge)


def grad_columns(lefts, rights, bucket, start, stride, size=None):
    count = len(lefts)
    size = size or count
    copies, _, strip, edge = bucket.shape
    width = rights[0].shape[1]
    rows = rights[0].shape[0]
    if all(right is rights[0] for right in rights):
        rows = rows // count
    units = width // edge
    row_blocks = range(count) if rights[0].shape[0] == count * rows else [0] * count
    return pl.pallas_call(
        functools.partial(grad_in_kernel, count),
        grid=(size,),
        in_specs=[pl.BlockSpec((rows, edge), lambda s: (0, s))] * count
        + [pl.BlockSpec((rows, width), lambda s, b=b: (b, 0)) for b in row_blocks]
        + [pl.BlockSpec(memory_space=pl.ANY)],
        out_specs=pl.BlockSpec(
            (copies, units, strip, edge), lambda s: (0, start // units + stride // units * s, 0, 0)
        ),
        out_shape=jax.ShapeDtypeStruct(bucket.shape, BF),
        input_output_aliases={2 * count: 0},
        compiler_params=params("arbitrary", limit=32),
        cost_estimate=cost(
            2 * size * rows * width * D, 2 * size * rows * (width + D) + 2 * width * D
        ),
        name="grad_columns",
    )(*lefts, *rights, bucket)


def state_kernel(talls, spots, *refs):
    count = len(talls)
    pieces, moments = refs[:count], refs[count : 2 * count]
    grads, news = refs[2 * count : 3 * count], refs[3 * count : 4 * count]
    for at in range(count):
        copies, units, strip, edge = pieces[at].shape
        for unit in range(units):
            span = slice(unit * edge, (unit + 1) * edge)
            span = (span, slice(None)) if talls[at] else (slice(None), span)
            grad = pieces[at][:, unit].reshape(copies * strip, edge).astype(F32)
            grads[at][span] = grad
            news[at][span] = MOMENTUM * moments[at][span] + grad


def state_spec(state, tall, size):
    rows, cols = state.shape
    if tall:
        return pl.BlockSpec((rows, D // size), lambda j, spots: (0, j))
    return pl.BlockSpec((rows, cols // size), lambda j, spots: (0, j))


def look_specs(whole, pieces, moments, talls, size):
    copies, _, strip, edge = whole.shape
    return [
        pl.BlockSpec((copies, units, strip, edge), functools.partial(where, size))
        for units, where in pieces
    ], [state_spec(m, tall, size) for m, tall in zip(moments, talls)]


FIRST = (3, 3, 6, {0: 0, 1: 1, 2: 2}, {0: 3, 1: 3, 2: 3})
SECOND = (2, 2, 4, {0: 1, 1: 2, 2: 3, 3: 0}, {0: 1, 1: 1, 2: 2, 3: 2})


def bucket_unit(plan, chip, size, y, unit):
    units, tall_units, row_units, _, counts = plan
    if chip == 2:
        return units * y + unit
    first = {(3, 0): 0, (3, 1): 3, (2, 0): 2, (2, 1): 3, (2, 3): 0}[(units, chip)]
    return tall_units * size + row_units * y + first + min(unit, counts[chip] - 1)


def deal_moments_kernel(plan, spots, *refs):
    units, _, _, places, counts = plan
    size = spots.shape[0] - 3
    refs, outs = refs[:-size], refs[-size:]
    edge = outs[0].shape[3]
    for r in range(size):
        for chip, place in places.items():

            @pl.when(spots[r] == chip)
            def _():
                for y in range(size):
                    for unit in range(units):
                        if chip == 2:
                            ref, at = refs[len(refs) - units + unit], y
                        else:
                            ref, at = refs[place], counts[chip] * y + min(unit, counts[chip] - 1)
                        outs[r][y, unit] = ref[:, at * edge : (at + 1) * edge]


def deal_moments(plan, wides, tall, spots, size, copies):
    units = plan[0]
    edge = D // size
    strip = edge // copies
    return pl.pallas_call(
        functools.partial(deal_moments_kernel, plan),
        grid_spec=pltpu.PrefetchScalarGridSpec(
            num_scalar_prefetch=1,
            grid=(1,),
            in_specs=[
                pl.BlockSpec((strip, m.shape[1]), lambda i, spots: (spots[size + 2], 0)) for m in wides
            ]
            + [
                pl.BlockSpec((strip, D), lambda i, spots, k=k: (k * copies + spots[size + 2], 0))
                for k in range(units)
            ],
            out_specs=[pl.BlockSpec((size, units, strip, edge), lambda i, spots: (0, 0, 0, 0))] * size,
        ),
        out_shape=[jax.ShapeDtypeStruct((size, units, strip, edge), F32)] * size,
        compiler_params=params("arbitrary", limit=16),
        cost_estimate=cost(0, 1),
        name="deal_moments",
    )(spots, *wides, *[tall] * units)


def deal_grads_kernel(plan, spots, summed, *outs):
    units, tall_units, row_units, places, _ = plan
    size = len(outs)
    start = tall_units * size
    for r in range(size):
        for chip in places:

            @pl.when(spots[r] == chip)
            def _():
                for y in range(size):
                    for unit in range(units):
                        outs[r][units * y + unit] = summed[bucket_unit(plan, chip, size, y, unit)]

        for unit in range(row_units):
            outs[r][units * size + unit] = summed[start + row_units * spots[r] + unit]
        for unit in range(summed.shape[0] - start - row_units * size):
            outs[r][units * size + row_units + unit] = summed[start + row_units * size + unit]


def deal_grads(plan, summed, spots, size):
    count, strip, edge = summed.shape
    units, tall_units, row_units = plan[:3]
    shape = (units * size + row_units + count - (tall_units + row_units) * size, strip, edge)
    return pl.pallas_call(
        functools.partial(deal_grads_kernel, plan),
        grid_spec=pltpu.PrefetchScalarGridSpec(
            num_scalar_prefetch=1,
            grid=(1,),
            in_specs=[pl.BlockSpec(summed.shape, lambda i, spots: (0, 0, 0))],
            out_specs=[pl.BlockSpec(shape, lambda i, spots: (0, 0, 0))] * size,
        ),
        out_shape=[jax.ShapeDtypeStruct(shape, BF)] * size,
        compiler_params=params("arbitrary", limit=16),
        cost_estimate=cost(0, 1),
        name="deal_grads",
    )(spots, summed)


def look_piece_kernel(plan, spots, *refs):
    units, tall_units, row_units = plan[:3]
    size = (len(refs) - 3) // 2
    grads, moments, (summed, out, rows_out) = refs[:size], refs[size:-3], refs[-3:]
    begin, end = tall_units * size, (tall_units + row_units) * size
    rows_out[:begin] = summed[:begin]
    for r in range(size):
        start = begin + row_units * r
        rows_out[start : start + row_units] = grads[r][units * size : units * size + row_units]
    if summed.shape[0] > end:
        rows_out[end:] = sum(g[units * size + row_units :].astype(F32) for g in grads).astype(BF)

    def put(row, sub, unit, grad, old):
        grad = grad.astype(F32)
        value = grad + MOMENTUM * (MOMENTUM * old + grad)
        out[(row * size + sub) * units + unit] = value.astype(BF)

    for r in range(size):
        for other in range(size):
            for unit in range(units):

                @pl.when(spots[0] == 2)
                def _():
                    put(spots[r], other, unit, grads[r][units * other + unit], moments[r][other, unit])

                @pl.when(spots[0] != 2)
                def _():
                    row, sub = spots[other], spots[r]
                    put(row, sub, unit, grads[r][units * row + unit], moments[other][sub, unit])


def look_piece(plan, grads, moments, summed, spots):
    size, units, strip, edge = moments[0].shape
    whole = lambda i, spots: (0, 0, 0)
    return pl.pallas_call(
        functools.partial(look_piece_kernel, plan),
        grid_spec=pltpu.PrefetchScalarGridSpec(
            num_scalar_prefetch=1,
            grid=(1,),
            in_specs=[pl.BlockSpec(grads[0].shape, whole)] * size
            + [pl.BlockSpec(moments[0].shape, lambda i, spots: (0, 0, 0, 0))] * size
            + [pl.BlockSpec(summed.shape, whole)],
            out_specs=[
                pl.BlockSpec((units * size * size, strip, edge), whole),
                pl.BlockSpec(summed.shape, whole),
            ],
        ),
        out_shape=[
            jax.ShapeDtypeStruct((units * size * size, strip, edge), BF),
            jax.ShapeDtypeStruct(summed.shape, BF),
        ],
        compiler_params=params("arbitrary", limit=24),
        cost_estimate=cost(0, 1),
        name="look_piece",
    )(spots, *grads, *moments, summed)


def state(whole, pieces, moments, talls, spots, size, name):
    piece_specs, specs = look_specs(whole, pieces, moments, talls, size)
    return pl.pallas_call(
        functools.partial(state_kernel, talls),
        grid_spec=pltpu.PrefetchScalarGridSpec(
            num_scalar_prefetch=1,
            grid=(size,),
            in_specs=piece_specs + specs,
            out_specs=specs + specs,
        ),
        out_shape=[jax.ShapeDtypeStruct(m.shape, F32) for m in moments] * 2,
        compiler_params=params("arbitrary", limit=60),
        cost_estimate=cost(0, whole.size * 2 + 12 * sum(m.size for m in moments)),
        name=name,
    )(spots, *[whole] * len(pieces), *moments)


def ortho_kernel(sizes, info, pieces, *refs):
    *outputs, z, gram, pair, moved = refs
    subs, inner_units, edge, _ = outputs[0].shape
    place, tall, units = info[0], info[1], info[2]

    def block_in(r, unit, sub):
        at = (((r ^ place) * subs) + sub) * inner_units + unit
        return pieces[:, at].reshape(edge, edge)

    def each_block(action):
        for r in range(len(outputs)):
            for unit in range(inner_units):

                @pl.when(unit < units)
                def _():
                    def body(sub, carry):
                        action(r, unit, sub)
                        return carry

                    lax.fori_loop(0, subs, body, 0)

    def target(source, unit, sub):
        at = source ^ place
        row = jnp.where(tall == 1, sub, at)
        col = unit * subs + jnp.where(tall == 1, at, sub)
        return (
            pl.ds(pl.multiple_of(row * edge, edge), edge),
            pl.ds(pl.multiple_of(col * edge, edge), edge),
        )

    def run(total_ref):
        total_ref[...] = jnp.zeros_like(total_ref)

        def add_square(r, unit, sub):
            block = block_in(r, unit, sub).astype(F32)
            total_ref[...] += jnp.sum((block * block).reshape(edge // 8, 8, edge), axis=0)

        each_block(add_square)
        total = jnp.sum(total_ref[...], keepdims=True)
        total_ref[...] = jnp.broadcast_to(1.0 / (jnp.sqrt(total) + 1e-07), total_ref.shape)

        def put(r, unit, sub):
            block = block_in(r, unit, sub).astype(F32) * total_ref[0:1, :]
            rows, cols = target(r, unit, sub)

            @pl.when(tall == 1)
            def _():
                z[rows, cols] = block.T.astype(BF)

            @pl.when(tall == 0)
            def _():
                z[rows, cols] = block.astype(BF)

        each_block(put)

    tile = 256

    def symmetric(out, value_of):
        for j in range(D // tile):
            at, below = slice(j * tile, (j + 1) * tile), slice((j + 1) * tile, D)
            block = value_of(j * tile, at).astype(BF)
            out[j * tile :, at] = block
            if j < D // tile - 1:
                out[at, below] = block[tile:].T

    def form_gram(count):
        width = count * D
        symmetric(gram, lambda low, at: dot_nt(z[low:, :width], z[at, :width]))

    def turns(step, carry):
        double = step < NS_TURNS // 2
        for count in sizes:
            pl.when(units == count)(functools.partial(form_gram, count))

        def one(k, c):
            poly = pair.at[k]
            symmetric(
                poly,
                lambda low, at: COEF_SQUARE * gram[low:, at].astype(F32)
                + COEF_CUBE * dot(gram[low:, :], gram[:, at]),
            )

            @pl.when(double & (k == 0))
            def _():
                symmetric(
                    moved,
                    lambda low, at: COEF_LINEAR * gram[low:, at].astype(F32)
                    + dot(poly[low:, :], gram[:, at]),
                )
                symmetric(
                    gram,
                    lambda low, at: COEF_LINEAR * moved[low:, at].astype(F32)
                    + dot(moved[low:, :], poly[:, at]),
                )

            return c

        lax.fori_loop(0, jnp.where(double, 2, 1), one, 0)

        @pl.when(double)
        def _():
            symmetric(
                moved,
                lambda low, at: COEF_LINEAR
                * (pair[0, low:, at].astype(F32) + pair[1, low:, at].astype(F32))
                + dot(pair[1, low:, :], pair[0, :, at]),
            )

        @pl.when(jnp.logical_not(double))
        def _():
            moved[...] = pair[0]

        factor = jnp.where(double, COEF_LINEAR * COEF_LINEAR, COEF_LINEAR)

        def update_block(p, c):
            cols = pl.ds(pl.multiple_of(p * D, D), D)
            now = z[:, cols]
            z[:, cols] = (factor * now.astype(F32) + dot(moved[...], now)).astype(BF)
            return c

        lax.fori_loop(0, units, update_block, 0)
        return carry

    @pl.when(units > 0)
    def _():
        pl.run_scoped(run, pltpu.VMEM((8, edge), F32))

    @pl.when(units > 0)
    def _():
        lax.fori_loop(0, (NS_TURNS + 1) // 2, turns, 0)

    def take(r, unit, sub):
        rows, cols = target(r, unit, sub)
        outputs[r][sub, unit] = z[rows, cols]

    each_block(take)


def ortho(info, pieces, sizes):
    spec = pl.BlockSpec(memory_space=pltpu.VMEM)
    copies, count, strip, edge = pieces.shape
    size = D // edge
    outs = [jax.ShapeDtypeStruct((size, count // size // size, edge, edge), BF)] * size
    return pl.pallas_call(
        functools.partial(ortho_kernel, sizes),
        in_specs=[pl.BlockSpec(memory_space=pltpu.SMEM), spec],
        out_specs=[spec] * size,
        out_shape=outs,
        scratch_shapes=[
            pltpu.VMEM((D, max(sizes) * D), BF),
            pltpu.VMEM((D, D), BF),
            pltpu.VMEM((2, D, D), BF),
            pltpu.VMEM((D, D), BF),
        ],
        compiler_params=params(limit=56),
        cost_estimate=cost(1, 1),
        name="ortho",
    )(info, pieces)


def update_kernel(table, spots, *refs):
    count = len(table)
    size = spots.shape[0] - 3
    near, far = refs[:size], refs[size : 2 * size]
    masters, outs = refs[2 * size : 2 * size + count], refs[2 * size + count :]
    for r in range(size):
        for chip, (at, tall, units) in enumerate(table):
            for piece, used in ((near[r], 1), (far[r], 0)):

                @pl.when((spots[r] == chip) & (spots[size + 1] == used))
                def _():
                    edge = piece.shape[2]
                    scale = MUON_RATE * (1.0 if tall else float(units) ** 0.5)
                    for unit in range(units):
                        span = slice(unit * edge, (unit + 1) * edge)
                        span = (span, slice(None)) if tall else (slice(None), span)
                        block = piece[0, unit]
                        block = block.T if tall else block
                        outs[at][span] = masters[at][span] * (
                            1.0 - MUON_RATE * MUON_DECAY
                        ) - scale * block.astype(F32)


def update(near, far, table, masters, talls, spots, name):
    size = near[0].shape[0]
    specs = [state_spec(m, tall, size) for m, tall in zip(masters, talls)]

    def block_spec(value, used):
        shape = (1,) + value.shape[1:]
        return pl.BlockSpec(shape, lambda j, spots: (j * (spots[size + 1] == used), 0, 0, 0))

    return pl.pallas_call(
        functools.partial(update_kernel, table),
        grid_spec=pltpu.PrefetchScalarGridSpec(
            num_scalar_prefetch=1,
            grid=(size,),
            in_specs=[block_spec(v, 1) for v in near] + [block_spec(v, 0) for v in far] + specs,
            out_specs=specs,
        ),
        out_shape=[jax.ShapeDtypeStruct(m.shape, F32) for m in masters],
        compiler_params=params("arbitrary", limit=48),
        cost_estimate=cost(0, 10 * sum(m.size for m in masters)),
        name=name,
    )(spots, *near, *far, *masters)


def norm_parts(values):
    return lax.rsqrt(jnp.mean(values * values, axis=-1, keepdims=True) + EPS_NORM)


def norm_back(values, gain, inverse, grad):
    scaled = gain * grad
    inner = jnp.mean(values * scaled, axis=-1, keepdims=True)
    return (
        inverse * scaled - values * (inverse * inverse * inverse * inner),
        jnp.sum(grad * values * inverse, axis=0),
    )


def on_device(
    tokens,
    cotangent,
    segments,
    master_query,
    master_key,
    master_value,
    master_out,
    master_gate,
    master_up,
    master_down,
    moment_query,
    moment_key,
    moment_value,
    moment_out,
    moment_gate,
    moment_up,
    moment_down,
    gains,
    gain_first,
    gain_second,
):
    size = lax.axis_size("shard")
    copies = lax.axis_size("dp")
    place = lax.axis_index("shard")
    core = lax.axis_index("dp") % 2
    part = tokens.shape[0]
    seq_len = part * size
    edge = D // size
    heads_q = HEADS // size
    heads_k = KV_HEADS // size
    perm = place ^ jnp.arange(size, dtype=jnp.int32)
    spots = jnp.concatenate([perm, jnp.stack([core, core, lax.axis_index("dp")]).astype(jnp.int32)])

    half = edge // 2
    qkv_cols = (heads_q + 2 * heads_k) * HEAD_DIM
    x_sent, tokens = lax.optimization_barrier((tokens, tokens))
    x_blocks = exchange([x_sent] * size, size)
    packed = pack(
        [[master_query, master_key, master_value], [master_gate, master_up]],
        segments.reshape(1, part),
        spots,
        size,
    )
    inverse_freq = ROPE_BASE ** (-(np.arange(HEAD_DIM // 2, dtype=np.float32) * 2.0 / HEAD_DIM))
    angles = np.arange(seq_len, dtype=np.float32)[:, None] * inverse_freq.astype(np.float32)[None, :]
    cos_half, sin_half = np.cos(angles), np.sin(angles)
    cos = jnp.asarray(np.concatenate([cos_half, cos_half], axis=-1), F32)
    sin = jnp.asarray(np.concatenate([-sin_half, sin_half], axis=-1), F32)
    messages = exchange(packed[:size], size)
    qkv_others = [xor_permute(m, "dp", copies, 1) for m in messages]
    x_blocks, messages, in_packed = lax.optimization_barrier((x_blocks, messages, packed[size:]))
    in_pieces = exchange(in_packed, size)
    w_down = master_down.astype(BF)

    gain_q = gains[:HEAD_DIM].reshape(1, HEAD_DIM)
    gain_k = gains[HEAD_DIM : 2 * HEAD_DIM].reshape(1, HEAD_DIM)
    gain_a = gains[2 * HEAD_DIM : 2 * HEAD_DIM + D]
    gain_f = gains[2 * HEAD_DIM + D :]

    x_blocks, messages, in_packed = lax.optimization_barrier((x_blocks, messages, in_packed))
    in_pieces = exchange(in_packed, size)
    def scatter(bucket):
        units = bucket.shape[1]
        flat = bucket.reshape(copies * units, *bucket.shape[2:])
        return lax.psum_scatter(flat, "dp", scatter_dimension=0, tiled=True)

    q_low, k_low, v_low, pre, w_qkv = project(
        x_blocks, messages, qkv_others, part, gain_q, gain_k, cos, sin, spots, heads_q, heads_k
    )
    q_low, in_pieces = lax.optimization_barrier((q_low, in_pieces))
    in_pieces = in_pieces + [xor_permute(piece, "dp", copies, 1) for piece in in_pieces]
    w_in = assemble(in_pieces, spots)
    o_low, first = attend(q_low, k_low, v_low, messages, spots)
    a_part = project_out(o_low, master_out, perm)

    def own_sum(partial):
        pieces = exchange([partial[r * part : (r + 1) * part] for r in range(size)], size)
        return sum(piece.astype(F32) for piece in pieces)

    a = own_sum(a_part)
    a_inverse = norm_parts(a)
    h = tokens.astype(F32) + a * a_inverse * gain_a
    h_blocks = gather_blocks(h.astype(BF), size)
    gates, ups, hids, f_parts = zip(*[feed(block, w_in, w_down) for block in h_blocks])
    f = sum(piece.astype(F32) for piece in exchange(list(f_parts), size))
    f_inverse = norm_parts(f)
    out_tokens = (h + f * f_inverse * gain_f).astype(BF)

    dy = cotangent.astype(F32)
    df, dgain_f = norm_back(f, gain_f, f_inverse, dy)
    df_blocks = gather_blocks(df.astype(BF), size)
    strip = edge // copies
    first_bucket = grad_down_bucket(hids, joined(df_blocks), copies, 9 * size)
    dgates, dups, dh_parts = zip(
        *[
            feed_back(df_blocks[r], gates[r], ups[r], w_in, w_down)
            for r in range(size)
        ]
    )
    h_blocks = joined(h_blocks)
    first_bucket = grad_columns(h_blocks, dgates, first_bucket, 3 * size, 6)
    first_bucket = grad_columns(h_blocks, dups, first_bucket, 3 * size + 3, 6)
    dh_pieces = exchange(list(dh_parts), size)
    dh_pieces, first_bucket = lax.optimization_barrier((dh_pieces, first_bucket))
    dh = dy + sum(piece.astype(F32) for piece in dh_pieces)
    first_sum = scatter(first_bucket)
    da, dgain_a = norm_back(a, gain_a, a_inverse, dh)
    da_blocks = gather_blocks(da.astype(BF), size)
    do_low, da_abs = project_out_back(da_blocks, master_out, perm)
    old_spots, do_low = lax.optimization_barrier((spots, do_low))
    first_old = exchange(
        deal_moments(FIRST, [moment_gate, moment_up], moment_down, old_spots, size, copies), size
    )
    dq, dk, dv = attend_back(q_low, k_low, v_low, do_low, first)
    dqkv, dx_part, dgain_qk = project_back(
        dq, dk, dv, pre, w_qkv, gain_q, gain_k, cos, sin, perm
    )
    first_sum, dqkv = lax.optimization_barrier((first_sum, dqkv))
    first_dealt = exchange(deal_grads(FIRST, first_sum, spots, size), size)
    first_piece, first_rows = look_piece(FIRST, first_dealt, first_old, first_sum, spots)
    first_in = lax.all_gather(first_piece, "dp", axis=0)
    old_spots, first_piece = lax.optimization_barrier((spots, first_piece))
    second_old = exchange(
        deal_moments(
            SECOND,
            [moment_query, moment_key, moment_value],
            moment_out,
            old_spots,
            size,
            copies,
        ),
        size,
    )
    gain_terms = jnp.concatenate([dgain_qk[0], dgain_qk[1], dgain_a, dgain_f])
    gain_count = gain_terms.shape[0] // copies
    gain_unit = jnp.pad(
        gain_terms.astype(BF).reshape(copies, gain_count), ((0, 0), (0, strip * edge - gain_count))
    ).reshape(copies, 1, strip, edge)
    second_bucket = grad_down_bucket([o_low], [da_abs], copies, 6 * size + 1, size)
    second_bucket = lax.dynamic_update_slice(second_bucket, gain_unit, (0, 6 * size, 0, 0))
    dqkv, _ = lax.optimization_barrier((dqkv, first_piece))
    second_bucket = grad_columns(x_blocks, [dqkv] * size, second_bucket, 2 * size, 4)
    second_sum = scatter(second_bucket)
    dx = own_sum(dx_part)

    first_in, grad_tokens = lax.optimization_barrier((first_in, dh + dx))
    first_pieces = [
        (3, lambda size, j, spots: (0, size + 2 * spots[j], 0, 0)),
        (3, lambda size, j, spots: (0, size + 2 * spots[j] + 1, 0, 0)),
        (3, lambda size, j, spots: (0, j, 0, 0)),
    ]
    first_moments, first_talls = [moment_gate, moment_up, moment_down], (False, False, True)
    three, four = (0, 1, 2), (0, 1, 2, 3)
    second_dealt = exchange(deal_grads(SECOND, second_sum, spots, size), size)
    second_piece, second_rows = look_piece(SECOND, second_dealt, second_old, second_sum, spots)
    second_in = lax.all_gather(second_piece, "dp", axis=0)
    first_rows, second_rows, second_piece = lax.optimization_barrier(
        (first_rows, second_rows, second_piece)
    )
    first_whole = lax.all_gather(first_rows, "dp", axis=0)
    second_whole = lax.all_gather(second_rows, "dp", axis=0)

    groups = tuple((r, 0) for r in range(size))
    is_two = (place == 2).astype(jnp.int32)
    first_units = jnp.where((core == 0) & (place < 3), 3, 0)
    second_units = jnp.where((core == 1) & (place < 4), jnp.where(place < 2, 1, 2), 0)
    first_info = jnp.stack([place, is_two, first_units]).astype(jnp.int32)
    second_info = jnp.stack([place, is_two, second_units]).astype(jnp.int32)
    first_in, _ = lax.optimization_barrier((first_in, second_rows))
    first_made = ortho(first_info, first_in, (3,))
    first_near = [first_made[0]] + [
        send_one_core(first_made[r], copies, size, r, 0, sources=three) for r in range(1, size)
    ]
    second_in, first_near[1] = lax.optimization_barrier((second_in, first_near[1]))
    second_made = ortho(second_info, second_in, (1, 2))
    second_pieces = [
        (2, lambda size, j, spots: (0, size + 2 * spots[j], 0, 0)),
        (1, lambda size, j, spots: (0, 2 * size + 4 * spots[j] + 2, 0, 0)),
        (1, lambda size, j, spots: (0, 2 * size + 4 * spots[j] + 3, 0, 0)),
        (2, lambda size, j, spots: (0, j, 0, 0)),
    ]
    second_moments = [moment_query, moment_key, moment_value, moment_out]
    second_talls = (False, False, False, True)

    second_near = [second_made[0]] + [
        send_one_core(second_made[r], copies, size, r, 1, sources=four) for r in range(1, size)
    ]
    state_spots, _ = lax.optimization_barrier((spots, second_made))
    first_state = state(
        first_whole, first_pieces, first_moments, first_talls, state_spots, size, "state_first"
    )
    g_gate, g_up, g_down, n_gate, n_up, n_down = first_state
    first_near, g_gate, second_near[1], second_near[2] = lax.optimization_barrier(
        (first_near, g_gate, second_near[1], second_near[2])
    )
    first_far = [to_other_core(value, copies, 0) for value in first_near]
    first_spots = spots.at[size + 1].set((1 - core).astype(jnp.int32))
    u_gate, u_up, u_down = update(
        first_near,
        first_far,
        ((0, False, 3), (1, False, 3), (2, True, 3)),
        [master_gate, master_up, master_down],
        (False, False, True),
        first_spots,
        "update_first",
    )
    state_spots, u_gate = lax.optimization_barrier((spots, u_gate))
    g_query, g_key, g_value, g_out, n_query, n_key, n_value, n_out = state(
        second_whole, second_pieces, second_moments, second_talls, state_spots, size, "state_second"
    )
    second_near, g_query = lax.optimization_barrier((second_near, g_query))
    second_far = [to_other_core(value, copies, 1) for value in second_near]
    second_spots = spots.at[size + 1].set(core.astype(jnp.int32))
    u_key, u_value, u_out, u_query = update(
        second_near,
        second_far,
        ((0, False, 1), (1, False, 1), (2, True, 2), (3, False, 2)),
        [master_key, master_value, master_out, master_query],
        (False, False, True, False),
        second_spots,
        "update_second",
    )
    grads = (g_query, g_key, g_value, g_out, g_gate, g_up, g_down)
    new_moments = (n_query, n_key, n_value, n_out, n_gate, n_up, n_down)
    new_masters = (u_query, u_key, u_value, u_out, u_gate, u_up, u_down)

    gain_part = gain_first.shape[0]
    gain_sums = second_whole[:, 6 * size].reshape(copies, strip * edge)[:, :gain_count]
    gain_grad = lax.dynamic_slice_in_dim(gain_sums.reshape(-1), place * gain_part, gain_part)
    gain_grad = gain_grad.astype(F32)
    own_gains = lax.dynamic_slice_in_dim(gains, place * gain_part, gain_part)
    first_new = BETA_FIRST * gain_first + (1.0 - BETA_FIRST) * gain_grad
    second_new = BETA_SECOND * gain_second + (1.0 - BETA_SECOND) * gain_grad * gain_grad
    gains_new = own_gains - GAIN_RATE * (first_new / (1.0 - BETA_FIRST**STEP)) / (
        jnp.sqrt(second_new / (1.0 - BETA_SECOND**STEP)) + ADAM_EPS
    )
    return (out_tokens, grad_tokens, *grads, *new_moments, *new_masters, gain_grad, second_new, gains_new)


def solution(mesh):
    rows = P(("dp", "shard"), None)
    state = P("shard", None)
    return jax.shard_map(
        on_device,
        mesh=mesh,
        in_specs=(rows, rows, P(("dp", "shard")), *[state] * 14, P(), P("shard"), P("shard")),
        out_specs=(rows, rows, *[state] * 21, P("shard"), P("shard"), P("shard")),
        check_vma=False,
    )
```

```python
import functools

import jax
import jax.numpy as jnp
import numpy as np
from jax import lax
from jax.experimental import pallas as pl
from jax.experimental.pallas import tpu as pltpu
from jax.sharding import PartitionSpec as P

D = 1024
HEADS = 16
KV_HEADS = 8
HEAD_DIM = 128
FF = 3072
NS_TURNS = 5
STEP = 10
DOCUMENTS = 4
GROUP = 2

EPS_NORM = 1e-06
ROPE_BASE = 1000000.0
MOMENTUM = 0.95
MUON_RATE = 0.5
MUON_DECAY = 0.1
BETA_FIRST = 0.9
BETA_SECOND = 0.95
GAIN_RATE = 0.6
ADAM_EPS = 1e-08
COEF_LINEAR = 3.4445
COEF_SQUARE = -4.775
COEF_CUBE = 2.0315
MASKED = -1e30

BF = jnp.bfloat16
F32 = jnp.float32
NT = (((1,), (1,)), ((), ()))
TN = (((0,), (0,)), ((), ()))


def dot(a, b):
    return jnp.dot(a, b, preferred_element_type=F32)


def dot_nt(a, b):
    return lax.dot_general(a, b, NT, preferred_element_type=F32)


def dot_tn(a, b):
    return lax.dot_general(a, b, TN, preferred_element_type=F32)


def params(*semantics, limit=32):
    return pltpu.CompilerParams(
        dimension_semantics=semantics or None, vmem_limit_bytes=limit * 1024 * 1024
    )


def cost(flops, moved, exps=0):
    return pl.CostEstimate(flops=int(flops), bytes_accessed=int(moved), transcendentals=int(exps))


def xor_permute(value, axis, size, mask):
    return lax.ppermute(value, axis, [(i, i ^ mask) for i in range(size)])


def exchange(blocks, size):
    return [blocks[0]] + [xor_permute(blocks[r], "shard", size, r) for r in range(1, size)]


def gather_blocks(value, size):
    if size != 4:
        return [[block] for block in exchange([value] * size, size)]
    half = value.shape[0] // 2
    low, high = value[:half], value[half:]
    low_two = xor_permute(low, "shard", size, 2)
    high_one = xor_permute(high, "shard", size, 1)
    high_two = xor_permute(high, "shard", size, 2)
    low_one = xor_permute(low, "shard", size, 1)
    low_three = xor_permute(low_two, "shard", size, 1)
    high_three = xor_permute(high_one, "shard", size, 2)
    return [[value], [low_one, high_one], [low_two, high_two], [low_three, high_three]]


def joined(blocks):
    return [jnp.concatenate(block, axis=0) if len(block) > 1 else block[0] for block in blocks]


def lay(parts, out):
    start = 0
    for part in parts:
        out[start : start + part.shape[0], :] = part[...]
        start += part.shape[0]


def pick(stacked, place):
    return lax.dynamic_index_in_dim(stacked, place, 0, keepdims=False)


def in_order(blocks, place):
    stacked = jnp.stack(blocks)
    return [pick(stacked, place ^ r) for r in range(len(blocks))]


def to_other_core(value, copies, from_core):
    return lax.ppermute(value, "dp", [(i + from_core, i + 1 - from_core) for i in range(0, copies, 2)])


def send_one_core(value, copies, size, mask, core, sources=None, targets=None):
    pairs = []
    for copy in range(core, copies, 2):
        for i in range(size):
            if sources is not None and i not in sources:
                continue
            if targets is not None and i ^ mask not in targets:
                continue
            pairs.append((copy * size + i, copy * size + (i ^ mask)))
    return lax.ppermute(value, ("dp", "shard"), pairs)


def pack_kernel(counts, spots, tail, *refs):
    weights, outs = refs[: sum(counts)], refs[sum(counts) :]
    size = len(outs) // len(counts)
    half = weights[0].shape[0]
    for group, count in enumerate(counts):
        for r in range(size):
            out = outs[group * size + r]
            start = 0
            for weight in weights[sum(counts[:group]) :][:count]:
                width = weight.shape[1] // size
                cols = pl.ds(pl.multiple_of(spots[r] * width, width), width)
                out[:half, start : start + width] = weight[:, cols].astype(BF)
                start += width
            if group == 0:
                out[half:, :] = jnp.zeros((16, out.shape[1]), BF)
                out[half : half + 1, : tail.shape[1]] = tail[...].astype(F32).astype(BF)


def pack(groups, tail, spots, size):
    half = groups[0][0].shape[0] // 2
    whole = lambda i, spots: (0, 0)
    cols = [sum(w.shape[1] // size for w in group) for group in groups]
    weights = [w for group in groups for w in group]
    shapes = [
        (half + 16 * (at == 0), n) for at, n in enumerate(cols) for _ in range(size)
    ]
    return pl.pallas_call(
        functools.partial(pack_kernel, [len(group) for group in groups]),
        grid_spec=pltpu.PrefetchScalarGridSpec(
            num_scalar_prefetch=1,
            grid=(1,),
            in_specs=[pl.BlockSpec(tail.shape, whole)]
            + [pl.BlockSpec((half, w.shape[1]), lambda i, spots: (spots[size], 0)) for w in weights],
            out_specs=[pl.BlockSpec(shape, whole) for shape in shapes],
        ),
        out_shape=[jax.ShapeDtypeStruct(shape, BF) for shape in shapes],
        compiler_params=params("arbitrary", limit=60),
        cost_estimate=cost(0, 1),
        name="pack",
    )(spots, tail, *weights)


def assemble_into(out, spots, mine, other):
    size = len(mine)
    half = out.shape[0] // (2 * size)
    core = spots[size]
    for r in range(size):
        for pieces, at in ((mine, core), (other, 1 - core)):
            rows = pl.ds(pl.multiple_of((2 * spots[r] + at) * half, half), half)
            out[rows, :] = pieces[r][...]


def assemble_kernel(spots, *refs):
    *pieces, out = refs
    size = len(pieces) // 2
    assemble_into(out, spots, pieces[:size], pieces[size:])


def assemble(pieces, spots):
    size = len(pieces) // 2
    half, cols = pieces[1].shape
    spec = pl.BlockSpec((half, cols), lambda i, spots: (0, 0))
    return pl.pallas_call(
        assemble_kernel,
        grid_spec=pltpu.PrefetchScalarGridSpec(
            num_scalar_prefetch=1,
            grid=(1,),
            in_specs=[spec] * (2 * size),
            out_specs=pl.BlockSpec((2 * size * half, cols), lambda i, spots: (0, 0)),
        ),
        out_shape=jax.ShapeDtypeStruct((2 * size * half, cols), BF),
        compiler_params=params("arbitrary", limit=24),
        cost_estimate=cost(0, 8 * size * half * cols),
        name="assemble",
    )(spots, *pieces)


def project_kernel(spots, gain_q, gain_k, cos, sin, *refs):
    *inputs, q_out, k_out, v_out, pre_out, w = refs
    size = len(inputs) // 3
    x_refs, pieces = inputs[:size], inputs[size:]

    @pl.when(pl.program_id(0) == 0)
    def _():
        assemble_into(w, spots, pieces[:size], pieces[size:])

    for r in range(size):
        pl.when(pl.program_id(0) == r)(
            functools.partial(
                project_block, x_refs[r], gain_q, gain_k, cos, sin, q_out, k_out, v_out, pre_out, w
            )
        )


def project_block(x, gain_q, gain_k, cos, sin, q_out, k_out, v_out, pre_out, w):
    heads_q = q_out.shape[1] // HEAD_DIM
    heads_k = k_out.shape[1] // HEAD_DIM
    cos_now, sin_now = cos[...], sin[...]
    for head in range(heads_q + 2 * heads_k):
        cols = slice(head * HEAD_DIM, (head + 1) * HEAD_DIM)
        if head % 2 == 0:
            wide = slice(head * HEAD_DIM, min(head + 2, heads_q + 2 * heads_k) * HEAD_DIM)
            both = dot(x[...], w[:, wide])
        pre = both[:, (head % 2) * HEAD_DIM : (head % 2 + 1) * HEAD_DIM]
        if head >= heads_q + heads_k:
            at = head - heads_q - heads_k
            v_out[:, at * HEAD_DIM : (at + 1) * HEAD_DIM] = pre.astype(BF)
            continue
        pre_out[:, cols] = pre
        inverse = lax.rsqrt(jnp.mean(pre * pre, axis=-1, keepdims=True) + EPS_NORM)
        normed = pre * inverse * (gain_q[...] if head < heads_q else gain_k[...])
        turned = normed * cos_now + rotate_half(normed) * sin_now
        if head < heads_q:
            q_out[:, cols] = (turned * HEAD_DIM ** (-0.5)).astype(BF)
        else:
            at = head - heads_q
            k_out[:, at * HEAD_DIM : (at + 1) * HEAD_DIM] = turned.astype(BF)


def project(x_blocks, mine, others, part, gain_q, gain_k, cos, sin, spots, heads_q, heads_k):
    size = len(x_blocks)
    rows = part * size
    cols = (heads_q + 2 * heads_k) * HEAD_DIM
    width = x_blocks[0].shape[1]
    half = width // size // 2
    there = lambda r, spots: (spots[r], 0)
    whole = lambda r, spots: (0, 0)
    piece_specs = [pl.BlockSpec((half, cols), whole)] * (2 * size)
    widths = (heads_q * HEAD_DIM, heads_k * HEAD_DIM, heads_k * HEAD_DIM, (heads_q + heads_k) * HEAD_DIM)
    return pl.pallas_call(
        project_kernel,
        grid_spec=pltpu.PrefetchScalarGridSpec(
            num_scalar_prefetch=1,
            grid=(size,),
            in_specs=[
                pl.BlockSpec((1, HEAD_DIM), whole),
                pl.BlockSpec((1, HEAD_DIM), whole),
                pl.BlockSpec((part, HEAD_DIM), there),
                pl.BlockSpec((part, HEAD_DIM), there),
            ]
            + [pl.BlockSpec((part, width), whole)] * size
            + piece_specs,
            out_specs=[pl.BlockSpec((part, n), there) for n in widths]
            + [pl.BlockSpec((width, cols), whole)],
        ),
        out_shape=[
            jax.ShapeDtypeStruct((rows, n), F32 if i == 3 else BF) for i, n in enumerate(widths)
        ]
        + [jax.ShapeDtypeStruct((width, cols), BF)],
        compiler_params=params("arbitrary", limit=32),
        cost_estimate=cost(2 * rows * width * cols, 2 * rows * width + 4 * width * cols + 6 * rows * cols),
        name="project",
    )(spots, gain_q, gain_k, cos, sin, *x_blocks, *mine, *others)


def rotate_half(values):
    return pltpu.roll(values, HEAD_DIM // 2, 1)


def attend_kernel(spots, q, k, v, *refs):
    *tails, o_out, first_out, first_col = refs
    rows = q.shape[0]
    part = min(256, rows)
    size = len(tails)
    block = rows // size

    @pl.when(pl.program_id(0) == 0)
    def _():
        for r in range(size):
            cols = pl.ds(pl.multiple_of(spots[r] * block, block), block)
            first_out[:, cols] = jnp.broadcast_to(tails[r][0:1, :block].astype(F32), (8, block))
        ids = first_out[...]
        found = jnp.zeros_like(ids)
        for document in range(1, DOCUMENTS):
            count = jnp.sum((ids == document - 1).astype(F32), axis=1, keepdims=True)
            found += jnp.where(ids >= document, count, 0.0)
        first_out[...] = found
        first_col[...] = jnp.broadcast_to(found[0:1, :], (128, rows)).T

    for i in range(rows // part):
        at = slice(i * part, (i + 1) * part)
        keys = (i + 1) * part
        scores = dot_nt(q[at, :], k[:keys, :])
        key_pos = lax.broadcasted_iota(jnp.int32, (part, keys), 1)
        row_pos = i * part + lax.broadcasted_iota(jnp.int32, (part, keys), 0)
        first = first_col[at, 0:1].astype(jnp.int32)
        allowed = (key_pos >= first) & (key_pos <= row_pos)
        masked = jnp.where(allowed, scores, MASKED)
        powers = jnp.exp(masked - jnp.max(masked, axis=-1, keepdims=True))
        weights = powers * (1.0 / jnp.sum(powers, axis=-1, keepdims=True))
        o_out[at, :] = dot(weights.astype(BF), v[:keys, :]).astype(BF)


def attend(q, k, v, messages, spots):
    rows, cols = q.shape
    heads = cols // HEAD_DIM
    tail = messages[0].shape[0] // 16 - 1
    return pl.pallas_call(
        attend_kernel,
        grid_spec=pltpu.PrefetchScalarGridSpec(
            num_scalar_prefetch=1,
            grid=(heads,),
            in_specs=[
                pl.BlockSpec((rows, HEAD_DIM), lambda h, spots: (0, h)),
                pl.BlockSpec((rows, HEAD_DIM), lambda h, spots: (0, h // GROUP)),
                pl.BlockSpec((rows, HEAD_DIM), lambda h, spots: (0, h // GROUP)),
            ]
            + [
                pl.BlockSpec((16, m.shape[1]), lambda h, spots: (tail, 0)) for m in messages
            ],
            out_specs=[
                pl.BlockSpec((rows, HEAD_DIM), lambda h, spots: (0, h)),
                pl.BlockSpec((8, rows), lambda h, spots: (0, 0)),
            ],
            scratch_shapes=[pltpu.VMEM((rows, 128), F32)],
        ),
        out_shape=[
            jax.ShapeDtypeStruct((rows, cols), BF),
            jax.ShapeDtypeStruct((8, rows), F32),
        ],
        compiler_params=params("arbitrary"),
        cost_estimate=cost(3 * rows * rows * cols, 6 * rows * cols, heads * rows * rows),
        name="attend",
    )(spots, q, k, v, *messages)


def attend_back_kernel(q, k, v, do, first, dq_out, dk_out, dv_out):
    rows = q.shape[0]
    part = min(256, rows)
    k_turned = k[...].T
    dk_out[...] = jnp.zeros_like(dk_out)
    dv_out[...] = jnp.zeros_like(dv_out)
    for head in range(GROUP):
        cols = slice(head * HEAD_DIM, (head + 1) * HEAD_DIM)
        for i in range(rows // part):
            at = slice(i * part, (i + 1) * part)
            keys = (i + 1) * part
            q_now, do_now = q[at, cols], do[at, cols]
            scores = dot_nt(k[:keys, :], q_now)
            key_pos = lax.broadcasted_iota(jnp.int32, (keys, part), 0)
            row_pos = i * part + lax.broadcasted_iota(jnp.int32, (keys, part), 1)
            allowed = (key_pos >= first[0:1, at].astype(jnp.int32)) & (key_pos <= row_pos)
            masked = jnp.where(allowed, scores, MASKED)
            powers = jnp.exp(masked - jnp.max(masked, axis=0, keepdims=True))
            weights = powers * (1.0 / jnp.sum(powers, axis=0, keepdims=True))
            dv_out[:keys, :] += dot(weights.astype(BF), do_now)
            dweights = dot_nt(v[:keys, :], do_now)
            delta = jnp.sum(weights * dweights, axis=0, keepdims=True)
            dscores = (weights * (dweights - delta)).astype(BF)
            dk_out[:keys, :] += dot(dscores, q_now)
            dq_out[at, cols] = dot(k_turned[:, :keys], dscores).T


def attend_back(q, k, v, do, first):
    rows, cols = q.shape
    groups = k.shape[1] // HEAD_DIM
    wide = pl.BlockSpec((rows, GROUP * HEAD_DIM), lambda g: (0, g))
    thin = pl.BlockSpec((rows, HEAD_DIM), lambda g: (0, g))
    return pl.pallas_call(
        attend_back_kernel,
        grid=(groups,),
        in_specs=[wide, thin, thin, wide, pl.BlockSpec((8, rows), lambda g: (0, 0))],
        out_specs=[wide, thin, thin],
        out_shape=[
            jax.ShapeDtypeStruct((rows, cols), F32),
            jax.ShapeDtypeStruct(k.shape, F32),
            jax.ShapeDtypeStruct(k.shape, F32),
        ],
        compiler_params=params("arbitrary"),
        cost_estimate=cost(7 * rows * rows * cols, 16 * rows * cols, rows * rows * cols // HEAD_DIM),
        name="attend_back",
    )(q, k, v, do, first)


def out_kernel(perm, o, w, a_out):
    a_out[...] = dot(o[...], w[...].astype(BF)).astype(BF)


def project_out(o, w, perm):
    rows, width = o.shape
    blocks = perm.shape[0]
    part = rows // blocks
    return pl.pallas_call(
        out_kernel,
        grid_spec=pltpu.PrefetchScalarGridSpec(
            num_scalar_prefetch=1,
            grid=(blocks,),
            in_specs=[
                pl.BlockSpec((part, width), lambda r, perm: (perm[r], 0)),
                pl.BlockSpec(w.shape, lambda r, perm: (0, 0)),
            ],
            out_specs=pl.BlockSpec((part, w.shape[1]), lambda r, perm: (r, 0)),
        ),
        out_shape=jax.ShapeDtypeStruct((rows, w.shape[1]), BF),
        compiler_params=params("arbitrary"),
        cost_estimate=cost(2 * rows * width * w.shape[1], 2 * rows * (width + D) + 2 * w.size),
        name="project_out",
    )(perm, o, w)


def out_back_kernel(counts, perm, *refs):
    *parts, w, do_out, da_out = refs
    for r in range(len(counts)):

        @pl.when(pl.program_id(0) == r)
        def _():
            start = sum(counts[:r])
            lay(parts[start : start + counts[r]], da_out)

    do_out[...] = dot_nt(da_out[...], w[...].astype(BF)).astype(BF)


def project_out_back(da_blocks, w, perm):
    blocks = perm.shape[0]
    parts = [part for block in da_blocks for part in block]
    width = parts[0].shape[1]
    rows = sum(part.shape[0] for part in parts)
    part = rows // blocks
    return pl.pallas_call(
        functools.partial(out_back_kernel, [len(block) for block in da_blocks]),
        grid_spec=pltpu.PrefetchScalarGridSpec(
            num_scalar_prefetch=1,
            grid=(blocks,),
            in_specs=[pl.BlockSpec(p.shape, lambda r, perm: (0, 0)) for p in parts]
            + [pl.BlockSpec(w.shape, lambda r, perm: (0, 0))],
            out_specs=[
                pl.BlockSpec((part, w.shape[0]), lambda r, perm: (perm[r], 0)),
                pl.BlockSpec((part, width), lambda r, perm: (perm[r], 0)),
            ],
        ),
        out_shape=[
            jax.ShapeDtypeStruct((rows, w.shape[0]), BF),
            jax.ShapeDtypeStruct((rows, width), BF),
        ],
        compiler_params=params("arbitrary"),
        cost_estimate=cost(2 * rows * width * w.shape[0], 4 * rows * width + 2 * w.size),
        name="project_out_back",
    )(perm, *parts, w)


def feed_kernel(*refs):
    *parts, w_gate, w_up, w_down, gate_out, up_out, hid_out, f_out, total, h = refs
    step = pl.program_id(0)

    @pl.when(step == 0)
    def _():
        lay(parts, h)

    gate = dot(h[...], w_gate[...])
    up = dot(h[...], w_up[...])
    gate_out[...] = gate
    up_out[...] = up
    hid = (gate * (1.0 / (1.0 + jnp.exp(-gate))) * up).astype(BF)
    hid_out[...] = hid
    part = dot(hid, w_down[...])

    @pl.when(step == 0)
    def _():
        total[...] = part

    @pl.when(step > 0)
    def _():
        total[...] += part

    @pl.when(step == pl.num_programs(0) - 1)
    def _():
        f_out[...] = total[...].astype(BF)


def feed(parts, w_in, w_down):
    rows = sum(part.shape[0] for part in parts)
    width = w_down.shape[0]
    tile = width // 3
    cols = lambda i: (0, i)
    return pl.pallas_call(
        feed_kernel,
        grid=(3,),
        in_specs=[
            *[pl.BlockSpec(part.shape, lambda i: (0, 0)) for part in parts],
            pl.BlockSpec((D, tile), cols),
            pl.BlockSpec((D, tile), lambda i: (0, i + 3)),
            pl.BlockSpec((tile, D), lambda i: (i, 0)),
        ],
        out_specs=[pl.BlockSpec((rows, tile), cols)] * 3
        + [pl.BlockSpec((rows, D), lambda i: (0, 0))],
        out_shape=[
            jax.ShapeDtypeStruct((rows, width), F32),
            jax.ShapeDtypeStruct((rows, width), F32),
            jax.ShapeDtypeStruct((rows, width), BF),
            jax.ShapeDtypeStruct((rows, D), BF),
        ],
        scratch_shapes=[pltpu.VMEM((rows, D), F32), pltpu.VMEM((rows, D), BF)],
        compiler_params=params("arbitrary", limit=24),
        cost_estimate=cost(1, 1),
        name="feed",
    )(*parts, w_in, w_in, w_down)


def feed_back_kernel(*refs):
    *parts, gate_in, up_in, w_gate, w_up, w_down, dgate_out, dup_out, dh_out, total, df = refs
    step = pl.program_id(0)

    @pl.when(step == 0)
    def _():
        lay(parts, df)

    dhid = dot_nt(df[...], w_down[...]).astype(BF).astype(F32)
    gate, up = gate_in[...], up_in[...]
    sigma = 1.0 / (1.0 + jnp.exp(-gate))
    dgate = (dhid * up * sigma * (1.0 + gate * (1.0 - sigma))).astype(BF)
    dup = (dhid * (gate * sigma)).astype(BF)
    dgate_out[...] = dgate
    dup_out[...] = dup
    part = dot_nt(dgate, w_gate[...]) + dot_nt(dup, w_up[...])

    @pl.when(step == 0)
    def _():
        total[...] = part

    @pl.when(step > 0)
    def _():
        total[...] += part

    @pl.when(step == pl.num_programs(0) - 1)
    def _():
        dh_out[...] = total[...].astype(BF)


def feed_back(parts, gate, up, w_in, w_down):
    rows = sum(part.shape[0] for part in parts)
    width = w_down.shape[0]
    tile = width // 3
    cols = lambda i: (0, i)
    return pl.pallas_call(
        feed_back_kernel,
        grid=(3,),
        in_specs=[
            *[pl.BlockSpec(part.shape, lambda i: (0, 0)) for part in parts],
            pl.BlockSpec((rows, tile), cols),
            pl.BlockSpec((rows, tile), cols),
            pl.BlockSpec((D, tile), cols),
            pl.BlockSpec((D, tile), lambda i: (0, i + 3)),
            pl.BlockSpec((tile, D), lambda i: (i, 0)),
        ],
        out_specs=[pl.BlockSpec((rows, tile), cols)] * 2
        + [pl.BlockSpec((rows, D), lambda i: (0, 0))],
        out_shape=[
            jax.ShapeDtypeStruct((rows, width), BF),
            jax.ShapeDtypeStruct((rows, width), BF),
            jax.ShapeDtypeStruct((rows, D), BF),
        ],
        scratch_shapes=[pltpu.VMEM((rows, D), F32), pltpu.VMEM((rows, D), BF)],
        compiler_params=params("arbitrary", limit=24),
        cost_estimate=cost(1, 1),
        name="feed_back",
    )(*parts, gate, up, w_in, w_in, w_down)


def project_back_kernel(
    perm, dq, dk, dv, pre_in, w, gain_q, gain_k, cos, sin, dqkv_out, dx_out, dgain_out
):
    heads_q = dq.shape[1] // HEAD_DIM
    heads_k = dk.shape[1] // HEAD_DIM

    @pl.when(pl.program_id(0) == 0)
    def _():
        dgain_out[...] = jnp.zeros_like(dgain_out)

    cos_now, sin_now = cos[...], sin[...]
    for head in range(heads_q + heads_k):
        cols = slice(head * HEAD_DIM, (head + 1) * HEAD_DIM)
        if head < heads_q:
            grad = dq[:, cols] * HEAD_DIM ** (-0.5)
            gain = gain_q[...]
        else:
            grad = dk[:, (head - heads_q) * HEAD_DIM : (head - heads_q + 1) * HEAD_DIM]
            gain = gain_k[...]
        turned = grad * cos_now - rotate_half(grad) * sin_now
        pre = pre_in[:, cols]
        inverse = lax.rsqrt(jnp.mean(pre * pre, axis=-1, keepdims=True) + EPS_NORM)
        scaled = gain * turned
        inner = jnp.mean(pre * scaled, axis=-1, keepdims=True)
        dqkv_out[:, cols] = (inverse * scaled - pre * (inverse * inverse * inverse * inner)).astype(BF)
        row = 0 if head < heads_q else 1
        dgain_out[row : row + 1, :] += jnp.sum(turned * pre * inverse, axis=0, keepdims=True)
    dqkv_out[:, (heads_q + heads_k) * HEAD_DIM :] = dv[...].astype(BF)
    dx_out[...] = dot_nt(dqkv_out[...], w[...]).astype(BF)


def project_back(dq, dk, dv, pre, w, gain_q, gain_k, cos, sin, perm):
    rows = dq.shape[0]
    blocks = perm.shape[0]
    part = rows // blocks
    width, cols = w.shape
    there = lambda r, perm: (perm[r], 0)
    here = lambda r, perm: (r, 0)
    whole = lambda r, perm: (0, 0)
    return pl.pallas_call(
        project_back_kernel,
        grid_spec=pltpu.PrefetchScalarGridSpec(
            num_scalar_prefetch=1,
            grid=(blocks,),
            in_specs=[
                pl.BlockSpec((part, dq.shape[1]), there),
                pl.BlockSpec((part, dk.shape[1]), there),
                pl.BlockSpec((part, dv.shape[1]), there),
                pl.BlockSpec((part, pre.shape[1]), there),
                pl.BlockSpec((width, cols), whole),
                pl.BlockSpec((1, HEAD_DIM), whole),
                pl.BlockSpec((1, HEAD_DIM), whole),
                pl.BlockSpec((part, HEAD_DIM), there),
                pl.BlockSpec((part, HEAD_DIM), there),
            ],
            out_specs=[
                pl.BlockSpec((part, cols), here),
                pl.BlockSpec((part, width), here),
                pl.BlockSpec((8, HEAD_DIM), whole),
            ],
        ),
        out_shape=[
            jax.ShapeDtypeStruct((rows, cols), BF),
            jax.ShapeDtypeStruct((rows, width), BF),
            jax.ShapeDtypeStruct((8, HEAD_DIM), F32),
        ],
        compiler_params=params("arbitrary"),
        cost_estimate=cost(2 * rows * width * cols, 10 * rows * cols + 2 * rows * width + 2 * w.size),
        name="project_back",
    )(perm, dq, dk, dv, pre, w, gain_q, gain_k, cos, sin)


def grad_first_kernel(size, *refs):
    lefts, rights, out = refs[:size], refs[size : 2 * size], refs[-1]
    value = dot_tn(lefts[0][...], rights[0][...])
    for r in range(1, size):
        value += dot_tn(lefts[r][...], rights[r][...])
    copies, units, strip, edge = out.shape
    for unit in range(units):
        rows = slice(unit * copies * strip, (unit + 1) * copies * strip)
        out[:, unit] = value[rows, :].astype(BF).reshape(copies, strip, edge)


def grad_down_bucket(hids, dfs, copies, units, size=None, limit=32):
    count = len(hids)
    size = size or count
    rows, width = hids[0].shape
    edge = D // size
    strip = edge // copies
    return pl.pallas_call(
        functools.partial(grad_first_kernel, count),
        grid=(size,),
        in_specs=[pl.BlockSpec((rows, width), lambda i: (0, 0))] * count
        + [pl.BlockSpec((rows, edge), lambda i: (0, i))] * count,
        out_specs=pl.BlockSpec((copies, width // copies // strip, strip, edge), lambda i: (0, i, 0, 0)),
        out_shape=jax.ShapeDtypeStruct((copies, units, strip, edge), BF),
        compiler_params=params("arbitrary", limit=limit),
        cost_estimate=cost(2 * size * rows * width * D, 2 * size * rows * (width + D) + 2 * width * D),
        name="grad_down",
    )(*hids, *dfs)


def grad_in_kernel(size, *refs):
    lefts, rights, out = refs[:size], refs[size : 2 * size], refs[-1]
    value = dot_tn(lefts[0][...], rights[0][...])
    for r in range(1, size):
        value += dot_tn(lefts[r][...], rights[r][...])
    copies, units, strip, edge = out.shape
    for unit in range(units):
        cols = slice(unit * edge, (unit + 1) * edge)
        out[:, unit] = value[:, cols].astype(BF).reshape(copies, strip, edge)


def grad_columns(lefts, rights, bucket, start, stride, size=None, limit=32):
    count = len(lefts)
    size = size or count
    copies, _, strip, edge = bucket.shape
    width = rights[0].shape[1]
    rows = rights[0].shape[0]
    if all(right is rights[0] for right in rights):
        rows = rows // count
    units = width // edge
    row_blocks = range(count) if rights[0].shape[0] == count * rows else [0] * count
    return pl.pallas_call(
        functools.partial(grad_in_kernel, count),
        grid=(size,),
        in_specs=[pl.BlockSpec((rows, edge), lambda s: (0, s))] * count
        + [pl.BlockSpec((rows, width), lambda s, b=b: (b, 0)) for b in row_blocks]
        + [pl.BlockSpec(memory_space=pl.ANY)],
        out_specs=pl.BlockSpec(
            (copies, units, strip, edge), lambda s: (0, start // units + stride // units * s, 0, 0)
        ),
        out_shape=jax.ShapeDtypeStruct(bucket.shape, BF),
        input_output_aliases={2 * count: 0},
        compiler_params=params("arbitrary", limit=limit),
        cost_estimate=cost(
            2 * size * rows * width * D, 2 * size * rows * (width + D) + 2 * width * D
        ),
        name="grad_columns",
    )(*lefts, *rights, bucket)


def state_kernel(talls, spots, *refs):
    count = len(talls)
    pieces, moments = refs[:count], refs[count : 2 * count]
    grads, news = refs[2 * count : 3 * count], refs[3 * count : 4 * count]
    for at in range(count):
        copies, units, strip, edge = pieces[at].shape
        for unit in range(units):
            span = slice(unit * edge, (unit + 1) * edge)
            span = (span, slice(None)) if talls[at] else (slice(None), span)
            grad = pieces[at][:, unit].reshape(copies * strip, edge).astype(F32)
            grads[at][span] = grad
            news[at][span] = MOMENTUM * moments[at][span] + grad


def state_spec(state, tall, size):
    rows, cols = state.shape
    if tall:
        return pl.BlockSpec((rows, D // size), lambda j, spots: (0, j))
    return pl.BlockSpec((rows, cols // size), lambda j, spots: (0, j))


def look_specs(whole, pieces, moments, talls, size):
    copies, _, strip, edge = whole.shape
    return [
        pl.BlockSpec((copies, units, strip, edge), functools.partial(where, size))
        for units, where in pieces
    ], [state_spec(m, tall, size) for m, tall in zip(moments, talls)]


FIRST = (3, 3, 6, {0: 0, 1: 1, 2: 2}, {0: 3, 1: 3, 2: 3})
SECOND = (2, 2, 4, {0: 1, 1: 2, 2: 3, 3: 0}, {0: 1, 1: 1, 2: 2, 3: 2})


def bucket_unit(plan, chip, size, y, unit):
    units, tall_units, row_units, _, counts = plan
    if chip == 2:
        return units * y + unit
    first = {(3, 0): 0, (3, 1): 3, (2, 0): 2, (2, 1): 3, (2, 3): 0}[(units, chip)]
    return tall_units * size + row_units * y + first + min(unit, counts[chip] - 1)


def deal_moments_kernel(plan, spots, *refs):
    units, _, _, places, counts = plan
    size = spots.shape[0] - 3
    refs, outs = refs[:-size], refs[-size:]
    edge = outs[0].shape[3]
    for r in range(size):
        for chip, place in places.items():

            @pl.when(spots[r] == chip)
            def _():
                for y in range(size):
                    for unit in range(units):
                        if chip == 2:
                            ref, at = refs[len(refs) - units + unit], y
                        else:
                            ref, at = refs[place], counts[chip] * y + min(unit, counts[chip] - 1)
                        outs[r][y, unit] = ref[:, at * edge : (at + 1) * edge]


def deal_moments(plan, wides, tall, spots, size, copies):
    units = plan[0]
    edge = D // size
    strip = edge // copies
    return pl.pallas_call(
        functools.partial(deal_moments_kernel, plan),
        grid_spec=pltpu.PrefetchScalarGridSpec(
            num_scalar_prefetch=1,
            grid=(1,),
            in_specs=[
                pl.BlockSpec((strip, m.shape[1]), lambda i, spots: (spots[size + 2], 0)) for m in wides
            ]
            + [
                pl.BlockSpec((strip, D), lambda i, spots, k=k: (k * copies + spots[size + 2], 0))
                for k in range(units)
            ],
            out_specs=[pl.BlockSpec((size, units, strip, edge), lambda i, spots: (0, 0, 0, 0))] * size,
        ),
        out_shape=[jax.ShapeDtypeStruct((size, units, strip, edge), F32)] * size,
        compiler_params=params("arbitrary", limit=16),
        cost_estimate=cost(0, 1),
        name="deal_moments",
    )(spots, *wides, *[tall] * units)


def deal_grads_kernel(plan, spots, summed, *outs):
    units, tall_units, row_units, places, _ = plan
    size = len(outs)
    start = tall_units * size
    for r in range(size):
        for chip in places:

            @pl.when(spots[r] == chip)
            def _():
                for y in range(size):
                    for unit in range(units):
                        outs[r][units * y + unit] = summed[bucket_unit(plan, chip, size, y, unit)]

        for unit in range(row_units):
            outs[r][units * size + unit] = summed[start + row_units * spots[r] + unit]
        for unit in range(summed.shape[0] - start - row_units * size):
            outs[r][units * size + row_units + unit] = summed[start + row_units * size + unit]


def deal_grads(plan, summed, spots, size):
    count, strip, edge = summed.shape
    units, tall_units, row_units = plan[:3]
    shape = (units * size + row_units + count - (tall_units + row_units) * size, strip, edge)
    return pl.pallas_call(
        functools.partial(deal_grads_kernel, plan),
        grid_spec=pltpu.PrefetchScalarGridSpec(
            num_scalar_prefetch=1,
            grid=(1,),
            in_specs=[pl.BlockSpec(summed.shape, lambda i, spots: (0, 0, 0))],
            out_specs=[pl.BlockSpec(shape, lambda i, spots: (0, 0, 0))] * size,
        ),
        out_shape=[jax.ShapeDtypeStruct(shape, BF)] * size,
        compiler_params=params("arbitrary", limit=16),
        cost_estimate=cost(0, 1),
        name="deal_grads",
    )(spots, summed)


def look_piece_kernel(plan, spots, *refs):
    units, tall_units, row_units = plan[:3]
    size = (len(refs) - 3) // 2
    grads, moments, (summed, out, rows_out) = refs[:size], refs[size:-3], refs[-3:]
    begin, end = tall_units * size, (tall_units + row_units) * size
    rows_out[:begin] = summed[:begin]
    for r in range(size):
        start = begin + row_units * r
        rows_out[start : start + row_units] = grads[r][units * size : units * size + row_units]
    if summed.shape[0] > end:
        rows_out[end:] = sum(g[units * size + row_units :].astype(F32) for g in grads).astype(BF)

    def put(row, sub, unit, grad, old):
        grad = grad.astype(F32)
        value = grad + MOMENTUM * (MOMENTUM * old + grad)
        out[(row * size + sub) * units + unit] = value.astype(BF)

    for r in range(size):
        for other in range(size):
            for unit in range(units):

                @pl.when(spots[0] == 2)
                def _():
                    put(spots[r], other, unit, grads[r][units * other + unit], moments[r][other, unit])

                @pl.when(spots[0] != 2)
                def _():
                    row, sub = spots[other], spots[r]
                    put(row, sub, unit, grads[r][units * row + unit], moments[other][sub, unit])


def look_piece(plan, grads, moments, summed, spots):
    size, units, strip, edge = moments[0].shape
    whole = lambda i, spots: (0, 0, 0)
    return pl.pallas_call(
        functools.partial(look_piece_kernel, plan),
        grid_spec=pltpu.PrefetchScalarGridSpec(
            num_scalar_prefetch=1,
            grid=(1,),
            in_specs=[pl.BlockSpec(grads[0].shape, whole)] * size
            + [pl.BlockSpec(moments[0].shape, lambda i, spots: (0, 0, 0, 0))] * size
            + [pl.BlockSpec(summed.shape, whole)],
            out_specs=[
                pl.BlockSpec((units * size * size, strip, edge), whole),
                pl.BlockSpec(summed.shape, whole),
            ],
        ),
        out_shape=[
            jax.ShapeDtypeStruct((units * size * size, strip, edge), BF),
            jax.ShapeDtypeStruct(summed.shape, BF),
        ],
        compiler_params=params("arbitrary", limit=24),
        cost_estimate=cost(0, 1),
        name="look_piece",
    )(spots, *grads, *moments, summed)


def state(whole, pieces, moments, talls, spots, size, name):
    piece_specs, specs = look_specs(whole, pieces, moments, talls, size)
    return pl.pallas_call(
        functools.partial(state_kernel, talls),
        grid_spec=pltpu.PrefetchScalarGridSpec(
            num_scalar_prefetch=1,
            grid=(size,),
            in_specs=piece_specs + specs,
            out_specs=specs + specs,
        ),
        out_shape=[jax.ShapeDtypeStruct(m.shape, F32) for m in moments] * 2,
        compiler_params=params("arbitrary", limit=60),
        cost_estimate=cost(0, whole.size * 2 + 12 * sum(m.size for m in moments)),
        name=name,
    )(spots, *[whole] * len(pieces), *moments)


def ortho_kernel(sizes, info, pieces, *refs):
    *outputs, z, gram, pair, moved = refs
    subs, inner_units, edge, _ = outputs[0].shape
    place, tall, units = info[0], info[1], info[2]

    def block_in(r, unit, sub):
        at = (((r ^ place) * subs) + sub) * inner_units + unit
        return pieces[:, at].reshape(edge, edge)

    def each_block(action):
        for r in range(len(outputs)):
            for unit in range(inner_units):

                @pl.when(unit < units)
                def _():
                    def body(sub, carry):
                        action(r, unit, sub)
                        return carry

                    lax.fori_loop(0, subs, body, 0)

    def target(source, unit, sub):
        at = source ^ place
        row = jnp.where(tall == 1, sub, at)
        col = unit * subs + jnp.where(tall == 1, at, sub)
        return (
            pl.ds(pl.multiple_of(row * edge, edge), edge),
            pl.ds(pl.multiple_of(col * edge, edge), edge),
        )

    def run(total_ref):
        total_ref[...] = jnp.zeros_like(total_ref)

        def add_square(r, unit, sub):
            block = block_in(r, unit, sub).astype(F32)
            total_ref[...] += jnp.sum((block * block).reshape(edge // 8, 8, edge), axis=0)

        each_block(add_square)
        total = jnp.sum(total_ref[...], keepdims=True)
        total_ref[...] = jnp.broadcast_to(1.0 / (jnp.sqrt(total) + 1e-07), total_ref.shape)

        def put(r, unit, sub):
            block = block_in(r, unit, sub).astype(F32) * total_ref[0:1, :]
            rows, cols = target(r, unit, sub)

            @pl.when(tall == 1)
            def _():
                z[rows, cols] = block.T.astype(BF)

            @pl.when(tall == 0)
            def _():
                z[rows, cols] = block.astype(BF)

        each_block(put)

    tile = 256

    def symmetric(out, value_of):
        for j in range(D // tile):
            at, below = slice(j * tile, (j + 1) * tile), slice((j + 1) * tile, D)
            block = value_of(j * tile, at).astype(BF)
            out[j * tile :, at] = block
            if j < D // tile - 1:
                out[at, below] = block[tile:].T

    def form_gram(count):
        width = count * D
        symmetric(gram, lambda low, at: dot_nt(z[low:, :width], z[at, :width]))

    def turns(step, carry):
        double = step < NS_TURNS // 2
        for count in sizes:
            pl.when(units == count)(functools.partial(form_gram, count))

        def one(k, c):
            poly = pair.at[k]
            symmetric(
                poly,
                lambda low, at: COEF_SQUARE * gram[low:, at].astype(F32)
                + COEF_CUBE * dot(gram[low:, :], gram[:, at]),
            )

            @pl.when(double & (k == 0))
            def _():
                symmetric(
                    moved,
                    lambda low, at: COEF_LINEAR * gram[low:, at].astype(F32)
                    + dot(poly[low:, :], gram[:, at]),
                )
                symmetric(
                    gram,
                    lambda low, at: COEF_LINEAR * moved[low:, at].astype(F32)
                    + dot(moved[low:, :], poly[:, at]),
                )

            return c

        lax.fori_loop(0, jnp.where(double, 2, 1), one, 0)

        @pl.when(double)
        def _():
            symmetric(
                moved,
                lambda low, at: COEF_LINEAR
                * (pair[0, low:, at].astype(F32) + pair[1, low:, at].astype(F32))
                + dot(pair[1, low:, :], pair[0, :, at]),
            )

        @pl.when(jnp.logical_not(double))
        def _():
            moved[...] = pair[0]

        factor = jnp.where(double, COEF_LINEAR * COEF_LINEAR, COEF_LINEAR)

        def update_block(p, c):
            cols = pl.ds(pl.multiple_of(p * D, D), D)
            now = z[:, cols]
            z[:, cols] = (factor * now.astype(F32) + dot(moved[...], now)).astype(BF)
            return c

        lax.fori_loop(0, units, update_block, 0)
        return carry

    @pl.when(units > 0)
    def _():
        pl.run_scoped(run, pltpu.VMEM((8, edge), F32))

    @pl.when(units > 0)
    def _():
        lax.fori_loop(0, (NS_TURNS + 1) // 2, turns, 0)

    def take(r, unit, sub):
        rows, cols = target(r, unit, sub)
        outputs[r][sub, unit] = z[rows, cols]

    each_block(take)


def ortho(info, pieces, sizes):
    spec = pl.BlockSpec(memory_space=pltpu.VMEM)
    copies, count, strip, edge = pieces.shape
    size = D // edge
    outs = [jax.ShapeDtypeStruct((size, count // size // size, edge, edge), BF)] * size
    return pl.pallas_call(
        functools.partial(ortho_kernel, sizes),
        in_specs=[pl.BlockSpec(memory_space=pltpu.SMEM), spec],
        out_specs=[spec] * size,
        out_shape=outs,
        scratch_shapes=[
            pltpu.VMEM((D, max(sizes) * D), BF),
            pltpu.VMEM((D, D), BF),
            pltpu.VMEM((2, D, D), BF),
            pltpu.VMEM((D, D), BF),
        ],
        compiler_params=params(limit=56),
        cost_estimate=cost(1, 1),
        name="ortho",
    )(info, pieces)


def update_kernel(table, spots, *refs):
    count = len(table)
    size = spots.shape[0] - 3
    near, far = refs[:size], refs[size : 2 * size]
    masters, outs = refs[2 * size : 2 * size + count], refs[2 * size + count :]
    for r in range(size):
        for chip, (at, tall, units) in enumerate(table):
            for piece, used in ((near[r], 1), (far[r], 0)):

                @pl.when((spots[r] == chip) & (spots[size + 1] == used))
                def _():
                    edge = piece.shape[2]
                    scale = MUON_RATE * (1.0 if tall else float(units) ** 0.5)
                    for unit in range(units):
                        span = slice(unit * edge, (unit + 1) * edge)
                        span = (span, slice(None)) if tall else (slice(None), span)
                        block = piece[0, unit]
                        block = block.T if tall else block
                        outs[at][span] = masters[at][span] * (
                            1.0 - MUON_RATE * MUON_DECAY
                        ) - scale * block.astype(F32)


def update(near, far, table, masters, talls, spots, name):
    size = near[0].shape[0]
    specs = [state_spec(m, tall, size) for m, tall in zip(masters, talls)]

    def block_spec(value, used):
        shape = (1,) + value.shape[1:]
        return pl.BlockSpec(shape, lambda j, spots: (j * (spots[size + 1] == used), 0, 0, 0))

    return pl.pallas_call(
        functools.partial(update_kernel, table),
        grid_spec=pltpu.PrefetchScalarGridSpec(
            num_scalar_prefetch=1,
            grid=(size,),
            in_specs=[block_spec(v, 1) for v in near] + [block_spec(v, 0) for v in far] + specs,
            out_specs=specs,
        ),
        out_shape=[jax.ShapeDtypeStruct(m.shape, F32) for m in masters],
        compiler_params=params("arbitrary", limit=48),
        cost_estimate=cost(0, 10 * sum(m.size for m in masters)),
        name=name,
    )(spots, *near, *far, *masters)


def norm_parts(values):
    return lax.rsqrt(jnp.mean(values * values, axis=-1, keepdims=True) + EPS_NORM)


def norm_back(values, gain, inverse, grad):
    scaled = gain * grad
    inner = jnp.mean(values * scaled, axis=-1, keepdims=True)
    return (
        inverse * scaled - values * (inverse * inverse * inverse * inner),
        jnp.sum(grad * values * inverse, axis=0),
    )


def on_device(
    tokens,
    cotangent,
    segments,
    master_query,
    master_key,
    master_value,
    master_out,
    master_gate,
    master_up,
    master_down,
    moment_query,
    moment_key,
    moment_value,
    moment_out,
    moment_gate,
    moment_up,
    moment_down,
    gains,
    gain_first,
    gain_second,
):
    size = lax.axis_size("shard")
    copies = lax.axis_size("dp")
    place = lax.axis_index("shard")
    core = lax.axis_index("dp") % 2
    part = tokens.shape[0]
    seq_len = part * size
    edge = D // size
    heads_q = HEADS // size
    heads_k = KV_HEADS // size
    perm = place ^ jnp.arange(size, dtype=jnp.int32)
    spots = jnp.concatenate([perm, jnp.stack([core, core, lax.axis_index("dp")]).astype(jnp.int32)])

    half = edge // 2
    qkv_cols = (heads_q + 2 * heads_k) * HEAD_DIM
    x_sent, tokens = lax.optimization_barrier((tokens, tokens))
    x_blocks = exchange([x_sent] * size, size)
    packed = pack(
        [[master_query, master_key, master_value], [master_gate, master_up]],
        segments.reshape(1, part),
        spots,
        size,
    )
    inverse_freq = ROPE_BASE ** (-(np.arange(HEAD_DIM // 2, dtype=np.float32) * 2.0 / HEAD_DIM))
    angles = np.arange(seq_len, dtype=np.float32)[:, None] * inverse_freq.astype(np.float32)[None, :]
    cos_half, sin_half = np.cos(angles), np.sin(angles)
    cos = jnp.asarray(np.concatenate([cos_half, cos_half], axis=-1), F32)
    sin = jnp.asarray(np.concatenate([-sin_half, sin_half], axis=-1), F32)
    messages = exchange(packed[:size], size)
    qkv_others = [xor_permute(m, "dp", copies, 1) for m in messages]
    x_blocks, messages, in_packed = lax.optimization_barrier((x_blocks, messages, packed[size:]))
    in_pieces = exchange(in_packed, size)
    w_down = master_down.astype(BF)

    gain_q = gains[:HEAD_DIM].reshape(1, HEAD_DIM)
    gain_k = gains[HEAD_DIM : 2 * HEAD_DIM].reshape(1, HEAD_DIM)
    gain_a = gains[2 * HEAD_DIM : 2 * HEAD_DIM + D]
    gain_f = gains[2 * HEAD_DIM + D :]

    x_blocks, messages, in_packed = lax.optimization_barrier((x_blocks, messages, in_packed))
    in_pieces = exchange(in_packed, size)
    def scatter(bucket):
        units = bucket.shape[1]
        flat = bucket.reshape(copies * units, *bucket.shape[2:])
        return lax.psum_scatter(flat, "dp", scatter_dimension=0, tiled=True)

    q_low, k_low, v_low, pre, w_qkv = project(
        x_blocks, messages, qkv_others, part, gain_q, gain_k, cos, sin, spots, heads_q, heads_k
    )
    o_low, first = attend(q_low, k_low, v_low, messages, spots)
    o_low, in_pieces = lax.optimization_barrier((o_low, in_pieces))
    in_pieces = in_pieces + [xor_permute(piece, "dp", copies, 1) for piece in in_pieces]
    w_in = assemble(in_pieces, spots)
    a_part = project_out(o_low, master_out, perm)

    def own_sum(partial):
        pieces = exchange([partial[r * part : (r + 1) * part] for r in range(size)], size)
        return sum(piece.astype(F32) for piece in pieces)

    a = own_sum(a_part)
    a_inverse = norm_parts(a)
    h = tokens.astype(F32) + a * a_inverse * gain_a
    h_blocks = gather_blocks(h.astype(BF), size)
    gates, ups, hids, f_parts = zip(*[feed(block, w_in, w_down) for block in h_blocks])
    f = sum(piece.astype(F32) for piece in exchange(list(f_parts), size))
    f_inverse = norm_parts(f)
    out_tokens = (h + f * f_inverse * gain_f).astype(BF)

    dy = cotangent.astype(F32)
    df, dgain_f = norm_back(f, gain_f, f_inverse, dy)
    df_blocks = gather_blocks(df.astype(BF), size)
    strip = edge // copies
    first_bucket = grad_down_bucket(hids, joined(df_blocks), copies, 9 * size)
    dgates, dups, dh_parts = zip(
        *[
            feed_back(df_blocks[r], gates[r], ups[r], w_in, w_down)
            for r in range(size)
        ]
    )
    h_blocks = joined(h_blocks)
    first_bucket = grad_columns(h_blocks, dgates, first_bucket, 3 * size, 6)
    first_bucket = grad_columns(h_blocks, dups, first_bucket, 3 * size + 3, 6)
    dh_pieces = exchange(list(dh_parts), size)
    dh_pieces, first_bucket = lax.optimization_barrier((dh_pieces, first_bucket))
    dh = dy + sum(piece.astype(F32) for piece in dh_pieces)
    first_sum = scatter(first_bucket)
    da, dgain_a = norm_back(a, gain_a, a_inverse, dh)
    da_blocks = gather_blocks(da.astype(BF), size)
    do_low, da_abs = project_out_back(da_blocks, master_out, perm)
    old_spots, do_low = lax.optimization_barrier((spots, do_low))
    first_old = exchange(
        deal_moments(FIRST, [moment_gate, moment_up], moment_down, old_spots, size, copies), size
    )
    dq, dk, dv = attend_back(q_low, k_low, v_low, do_low, first)
    dqkv, dx_part, dgain_qk = project_back(
        dq, dk, dv, pre, w_qkv, gain_q, gain_k, cos, sin, perm
    )
    first_sum, dqkv = lax.optimization_barrier((first_sum, dqkv))
    first_dealt = exchange(deal_grads(FIRST, first_sum, spots, size), size)
    first_piece, first_rows = look_piece(FIRST, first_dealt, first_old, first_sum, spots)
    first_in = lax.all_gather(first_piece, "dp", axis=0)
    old_spots, first_piece = lax.optimization_barrier((spots, first_piece))
    second_old = exchange(
        deal_moments(
            SECOND,
            [moment_query, moment_key, moment_value],
            moment_out,
            old_spots,
            size,
            copies,
        ),
        size,
    )
    gain_terms = jnp.concatenate([dgain_qk[0], dgain_qk[1], dgain_a, dgain_f])
    gain_count = gain_terms.shape[0] // copies
    gain_unit = jnp.pad(
        gain_terms.astype(BF).reshape(copies, gain_count), ((0, 0), (0, strip * edge - gain_count))
    ).reshape(copies, 1, strip, edge)
    second_bucket = grad_down_bucket([o_low], [da_abs], copies, 6 * size + 1, size, 60)
    second_bucket = lax.dynamic_update_slice(second_bucket, gain_unit, (0, 6 * size, 0, 0))
    dqkv, _ = lax.optimization_barrier((dqkv, first_piece))
    second_bucket = grad_columns(x_blocks, [dqkv] * size, second_bucket, 2 * size, 4, None, 60)
    second_sum = scatter(second_bucket)
    dx = own_sum(dx_part)

    first_in, grad_tokens = lax.optimization_barrier((first_in, dh + dx))
    first_pieces = [
        (3, lambda size, j, spots: (0, size + 2 * spots[j], 0, 0)),
        (3, lambda size, j, spots: (0, size + 2 * spots[j] + 1, 0, 0)),
        (3, lambda size, j, spots: (0, j, 0, 0)),
    ]
    first_moments, first_talls = [moment_gate, moment_up, moment_down], (False, False, True)
    three, four = (0, 1, 2), (0, 1, 2, 3)
    second_dealt = exchange(deal_grads(SECOND, second_sum, spots, size), size)
    second_piece, second_rows = look_piece(SECOND, second_dealt, second_old, second_sum, spots)
    second_in = lax.all_gather(second_piece, "dp", axis=0)
    first_rows, second_rows, second_piece = lax.optimization_barrier(
        (first_rows, second_rows, second_piece)
    )
    first_whole = lax.all_gather(first_rows, "dp", axis=0)
    second_whole = lax.all_gather(second_rows, "dp", axis=0)

    groups = tuple((r, 0) for r in range(size))
    is_two = (place == 2).astype(jnp.int32)
    first_units = jnp.where((core == 0) & (place < 3), 3, 0)
    second_units = jnp.where((core == 1) & (place < 4), jnp.where(place < 2, 1, 2), 0)
    first_info = jnp.stack([place, is_two, first_units]).astype(jnp.int32)
    second_info = jnp.stack([place, is_two, second_units]).astype(jnp.int32)
    first_in, _ = lax.optimization_barrier((first_in, second_rows))
    first_made = ortho(first_info, first_in, (3,))
    first_near = [first_made[0]] + [
        send_one_core(first_made[r], copies, size, r, 0, sources=three) for r in range(1, size)
    ]
    second_in, first_near[1] = lax.optimization_barrier((second_in, first_near[1]))
    second_made = ortho(second_info, second_in, (1, 2))
    second_pieces = [
        (2, lambda size, j, spots: (0, size + 2 * spots[j], 0, 0)),
        (1, lambda size, j, spots: (0, 2 * size + 4 * spots[j] + 2, 0, 0)),
        (1, lambda size, j, spots: (0, 2 * size + 4 * spots[j] + 3, 0, 0)),
        (2, lambda size, j, spots: (0, j, 0, 0)),
    ]
    second_moments = [moment_query, moment_key, moment_value, moment_out]
    second_talls = (False, False, False, True)

    second_near = [second_made[0]] + [
        send_one_core(second_made[r], copies, size, r, 1, sources=four) for r in range(1, size)
    ]
    state_spots, _ = lax.optimization_barrier((spots, second_made))
    first_state = state(
        first_whole, first_pieces, first_moments, first_talls, state_spots, size, "state_first"
    )
    g_gate, g_up, g_down, n_gate, n_up, n_down = first_state
    first_near, g_gate, second_near[1], second_near[2] = lax.optimization_barrier(
        (first_near, g_gate, second_near[1], second_near[2])
    )
    first_far = [to_other_core(value, copies, 0) for value in first_near]
    first_spots = spots.at[size + 1].set((1 - core).astype(jnp.int32))
    u_gate, u_up, u_down = update(
        first_near,
        first_far,
        ((0, False, 3), (1, False, 3), (2, True, 3)),
        [master_gate, master_up, master_down],
        (False, False, True),
        first_spots,
        "update_first",
    )
    state_spots, u_gate = lax.optimization_barrier((spots, u_gate))
    g_query, g_key, g_value, g_out, n_query, n_key, n_value, n_out = state(
        second_whole, second_pieces, second_moments, second_talls, state_spots, size, "state_second"
    )
    second_near, g_query = lax.optimization_barrier((second_near, g_query))
    second_far = [to_other_core(value, copies, 1) for value in second_near]
    second_spots = spots.at[size + 1].set(core.astype(jnp.int32))
    u_key, u_value, u_out, u_query = update(
        second_near,
        second_far,
        ((0, False, 1), (1, False, 1), (2, True, 2), (3, False, 2)),
        [master_key, master_value, master_out, master_query],
        (False, False, True, False),
        second_spots,
        "update_second",
    )
    grads = (g_query, g_key, g_value, g_out, g_gate, g_up, g_down)
    new_moments = (n_query, n_key, n_value, n_out, n_gate, n_up, n_down)
    new_masters = (u_query, u_key, u_value, u_out, u_gate, u_up, u_down)

    gain_part = gain_first.shape[0]
    gain_sums = second_whole[:, 6 * size].reshape(copies, strip * edge)[:, :gain_count]
    gain_grad = lax.dynamic_slice_in_dim(gain_sums.reshape(-1), place * gain_part, gain_part)
    gain_grad = gain_grad.astype(F32)
    own_gains = lax.dynamic_slice_in_dim(gains, place * gain_part, gain_part)
    first_new = BETA_FIRST * gain_first + (1.0 - BETA_FIRST) * gain_grad
    second_new = BETA_SECOND * gain_second + (1.0 - BETA_SECOND) * gain_grad * gain_grad
    gains_new = own_gains - GAIN_RATE * (first_new / (1.0 - BETA_FIRST**STEP)) / (
        jnp.sqrt(second_new / (1.0 - BETA_SECOND**STEP)) + ADAM_EPS
    )
    return (out_tokens, grad_tokens, *grads, *new_moments, *new_masters, gain_grad, second_new, gains_new)


def solution(mesh):
    rows = P(("dp", "shard"), None)
    state = P("shard", None)
    return jax.shard_map(
        on_device,
        mesh=mesh,
        in_specs=(rows, rows, P(("dp", "shard")), *[state] * 14, P(), P("shard"), P("shard")),
        out_specs=(rows, rows, *[state] * 21, P("shard"), P("shard"), P("shard")),
        check_vma=False,
    )
```
